32 devices in a mesh: inp: 4 (over x, core), wt: 4 (over z), out: 2 (over y).
Axes of the slice: x: 2, y: 2, z: 4, core: 2. Of those that a mesh axis runs over, the one named last changes fastest.
Arguments:
- tokens: bfloat16 [2, 4096, 2048], P(None, ('inp', 'wt'), 'out'), may hold values from -6 to 6
- gate_weight: bfloat16 [2048, 4096], P('out', ('wt', 'inp')), may hold values from -0.125 to 0.125
- up_weight: bfloat16 [2048, 4096], P('out', ('wt', 'inp')), may hold values from -0.125 to 0.125
- down_weight: bfloat16 [4096, 2048], P(('wt', 'inp'), 'out'), may hold values from -0.09375 to 0.09375
- cotangent: bfloat16 [2, 4096, 2048], P(None, ('inp', 'wt'), 'out'), may hold values from -3 to 3
Outputs:
- output: bfloat16 [2, 4096, 2048], P(None, ('inp', 'wt'), 'out')
- grad_tokens: bfloat16 [2, 4096, 2048], P(None, ('inp', 'wt'), 'out')
- grad_gate: float32 [2048, 4096], P('out', ('wt', 'inp'))
- grad_up: float32 [2048, 4096], P('out', ('wt', 'inp'))
- grad_down: float32 [4096, 2048], P(('wt', 'inp'), 'out')
The draws below stay inside these ranges and needn't reach their ends.
All inputs are finite; a program needn't handle non-finite values.
Results may differ from the reference program's by a relative error of at most 0.035.
Values may be sent and summed in bfloat16 or wider, within the bound.
No kernel may reach another device: no remote copies, remote signals or barrier semaphores. Data moves between devices by JAX's collectives and lax.ppermute only.
A program may use at most 128 MiB of HBM per device.

```python
import jax
import jax.numpy as jnp
from jax import lax

D = 2048
FF = 4096
MB = 2
TOK_DEV = 1024
TOKENS = 4096
N_INP = 4
N_OUT = 2


def steps_of(stream_key, extent, split, smallest, largest):
    def one(axis_at, shards_of):
        steps = jax.random.uniform(jax.random.fold_in(jax.random.fold_in(stream_key, 6), axis_at), (shards_of,), jnp.float32, smallest / len(split), largest / len(split))
        return jnp.repeat(jnp.exp(steps), extent[axis_at] // shards_of).reshape((-1,) + (1,) * (len(extent) - axis_at - 1))

    gain = one(*split[0])
    for cut in split[1:]:
        gain = gain * one(*cut)
    return gain


def noise(own_key, extent, deviation, limit, shards=(), kind=jnp.bfloat16):
    values = deviation * jax.random.normal(own_key, extent, jnp.float32)
    if shards:
        values = values * steps_of(own_key, extent, shards, -0.22, 0.18)
    return jnp.clip(values, -limit, limit).astype(kind)


def setup_inputs(seed: int = 0) -> dict:
    key_list = jax.random.split(jax.random.key(seed), 6)
    tokens = noise(key_list[0], (MB, TOKENS, D), 1.0, 6.0, ((1, 16), (2, 2)))
    gate_weight = noise(key_list[1], (D, FF), D ** -0.5, 0.125, ((0, 2), (1, 16)))
    up_weight = noise(key_list[2], (D, FF), D ** -0.5, 0.125, ((0, 2), (1, 16)))
    down_weight = noise(key_list[3], (FF, D), FF ** -0.5, 0.09375, ((0, 16), (1, 2)))
    cotangent = noise(key_list[4], (MB, TOKENS, D), 0.5, 3.0, ((1, 16), (2, 2)))
    return {"tokens": tokens, "gate_weight": gate_weight, "up_weight": up_weight, "down_weight": down_weight, "cotangent": cotangent}


def rounded(value):
    return lax.optimization_barrier(value.astype(jnp.bfloat16)).astype(jnp.float32)


def group_rows(array, group):
    batches = array.shape[0]
    shaped = array.reshape(batches, N_INP, TOK_DEV, array.shape[2])
    return shaped[:, group].reshape(batches * TOK_DEV, array.shape[2])


def reference(tokens, gate_weight, up_weight, down_weight, cotangent):
    batches, length, model_dim = tokens.shape
    hidden_dim = gate_weight.shape[1]
    flat_in = tokens.reshape(batches * length, model_dim)
    flat_cot = cotangent.reshape(batches * length, model_dim)
    block_cols = model_dim // N_OUT
    gate_sum = jnp.zeros((batches * length, hidden_dim), jnp.float32)
    up_sum = jnp.zeros((batches * length, hidden_dim), jnp.float32)
    back_sum = jnp.zeros((batches * length, hidden_dim), jnp.float32)
    for block in range(N_OUT):
        lower = block * block_cols
        upper = lower + block_cols
        in_cols = flat_in[:, lower:upper]
        cot_cols = flat_cot[:, lower:upper]
        gate_sum = gate_sum + rounded(jnp.dot(in_cols, gate_weight[lower:upper], preferred_element_type=jnp.float32))
        up_sum = up_sum + rounded(jnp.dot(in_cols, up_weight[lower:upper], preferred_element_type=jnp.float32))
        back_sum = back_sum + rounded(jnp.dot(cot_cols, down_weight[:, lower:upper].T, preferred_element_type=jnp.float32))
    sigmoid_g = jax.nn.sigmoid(gate_sum)
    silu_g = gate_sum * sigmoid_g
    hidden = (silu_g * up_sum).astype(jnp.bfloat16)
    slope = sigmoid_g * (1.0 + gate_sum * (1.0 - sigmoid_g))
    grad_gate_act = (back_sum * up_sum * slope).astype(jnp.bfloat16)
    grad_up_act = (back_sum * silu_g).astype(jnp.bfloat16)
    output = jnp.dot(hidden, down_weight, preferred_element_type=jnp.float32).astype(jnp.bfloat16)
    grad_flat = jnp.dot(grad_gate_act, gate_weight.T, preferred_element_type=jnp.float32)
    grad_flat = grad_flat + jnp.dot(grad_up_act, up_weight.T, preferred_element_type=jnp.float32)
    grad_tokens = grad_flat.astype(jnp.bfloat16)
    shaped_in = flat_in.reshape(batches, length, model_dim)
    shaped_cot = flat_cot.reshape(batches, length, model_dim)
    shaped_hidden = hidden.reshape(batches, length, hidden_dim)
    shaped_gate = grad_gate_act.reshape(batches, length, hidden_dim)
    shaped_up = grad_up_act.reshape(batches, length, hidden_dim)
    grad_gate = jnp.zeros((model_dim, hidden_dim), jnp.float32)
    grad_up = jnp.zeros((model_dim, hidden_dim), jnp.float32)
    grad_down = jnp.zeros((hidden_dim, model_dim), jnp.float32)
    for group in range(N_INP):
        in_group = group_rows(shaped_in, group)
        grad_gate = grad_gate + rounded(jnp.dot(in_group.T, group_rows(shaped_gate, group), preferred_element_type=jnp.float32))
        grad_up = grad_up + rounded(jnp.dot(in_group.T, group_rows(shaped_up, group), preferred_element_type=jnp.float32))
        grad_down = grad_down + rounded(jnp.dot(group_rows(shaped_hidden, group).T, group_rows(shaped_cot, group), preferred_element_type=jnp.float32))
    return (output.reshape(batches, length, model_dim), grad_tokens.reshape(batches, length, model_dim), grad_gate, grad_up, grad_down)
```

```python
import jax
import jax.numpy as jnp
from jax import lax
from jax.sharding import PartitionSpec as P

F32 = jnp.float32
BF16 = jnp.bfloat16


def matmul(a, b, contract):
    return lax.dot_general(a, b, ((contract[:1], contract[1:]), ((), ())), preferred_element_type=F32)


def flip(array, axis, size, bit):
    return lax.ppermute(array, axis, [(at, at ^ bit) for at in range(size)])


def activation_grads(gate_sum, up_sum, back_sum):
    sigmoid_g = jax.nn.sigmoid(gate_sum)
    silu_g = gate_sum * sigmoid_g
    slope = sigmoid_g * (1.0 + gate_sum * (1.0 - sigmoid_g))
    return ((back_sum * up_sum * slope).astype(BF16), (back_sum * silu_g).astype(BF16))


class Square:
    def __init__(self, n_inp):
        self.n_inp = n_inp

    def core(self, array):
        return flip(array, "inp", self.n_inp, 1)

    def chip(self, array):
        return flip(array, "inp", self.n_inp, 2)

    def other(self, array):
        return flip(array, "out", 2, 1)

    def own_units(self, weight):
        half = weight.shape[0] // 2
        at = lax.axis_index("out")
        mine = lax.dynamic_slice_in_dim(weight, at * half, half, 0)
        theirs = lax.dynamic_slice_in_dim(weight, (1 - at) * half, half, 0)
        return jnp.concatenate([mine, self.other(theirs)], axis=1)

    def return_units(self, grad):
        cols = grad.shape[1] // 2
        mine = grad[:, :cols].astype(F32)
        theirs = self.other(grad[:, cols:]).astype(F32)
        first = lax.axis_index("out") == 0
        return jnp.where(first, jnp.concatenate([mine, theirs]), jnp.concatenate([theirs, mine]))

    def gather(self, array):
        own = [array[0], array[1]]
        by_chip = [self.chip(a) for a in own]
        by_other = [self.other(a) for a in own]
        diagonal = [self.other(by_chip[0]), self.chip(by_other[1])]
        same = [own, by_other, by_chip, diagonal]
        cross = [[self.core(a) for a in pair] for pair in same]
        rows = []
        for half in (same, cross):
            for left, right in ((half[0], half[1]), (half[2], half[3])):
                for batch in range(2):
                    rows.append(jnp.concatenate([left[batch], right[batch]], axis=1))
        return jnp.concatenate(rows)

    def scatter(self, product, rows, cols):
        half, quarter = rows // 2, rows // 4
        blocks = {}
        for chip in (1, 0):
            for other in (1, 0):
                at = slice(half + chip * quarter, half + (chip + 1) * quarter)
                span = slice(other * cols // 2, (other + 1) * cols // 2)
                blocks[chip, other] = self.core(product(at, span).astype(BF16))
        sums = {}
        for chip in (1, 0):
            for other in (1, 0):
                at = slice(chip * quarter, (chip + 1) * quarter)
                span = slice(other * cols // 2, (other + 1) * cols // 2)
                sums[chip, other] = product(at, span) + blocks[chip, other].astype(F32)
        batch = quarter // 2
        diagonal = sums[1, 1].astype(BF16)
        from_other = self.other(diagonal[:batch]).astype(F32)
        from_chip = self.chip(diagonal[batch:]).astype(F32)
        zeros = jnp.zeros_like(from_other)
        to_chip = sums[1, 0] + jnp.concatenate([from_other, zeros])
        to_other = sums[0, 1] + jnp.concatenate([zeros, from_chip])
        total = sums[0, 0] + self.chip(to_chip.astype(BF16)).astype(F32) + self.other(to_other.astype(BF16)).astype(F32)
        return total.astype(BF16).reshape(2, batch, cols // 2)


class Plain:
    def own_units(self, weight):
        return lax.all_to_all(weight, "out", split_axis=0, concat_axis=1, tiled=True)

    def return_units(self, grad):
        return lax.all_to_all(grad, "out", split_axis=1, concat_axis=0, tiled=True).astype(F32)

    def gather(self, array):
        array = lax.all_gather(lax.all_gather(array, "inp", axis=1, tiled=True), "out", axis=2, tiled=True)
        self.batches = array.shape[0]
        return array.reshape(-1, array.shape[2])

    def scatter(self, product, rows, cols):
        partial = product(slice(0, rows), slice(0, cols)).astype(BF16).reshape(self.batches, -1, cols)
        partial = lax.psum_scatter(partial, "out", scatter_dimension=2, tiled=True)
        return lax.psum_scatter(partial, "inp", scatter_dimension=1, tiled=True)


def layer(places, tokens, gate_weight, up_weight, down_weight, cotangent):
    def gather_units(weight):
        return lax.all_gather(places.own_units(weight), "wt", axis=0, tiled=True)

    def scatter_units(grad):
        return places.return_units(lax.psum_scatter(grad.astype(BF16), "wt", scatter_dimension=0, tiled=True))

    gate = gather_units(gate_weight.T)
    up = gather_units(up_weight.T)
    down = gather_units(down_weight)
    rows_in = places.gather(tokens)
    rows_cot = places.gather(cotangent)
    rows, cols = rows_in.shape

    gate_sum = matmul(rows_in, gate, (1, 1))
    up_sum = matmul(rows_in, up, (1, 1))
    hidden = (gate_sum * jax.nn.sigmoid(gate_sum) * up_sum).astype(BF16)
    grad_down = scatter_units(matmul(hidden, rows_cot, (0, 0)))
    back_sum = matmul(rows_cot, down, (1, 1))
    gate_act, up_act = activation_grads(gate_sum, up_sum, back_sum)
    grad_gate = scatter_units(matmul(gate_act, rows_in, (0, 0))).T
    grad_up = scatter_units(matmul(up_act, rows_in, (0, 0))).T

    def output_block(at, span):
        return matmul(hidden[at], down[:, span], (1, 0))

    def input_block(at, span):
        return matmul(gate_act[at], gate[:, span], (1, 0)) + matmul(up_act[at], up[:, span], (1, 0))

    output = places.scatter(output_block, rows, cols)
    grad_tokens = places.scatter(input_block, rows, cols)
    return (output, grad_tokens, grad_gate, grad_up, grad_down)


def solution(mesh):
    n_inp, n_out = mesh.shape["inp"], mesh.shape["out"]

    def on_device(tokens, gate_weight, up_weight, down_weight, cotangent):
        square = n_inp == 4 and n_out == 2 and tokens.shape[0] == 2
        places = Square(n_inp) if square else Plain()
        return layer(places, tokens, gate_weight, up_weight, down_weight, cotangent)

    rows_spec = P(None, ("inp", "wt"), "out")
    in_spec = P("out", ("wt", "inp"))
    down_spec = P(("wt", "inp"), "out")
    return jax.shard_map(
        on_device,
        mesh=mesh,
        in_specs=(rows_spec, in_spec, in_spec, down_spec, rows_spec),
        out_specs=(rows_spec, rows_spec, in_spec, in_spec, down_spec),
        check_vma=False,
    )
```

```python
import functools

import jax
import jax.numpy as jnp
from jax import lax
from jax.experimental import pallas as pl
from jax.experimental.pallas import tpu as pltpu
from jax.sharding import PartitionSpec as P

F32 = jnp.float32
BF16 = jnp.bfloat16
MIB = 1024 * 1024


def matmul(a, b, contract):
    return lax.dot_general(a, b, ((contract[:1], contract[1:]), ((), ())), preferred_element_type=F32)


def gated(gate_sum, up_sum):
    sigmoid_g = jax.nn.sigmoid(gate_sum)
    silu_g = gate_sum * sigmoid_g
    slope = sigmoid_g * (1.0 + gate_sum * (1.0 - sigmoid_g))
    return silu_g, silu_g * up_sum, up_sum * slope


def call(kernel, outs, flops, *args):
    moved = sum(a.size * a.dtype.itemsize for a in args) + sum(o.size * o.dtype.itemsize for o in outs)
    return pl.pallas_call(
        kernel,
        out_shape=outs,
        in_specs=[pl.BlockSpec(memory_space=pltpu.VMEM)] * len(args),
        out_specs=[pl.BlockSpec(memory_space=pltpu.VMEM)] * len(outs),
        compiler_params=pltpu.CompilerParams(vmem_limit_bytes=44 * MIB),
        cost_estimate=pl.CostEstimate(flops=flops, bytes_accessed=moved, transcendentals=0),
    )(*args)


def shape(*dims):
    return jax.ShapeDtypeStruct(dims, BF16)


class Rows:
    def __init__(self, pieces, blocks, step):
        self.pieces, self.blocks, self.step = pieces, blocks, step

    def read(self, refs, at, side):
        piece, first = self.blocks[at][side]
        return refs[piece].at[first : first + self.step]


def hidden_kernel(rows, width, *refs):
    count = len(rows.pieces)
    pieces, (own_ref, other_ref, hidden_ref, turned_ref, silu_ref, rest_ref) = refs[:count], refs[count:]
    groups = own_ref.shape[0] // (2 * width)
    for at in range(len(rows.blocks)):
        span = slice(at * rows.step, (at + 1) * rows.step)
        sums = matmul(rows.read(pieces, at, 0)[...], own_ref[...], (1, 1))
        sums = sums + matmul(rows.read(pieces, at, 1)[...], other_ref[...], (1, 1))
        for group in range(groups):
            low = 2 * group * width
            silu_g, hidden, rest = gated(sums[:, low : low + width], sums[:, low + width : low + 2 * width])
            cols = slice(group * width, (group + 1) * width)
            hidden_ref[span, cols] = hidden.astype(BF16)
            turned_ref[cols, span] = hidden.T.astype(BF16)
            silu_ref[span, cols] = silu_g.astype(BF16)
            rest_ref[span, cols] = rest.astype(BF16)


def grads_kernel(rows, width, *refs):
    count = len(rows.pieces)
    pieces, (down_ref, silu_ref, rest_ref, act_ref, turned_ref) = refs[:count], refs[count:]
    groups = down_ref.shape[0] // width
    half = down_ref.shape[1] // 2
    for at in range(len(rows.blocks)):
        span = slice(at * rows.step, (at + 1) * rows.step)
        back = matmul(rows.read(pieces, at, 0)[...], down_ref[:, :half], (1, 1))
        back = back + matmul(rows.read(pieces, at, 1)[...], down_ref[:, half:], (1, 1))
        for group in range(groups):
            cols = slice(group * width, (group + 1) * width)
            for part, factor in enumerate((rest_ref, silu_ref)):
                grad = back[:, cols] * factor[span, cols].astype(F32)
                low = (2 * group + part) * width
                act_ref[span, low : low + width] = grad.astype(BF16)
                turned_ref[low : low + width, span] = grad.T.astype(BF16)


def weight_kernel(rows, sides, tile, *refs):
    count = len(rows.pieces)
    pieces, (turned_ref, out_ref) = refs[:count], refs[count:]
    half = out_ref.shape[1] // len(sides)
    for place, side in enumerate(sides):

        @pl.loop(0, half // tile)
        def _(index):
            cols = pl.ds(pl.multiple_of(index * tile, tile), tile)
            total = jnp.zeros((out_ref.shape[0], tile), F32)
            for at in range(len(rows.blocks)):
                span = slice(at * rows.step, (at + 1) * rows.step)
                total = total + matmul(turned_ref[:, span], rows.read(pieces, at, side)[:, cols], (1, 0))
            out_ref[:, pl.ds(pl.multiple_of(place * half + index * tile, tile), tile)] = total.astype(BF16)


class Square:
    def core(self, array):
        return lax.ppermute(array, "inp", [(at, at ^ 1) for at in range(4)])

    def chip(self, array):
        return lax.ppermute(array, "inp", [(at, at ^ 2) for at in range(4)])

    def other(self, array):
        return lax.ppermute(array, "out", [(0, 1), (1, 0)])

    def unit_halves(self, weight):
        half = weight.shape[0] // 2
        at = lax.axis_index("out")
        return (
            lax.dynamic_slice_in_dim(weight, at * half, half, 0),
            lax.dynamic_slice_in_dim(weight, (1 - at) * half, half, 0),
        )

    def in_order(self, mine, theirs):
        mine, theirs = mine.astype(F32), theirs.astype(F32)
        first = lax.axis_index("out") == 0
        return jnp.where(first, jnp.concatenate([mine, theirs]), jnp.concatenate([theirs, mine]))

    def gather(self, array):
        step = array.shape[1]
        own = array.reshape(2 * step, array.shape[2])
        by_chip, by_other = self.chip(own), self.other(own)
        corner = [self.other(by_chip[:step]), self.chip(by_other[step:])]
        pieces = [own, by_other, by_chip] + corner
        pieces = pieces + [self.core(piece) for piece in pieces]
        blocks = []
        for base in (0, 5):
            blocks += [((base, 0), (base + 1, 0)), ((base, step), (base + 1, step))]
            blocks += [((base + 2, 0), (base + 3, 0)), ((base + 2, step), (base + 4, 0))]
        return Rows(pieces, blocks, step)

    def scatter(self, product, rows, cols):
        half, quarter = rows // 2, rows // 4
        far = {}
        for chip in (1, 0):
            for other in (1, 0):
                at = slice(half + chip * quarter, half + (chip + 1) * quarter)
                far[chip, other] = self.core(product(at, other).astype(BF16))
        sums = {}
        for chip in (1, 0):
            for other in (1, 0):
                at = slice(chip * quarter, (chip + 1) * quarter)
                sums[chip, other] = product(at, other) + far[chip, other].astype(F32)
        batch = quarter // 2
        corner = sums[1, 1].astype(BF16)
        from_other = self.other(corner[:batch]).astype(F32)
        from_chip = self.chip(corner[batch:]).astype(F32)
        zeros = jnp.zeros_like(from_other)
        to_chip = sums[1, 0] + jnp.concatenate([from_other, zeros])
        to_other = sums[0, 1] + jnp.concatenate([zeros, from_chip])
        total = sums[0, 0] + self.chip(to_chip.astype(BF16)).astype(F32) + self.other(to_other.astype(BF16)).astype(F32)
        return total.astype(BF16).reshape(2, batch, cols // 2)

    def layer(self, tokens, gate_weight, up_weight, down_weight, cotangent):
        def gather_units(array):
            return lax.all_gather(array, "wt", axis=0, tiled=True)

        def scatter_units(array):
            return lax.psum_scatter(array, "wt", scatter_dimension=0, tiled=True)

        gate_mine, gate_theirs = self.unit_halves(gate_weight.T)
        up_mine, up_theirs = self.unit_halves(up_weight.T)
        down_mine, down_theirs = self.unit_halves(down_weight)
        width, half = gate_mine.shape
        own_units = gather_units(jnp.concatenate([gate_mine, up_mine]))
        other_units = gather_units(self.other(jnp.concatenate([gate_theirs, up_theirs])))
        down = gather_units(jnp.concatenate([down_mine, self.other(down_theirs)], axis=1))
        rows_in = self.gather(tokens)
        rows_cot = self.gather(cotangent)
        count = len(rows_in.blocks) * rows_in.step
        units = down.shape[0]

        hidden, hidden_turned, silu, rest = call(
            functools.partial(hidden_kernel, rows_in, width),
            [shape(count, units), shape(units, count), shape(count, units), shape(count, units)],
            8 * count * units * half,
            *rows_in.pieces,
            own_units,
            other_units,
        )
        (down_term,) = call(
            functools.partial(weight_kernel, rows_cot, (0, 1), 256),
            [shape(units, 2 * half)],
            4 * count * units * half,
            *rows_cot.pieces,
            hidden_turned,
        )
        down_sum = scatter_units(down_term)
        act, act_turned = call(
            functools.partial(grads_kernel, rows_cot, width),
            [shape(count, 2 * units), shape(2 * units, count)],
            4 * count * units * half,
            *rows_cot.pieces,
            down,
            silu,
            rest,
        )
        terms = [
            call(
                functools.partial(weight_kernel, rows_in, (side,), 256),
                [shape(2 * units, half)],
                4 * count * units * half,
                *rows_in.pieces,
                act_turned,
            )[0]
            for side in (1, 0)
        ]
        other_sum, own_sum = scatter_units(terms[0]), scatter_units(terms[1])
        down_back = self.other(down_sum[:, half:])
        units_back = self.other(other_sum)
        grad_down = self.in_order(down_sum[:, :half], down_back)
        grad_gate = self.in_order(own_sum[:width], units_back[:width]).T
        grad_up = self.in_order(own_sum[width:], units_back[width:]).T

        def output_block(at, other):
            return matmul(hidden[at], down[:, other * half : (other + 1) * half], (1, 0))

        def input_block(at, other):
            return matmul(act[at], other_units if other else own_units, (1, 0))

        output = self.scatter(output_block, count, 2 * half)
        grad_tokens = self.scatter(input_block, count, 2 * half)
        return (output, grad_tokens, grad_gate, grad_up, grad_down)


class Plain:
    def units(self, weight):
        own = lax.all_to_all(weight, "out", split_axis=0, concat_axis=1, tiled=True)
        return lax.all_gather(own, "wt", axis=0, tiled=True)

    def unit_sums(self, grad):
        own = lax.psum_scatter(grad.astype(BF16), "wt", scatter_dimension=0, tiled=True)
        return lax.all_to_all(own, "out", split_axis=1, concat_axis=0, tiled=True).astype(F32)

    def gather(self, array):
        array = lax.all_gather(lax.all_gather(array, "inp", axis=1, tiled=True), "out", axis=2, tiled=True)
        return array.reshape(-1, array.shape[2])

    def scatter(self, partial, batches):
        partial = partial.astype(BF16).reshape(batches, -1, partial.shape[1])
        partial = lax.psum_scatter(partial, "out", scatter_dimension=2, tiled=True)
        return lax.psum_scatter(partial, "inp", scatter_dimension=1, tiled=True)

    def layer(self, tokens, gate_weight, up_weight, down_weight, cotangent):
        gate, up, down = self.units(gate_weight.T), self.units(up_weight.T), self.units(down_weight)
        rows_in, rows_cot = self.gather(tokens), self.gather(cotangent)
        gate_sum = matmul(rows_in, gate, (1, 1))
        up_sum = matmul(rows_in, up, (1, 1))
        silu_g, hidden, rest = gated(gate_sum, up_sum)
        hidden = hidden.astype(BF16)
        grad_down = self.unit_sums(matmul(hidden, rows_cot, (0, 0)))
        back_sum = matmul(rows_cot, down, (1, 1))
        gate_act, up_act = (back_sum * rest).astype(BF16), (back_sum * silu_g).astype(BF16)
        grad_gate = self.unit_sums(matmul(gate_act, rows_in, (0, 0))).T
        grad_up = self.unit_sums(matmul(up_act, rows_in, (0, 0))).T
        output = self.scatter(matmul(hidden, down, (1, 0)), tokens.shape[0])
        partial = matmul(gate_act, gate, (1, 0)) + matmul(up_act, up, (1, 0))
        grad_tokens = self.scatter(partial, tokens.shape[0])
        return (output, grad_tokens, grad_gate, grad_up, grad_down)


def solution(mesh):
    square = mesh.shape["inp"] == 4 and mesh.shape["out"] == 2

    def on_device(tokens, *others):
        places = Square() if square and tokens.shape[0] == 2 else Plain()
        return places.layer(tokens, *others)

    rows_spec = P(None, ("inp", "wt"), "out")
    in_spec = P("out", ("wt", "inp"))
    down_spec = P(("wt", "inp"), "out")
    return jax.shard_map(
        on_device,
        mesh=mesh,
        in_specs=(rows_spec, in_spec, in_spec, down_spec, rows_spec),
        out_specs=(rows_spec, rows_spec, in_spec, in_spec, down_spec),
        check_vma=False,
    )
```

```python
import functools

import jax
import jax.numpy as jnp
from jax import lax
from jax.experimental import pallas as pl
from jax.experimental.pallas import tpu as pltpu
from jax.sharding import PartitionSpec as P

F32 = jnp.float32
BF16 = jnp.bfloat16
MIB = 1024 * 1024


def matmul(a, b, contract):
    return lax.dot_general(a, b, ((contract[:1], contract[1:]), ((), ())), preferred_element_type=F32)


def gated(gate_sum, up_sum):
    sigmoid_g = jax.nn.sigmoid(gate_sum)
    silu_g = gate_sum * sigmoid_g
    slope = sigmoid_g * (1.0 + gate_sum * (1.0 - sigmoid_g))
    return silu_g, silu_g * up_sum, up_sum * slope


def shape(*dims, dtype=BF16):
    return jax.ShapeDtypeStruct(dims, dtype)


def call(kernel, outs, flops, args, after=(), specs=None, scratch=(), limit=24):
    everything = [*args, *after]
    moved = sum(a.size * a.dtype.itemsize for a in args) + sum(o.size * o.dtype.itemsize for o in outs)
    specs = specs or [pl.BlockSpec(memory_space=pltpu.VMEM)] * len(args)

    def body(*refs):
        kernel(*refs[: len(args)], *refs[len(everything) :])

    return pl.pallas_call(
        body,
        out_shape=list(outs),
        in_specs=[*specs, *[pl.BlockSpec(memory_space=pl.ANY)] * len(after)],
        out_specs=[pl.BlockSpec(memory_space=pltpu.VMEM)] * len(outs),
        scratch_shapes=list(scratch),
        compiler_params=pltpu.CompilerParams(vmem_limit_bytes=limit * MIB),
        cost_estimate=pl.CostEstimate(flops=flops, bytes_accessed=moved, transcendentals=0),
    )(*everything)


ANY = pl.BlockSpec(memory_space=pl.ANY)
VMEM = pl.BlockSpec(memory_space=pltpu.VMEM)
SMEM = pl.BlockSpec(memory_space=pltpu.SMEM)


class Rows:
    def __init__(self, pieces, blocks, step):
        self.pieces, self.blocks, self.step = pieces, blocks, step
        self.count, self.half = len(blocks) * step, pieces[0].shape[1]

    def copies(self, refs, sides, scratch, sems):
        found = []
        for at, pair in enumerate(self.blocks):
            found.append([])
            for place, side in enumerate(sides):
                piece, first = pair[side]
                into = scratch.at[pl.ds(at * self.step, self.step), pl.ds(place * self.half, self.half)]
                source = refs[piece].at[pl.ds(first, self.step)]
                found[-1].append(pltpu.make_async_copy(source, into, sems.at[at * len(sides) + place]))
        return found


def hidden_kernel(rows, width, *refs):
    count = len(rows.pieces)
    pieces = refs[:count]
    own_ref, other_ref, hidden_ref, turned_ref, silu_ref, rest_ref, in_ref, unit_ref, sems, unit_sems = refs[count:]
    half = rows.half
    loads = [
        pltpu.make_async_copy(own_ref, unit_ref.at[:, pl.ds(0, half)], unit_sems.at[0]),
        pltpu.make_async_copy(other_ref, unit_ref.at[:, pl.ds(half, half)], unit_sems.at[1]),
    ]
    copies = rows.copies(pieces, (0, 1), in_ref, sems)
    for copy in loads + [copy for block in copies for copy in block]:
        copy.start()
    for copy in loads:
        copy.wait()
    for pair in range(len(copies) // 2):
        for copy in copies[2 * pair] + copies[2 * pair + 1]:
            copy.wait()
        span = slice(2 * pair * rows.step, 2 * (pair + 1) * rows.step)

        @pl.loop(0, unit_ref.shape[0] // (2 * width))
        def _(group):
            units = pl.ds(pl.multiple_of(group * 2 * width, 2 * width), 2 * width)
            sums = matmul(in_ref[span], unit_ref[units], (1, 1))
            silu_g, hidden, rest = gated(sums[:, :width], sums[:, width:])
            cols = pl.ds(pl.multiple_of(group * width, width), width)
            hidden_ref[span, cols] = hidden.astype(BF16)
            turned_ref[cols, span] = hidden.T.astype(BF16)
            silu_ref[span, cols] = silu_g.astype(BF16)
            rest_ref[span, cols] = rest.astype(BF16)


def grads_kernel(rows, width, *refs):
    count = len(rows.pieces)
    pieces = refs[:count]
    down_ref, silu_ref, rest_ref, act_ref, turned_ref, cot_ref, sems = refs[count:]
    copies = rows.copies(pieces, (0, 1), cot_ref, sems)
    for copy in [copy for block in copies for copy in block]:
        copy.start()
    for pair in range(len(copies) // 2):
        for copy in copies[2 * pair] + copies[2 * pair + 1]:
            copy.wait()
        span = slice(2 * pair * rows.step, 2 * (pair + 1) * rows.step)

        @pl.loop(0, down_ref.shape[0] // (2 * width))
        def _(group):
            units = pl.ds(pl.multiple_of(group * 2 * width, 2 * width), 2 * width)
            back = matmul(cot_ref[span], down_ref[units], (1, 1))
            for part, factor in enumerate((rest_ref, silu_ref)):
                grads = back * factor[span, units].astype(F32)
                for side in range(2):
                    grad = grads[:, side * width : (side + 1) * width]
                    low = pl.ds(pl.multiple_of((4 * group + 2 * side + part) * width, width), width)
                    act_ref[span, low] = grad.astype(BF16)
                    turned_ref[low, span] = grad.T.astype(BF16)


def weight_kernel(rows, sides, tile, *refs):
    count = len(rows.pieces)
    pieces, (turned_ref, out_ref, rows_ref, sems) = refs[:count], refs[count:]
    copies = [copy for block in rows.copies(pieces, sides, rows_ref, sems) for copy in block]
    for copy in copies:
        copy.start()
    for copy in copies:
        copy.wait()

    @pl.loop(0, out_ref.shape[1] // tile)
    def _(index):
        cols = pl.ds(pl.multiple_of(index * tile, tile), tile)
        out_ref[:, cols] = matmul(turned_ref[...], rows_ref[:, cols], (1, 0)).astype(BF16)


def block_kernel(first, places, sides, added, *refs):
    rights, many = len(sides), len(places)
    left_any, right_any, refs = refs[0], refs[1 : 1 + rights], refs[1 + rights :]
    adds, refs = refs[: many * added], refs[many * added :]
    outs, (left_ref, right_ref, sems) = refs[:many], refs[many:]
    depth, half = right_ref.shape[1:]
    copies = [pltpu.make_async_copy(left_any.at[pl.ds(first, left_ref.shape[0])], left_ref, sems.at[0])]
    for at, side in enumerate(sides):
        source = right_any[at].at[:, pl.ds(side * half, half)]
        copies.append(pltpu.make_async_copy(source, right_ref.at[at], sems.at[1 + at]))
    for copy in copies:
        copy.start()
    for copy in copies:
        copy.wait()
    for at, (row, right) in enumerate(places):
        total = matmul(left_ref[row : row + outs[at].shape[0]], right_ref[right], (1, 0))
        if added:
            total = total + adds[at][...].astype(F32)
        outs[at][...] = total.astype(BF16)


def halves_kernel(at_ref, gate_ref, up_ref, mine_ref, theirs_ref):
    width = gate_ref.shape[1] // 2
    for part, ref in enumerate((gate_ref, up_ref)):
        span = slice(part * width, (part + 1) * width)
        low, high = ref[:, :width].astype(F32).T.astype(BF16), ref[:, width:].astype(F32).T.astype(BF16)
        first = at_ref[0] == 0
        mine_ref[span] = jnp.where(first, low, high)
        theirs_ref[span] = jnp.where(first, high, low)


def copy_kernel(in_ref, out_ref):
    out_ref[...] = in_ref[...]


def beside_kernel(left_ref, right_ref, out_ref):
    half = left_ref.shape[1]
    out_ref[:, :half] = left_ref[...]
    out_ref[:, half:] = right_ref[...]


def line_kernel(places, at_ref, own_ref, *refs):
    before, after, out_ref = refs[: places - 1], refs[places - 1 : -1], refs[-1]
    step = own_ref.shape[0]
    for block in range(places):
        for at in range(places):
            source = own_ref if at == block else before[at - block - 1] if at > block else after[block - at - 1]

            @pl.when(at_ref[0] == at)
            def _(source=source):
                out_ref[block * step : (block + 1) * step] = source[...]


def finish_kernel(at_ref, mine_ref, theirs_ref, gate_ref, up_ref):
    width = mine_ref.shape[0] // 2
    for part, out_ref in enumerate((gate_ref, up_ref)):
        span = slice(part * width, (part + 1) * width)
        mine, theirs = mine_ref[span].astype(F32).T, theirs_ref[span].astype(F32).T
        first = at_ref[0] == 0
        out_ref[:, :width] = jnp.where(first, mine, theirs)
        out_ref[:, width:] = jnp.where(first, theirs, mine)


class Square:
    def __init__(self, places):
        self.places = places

    def core(self, array):
        return lax.ppermute(array, "inp", [(at, at ^ 1) for at in range(4)])

    def chip(self, array):
        return lax.ppermute(array, "inp", [(at, at ^ 2) for at in range(4)])

    def other(self, array):
        return lax.ppermute(array, "out", [(0, 1), (1, 0)])

    def gather(self, array, split):
        step = array.shape[1]
        own = array.reshape(2 * step, array.shape[2])
        by_chip, by_other = self.chip(own), self.other(own)
        if split:
            corner = [self.other(by_chip[:step]), self.chip(by_other[step:])]
        else:
            corner = [self.chip(by_other)]
        pieces = [own, by_other, by_chip] + corner
        many = len(pieces)
        pieces = pieces + [self.core(piece) for piece in pieces]
        blocks = []
        for base in (0, many):
            blocks += [((base, 0), (base + 1, 0)), ((base, step), (base + 1, step))]
            last = (base + 4, 0) if split else (base + 3, step)
            blocks += [((base + 2, 0), (base + 3, 0)), ((base + 2, step), last)]
        return Rows(pieces, blocks, step)

    def line(self, own, at):
        many = self.places

        def shift(array, by):
            return lax.ppermute(array, "wt", [(i, i + by) for i in range(many) if 0 <= i + by < many])

        near = {by: shift(own, by) for by in (1, -1, 2, -2) if abs(by) < many}
        before, beyond = [near[1], near[2]], [near[-1], near[-2]]
        for by in range(3, many):
            before.append(lax.ppermute(before[-1], "wt", [(i, i + 1) for i in range(by - 1, many - 1)]))
            beyond.append(lax.ppermute(beyond[-1], "wt", [(i, i - 1) for i in range(1, many - by + 1)]))
        (out,) = call(
            functools.partial(line_kernel, many),
            [shape(many * own.shape[0], own.shape[1])],
            0,
            [at, own, *before, *beyond],
            specs=[SMEM] + [VMEM] * (2 * many - 1),
        )
        return out

    def products(self, left, rights, places, adds=(), after=()):
        far = int(not adds)
        quarter, depth = left.shape[0] // 4, left.shape[1]
        half = rights[0][2]
        outs = [shape(quarter, half)] * len(places)
        use = sorted({other for _, other in places})
        chips = sorted({chip for chip, _ in places})
        first = 2 * far * quarter + chips[0] * quarter
        wanted = [((chip - chips[0]) * quarter, use.index(other)) for chip, other in places]
        args = [left] + [rights[other][0] for other in use] + [adds[place] for place in places if adds]
        blocks = call(
            functools.partial(block_kernel, first, wanted, [rights[other][1] for other in use], bool(adds)),
            outs,
            2 * len(places) * quarter * depth * half,
            args,
            after,
            specs=[ANY] * (1 + len(use)) + [VMEM] * (len(args) - 1 - len(use)),
            scratch=[
                pltpu.VMEM((len(chips) * quarter, depth), BF16),
                pltpu.VMEM((len(use), depth, half), BF16),
                pltpu.SemaphoreType.DMA((1 + len(use),)),
            ],
        )
        return dict(zip(places, blocks))

    def scatter_far(self, left, rights):
        first = self.products(left, rights, [(1, 1)])
        second = self.products(left, rights, [(0, 1), (1, 0), (0, 0)], after=list(first.values()))
        return first | second

    def scatter_near(self, left, rights, far, split, after=()):
        far = {place: self.core(block) for place, block in far.items()}
        sums = self.products(left, rights, [(1, 1)], far, after)
        sums |= self.products(left, rights, [(0, 1), (1, 0), (0, 0)], far, list(sums.values()))
        corner = sums[1, 1]
        step = corner.shape[0] // 2
        if split:
            by_other = self.other(corner[:step]).astype(F32)
            by_chip = self.chip(corner[step:]).astype(F32)
            zeros = jnp.zeros_like(by_other)
            to_chip = (sums[1, 0].astype(F32) + jnp.concatenate([by_other, zeros])).astype(BF16)
            to_other = (sums[0, 1].astype(F32) + jnp.concatenate([zeros, by_chip])).astype(BF16)
        else:
            to_chip = sums[1, 0]
            to_other = (sums[0, 1].astype(F32) + self.chip(corner).astype(F32)).astype(BF16)
        return sums[0, 0], self.chip(to_chip), self.other(to_other)

    def scatter_end(self, own, by_chip, by_other):
        total = own.astype(F32) + by_chip.astype(F32) + by_other.astype(F32)
        return total.astype(BF16).reshape(2, own.shape[0] // 2, own.shape[1])

    def layer(self, tokens, gate_weight, up_weight, down_weight, cotangent):
        def gather_units(array):
            return lax.all_gather(array, "wt", axis=0, tiled=True)

        def scatter_units(array):
            return lax.psum_scatter(array, "wt", scatter_dimension=0, tiled=True)

        at_out = lax.axis_index("out").astype(jnp.int32)
        half, width = gate_weight.shape[0], gate_weight.shape[1] // 2
        pair = [shape(2 * width, half)] * 2
        mine, theirs = call(halves_kernel, pair, 0, [at_out.reshape(1), gate_weight, up_weight], specs=[SMEM, VMEM, VMEM])
        own_units = gather_units(mine)
        theirs = self.other(theirs)
        rows_in = self.gather(tokens, True)
        (theirs,) = call(copy_kernel, pair[:1], 0, [theirs], after=[rows_in.pieces[2]])
        other_units = gather_units(theirs)
        down_mine = lax.dynamic_slice_in_dim(down_weight, at_out * width, width, 0)
        down_theirs = self.other(lax.dynamic_slice_in_dim(down_weight, (1 - at_out) * width, width, 0))
        rows_cot = self.gather(cotangent, False)
        (down_own,) = call(
            beside_kernel, [shape(width, 2 * half)], 0, [down_mine, down_theirs], after=[other_units]
        )

        count = rows_in.count
        units = self.places * width
        loads = len(rows_in.blocks)
        both = pltpu.VMEM((count, 2 * half), BF16)
        hidden, hidden_turned, silu, rest = call(
            functools.partial(hidden_kernel, rows_in, width),
            [shape(count, units), shape(units, count), shape(count, units), shape(count, units)],
            8 * count * units * half,
            [*rows_in.pieces, own_units, other_units],
            after=[down_own],
            specs=[ANY] * (len(rows_in.pieces) + 2),
            scratch=[
                both,
                pltpu.VMEM((2 * units, 2 * half), BF16),
                pltpu.SemaphoreType.DMA((2 * loads,)),
                pltpu.SemaphoreType.DMA((2,)),
            ],
            limit=32,
        )
        (down_term,) = call(
            functools.partial(weight_kernel, rows_cot, (0, 1), 256),
            [shape(units, 2 * half)],
            4 * count * units * half,
            [*rows_cot.pieces, hidden_turned],
            specs=[ANY] * len(rows_cot.pieces) + [VMEM],
            scratch=[both, pltpu.SemaphoreType.DMA((2 * loads,))],
        )
        down_sum = scatter_units(down_term)
        at_wt = lax.axis_index("wt").astype(jnp.int32).reshape(1)
        down = self.line(down_own, at_wt)
        down_sides = [(down, 0, half), (down, 1, half)]
        output_far = self.scatter_far(hidden, down_sides)
        act, act_turned = call(
            functools.partial(grads_kernel, rows_cot, width),
            [shape(count, 2 * units), shape(2 * units, count)],
            4 * count * units * half,
            [*rows_cot.pieces, down, silu, rest],
            after=list(output_far.values()),
            specs=[ANY] * len(rows_cot.pieces) + [VMEM] * 3,
            scratch=[both, pltpu.SemaphoreType.DMA((2 * loads,))],
            limit=32,
        )
        terms = [
            call(
                functools.partial(weight_kernel, rows_in, (side,), 256),
                [shape(2 * units, half)],
                4 * count * units * half,
                [*rows_in.pieces, act_turned],
                specs=[ANY] * len(rows_in.pieces) + [VMEM],
                scratch=[pltpu.VMEM((count, half), BF16), pltpu.SemaphoreType.DMA((loads,))],
            )[0]
            for side in (1, 0)
        ]
        other_sum, own_sum = scatter_units(terms[0]), scatter_units(terms[1])
        down_back = self.other(down_sum[:, half:])
        units_back = self.other(other_sum)
        mine, theirs = down_sum[:, :half].astype(F32), down_back.astype(F32)
        grad_down = jnp.where(at_out == 0, jnp.concatenate([mine, theirs]), jnp.concatenate([theirs, mine]))
        grad_gate, grad_up = call(
            finish_kernel,
            [shape(half, 2 * width, dtype=F32)] * 2,
            0,
            [at_out.reshape(1), own_sum, units_back],
            specs=[SMEM, VMEM, VMEM],
        )

        output = self.scatter_end(*self.scatter_near(hidden, down_sides, output_far, True))
        unit_sides = [(own_units, 0, half), (other_units, 0, half)]
        grads_far = self.scatter_far(act, unit_sides)
        grad_tokens = self.scatter_end(*self.scatter_near(act, unit_sides, grads_far, False, [down_back]))
        return (output, grad_tokens, grad_gate, grad_up, grad_down)


class Plain:
    def units(self, weight):
        own = lax.all_to_all(weight, "out", split_axis=0, concat_axis=1, tiled=True)
        return lax.all_gather(own, "wt", axis=0, tiled=True)

    def unit_sums(self, grad):
        own = lax.psum_scatter(grad.astype(BF16), "wt", scatter_dimension=0, tiled=True)
        return lax.all_to_all(own, "out", split_axis=1, concat_axis=0, tiled=True).astype(F32)

    def gather(self, array):
        array = lax.all_gather(lax.all_gather(array, "inp", axis=1, tiled=True), "out", axis=2, tiled=True)
        return array.reshape(-1, array.shape[2])

    def scatter(self, partial, batches):
        partial = partial.astype(BF16).reshape(batches, -1, partial.shape[1])
        partial = lax.psum_scatter(partial, "out", scatter_dimension=2, tiled=True)
        return lax.psum_scatter(partial, "inp", scatter_dimension=1, tiled=True)

    def layer(self, tokens, gate_weight, up_weight, down_weight, cotangent):
        gate, up, down = self.units(gate_weight.T), self.units(up_weight.T), self.units(down_weight)
        rows_in, rows_cot = self.gather(tokens), self.gather(cotangent)
        gate_sum = matmul(rows_in, gate, (1, 1))
        up_sum = matmul(rows_in, up, (1, 1))
        silu_g, hidden, rest = gated(gate_sum, up_sum)
        hidden = hidden.astype(BF16)
        grad_down = self.unit_sums(matmul(hidden, rows_cot, (0, 0)))
        back_sum = matmul(rows_cot, down, (1, 1))
        gate_act, up_act = (back_sum * rest).astype(BF16), (back_sum * silu_g).astype(BF16)
        grad_gate = self.unit_sums(matmul(gate_act, rows_in, (0, 0))).T
        grad_up = self.unit_sums(matmul(up_act, rows_in, (0, 0))).T
        output = self.scatter(matmul(hidden, down, (1, 0)), tokens.shape[0])
        partial = matmul(gate_act, gate, (1, 0)) + matmul(up_act, up, (1, 0))
        grad_tokens = self.scatter(partial, tokens.shape[0])
        return (output, grad_tokens, grad_gate, grad_up, grad_down)


def solution(mesh):
    square = mesh.shape["inp"] == 4 and mesh.shape["out"] == 2 and mesh.shape["wt"] > 2

    def on_device(tokens, *others):
        places = Square(mesh.shape["wt"]) if square and tokens.shape[0] == 2 else Plain()
        return places.layer(tokens, *others)

    rows_spec = P(None, ("inp", "wt"), "out")
    in_spec = P("out", ("wt", "inp"))
    down_spec = P(("wt", "inp"), "out")
    return jax.shard_map(
        on_device,
        mesh=mesh,
        in_specs=(rows_spec, in_spec, in_spec, down_spec, rows_spec),
        out_specs=(rows_spec, rows_spec, in_spec, in_spec, down_spec),
        check_vma=False,
    )
```

```python
import functools

import jax
import jax.numpy as jnp
from jax import lax
from jax.experimental import pallas as pl
from jax.experimental.pallas import tpu as pltpu
from jax.sharding import PartitionSpec as P

F32 = jnp.float32
BF16 = jnp.bfloat16
MIB = 1024 * 1024


def matmul(a, b, contract):
    return lax.dot_general(a, b, ((contract[:1], contract[1:]), ((), ())), preferred_element_type=F32)


def gated(gate_sum, up_sum):
    sigmoid_g = jax.nn.sigmoid(gate_sum)
    silu_g = gate_sum * sigmoid_g
    slope = sigmoid_g * (1.0 + gate_sum * (1.0 - sigmoid_g))
    return silu_g, silu_g * up_sum, up_sum * slope


def shape(*dims, dtype=BF16):
    return jax.ShapeDtypeStruct(dims, dtype)


def call(kernel, outs, flops, args, after=(), specs=None, scratch=(), limit=24):
    everything = [*args, *after]
    moved = sum(a.size * a.dtype.itemsize for a in args) + sum(o.size * o.dtype.itemsize for o in outs)
    specs = specs or [pl.BlockSpec(memory_space=pltpu.VMEM)] * len(args)

    def body(*refs):
        kernel(*refs[: len(args)], *refs[len(everything) :])

    return pl.pallas_call(
        body,
        out_shape=list(outs),
        in_specs=[*specs, *[pl.BlockSpec(memory_space=pl.ANY)] * len(after)],
        out_specs=[pl.BlockSpec(memory_space=pltpu.VMEM)] * len(outs),
        scratch_shapes=list(scratch),
        compiler_params=pltpu.CompilerParams(vmem_limit_bytes=limit * MIB),
        cost_estimate=pl.CostEstimate(flops=flops, bytes_accessed=moved, transcendentals=0),
    )(*everything)


ANY = pl.BlockSpec(memory_space=pl.ANY)
VMEM = pl.BlockSpec(memory_space=pltpu.VMEM)
SMEM = pl.BlockSpec(memory_space=pltpu.SMEM)


def hidden_kernel(width, step, rows_ref, unit_ref, hidden_ref, turned_ref, silu_ref, rest_ref):
    @pl.loop(0, rows_ref.shape[0] // step)
    def _(at):
        span = pl.ds(pl.multiple_of(at * step, step), step)
        for group in range(unit_ref.shape[0] // (2 * width)):
            units = slice(2 * group * width, 2 * (group + 1) * width)
            sums = matmul(rows_ref[span], unit_ref[units], (1, 1))
            silu_g, hidden, rest = gated(sums[:, :width], sums[:, width:])
            cols = slice(group * width, (group + 1) * width)
            hidden_ref[span, cols] = hidden.astype(BF16)
            turned_ref[cols, span] = hidden.T.astype(BF16)
            silu_ref[span, cols] = silu_g.astype(BF16)
            rest_ref[span, cols] = rest.astype(BF16)


def grads_kernel(width, step, rows_ref, down_ref, silu_ref, rest_ref, act_ref, turned_ref):
    @pl.loop(0, rows_ref.shape[0] // step)
    def _(at):
        span = pl.ds(pl.multiple_of(at * step, step), step)
        for pair in range(down_ref.shape[0] // (2 * width)):
            units = slice(2 * pair * width, 2 * (pair + 1) * width)
            back = matmul(rows_ref[span], down_ref[units], (1, 1))
            for part, factor in enumerate((rest_ref, silu_ref)):
                grads = back * factor[span, units].astype(F32)
                for side in range(2):
                    grad = grads[:, side * width : (side + 1) * width]
                    first = (4 * pair + 2 * side + part) * width
                    low = slice(first, first + width)
                    act_ref[span, low] = grad.astype(BF16)
                    turned_ref[low, span] = grad.T.astype(BF16)


def weight_kernel(first, tile, turned_ref, rows_ref, away_ref, stay_ref):
    half = away_ref.shape[0]

    @pl.loop(0, away_ref.shape[1] // tile)
    def _(index):
        cols = pl.ds(pl.multiple_of(index * tile, tile), tile)
        right = rows_ref[:, pl.ds(pl.multiple_of(first + index * tile, tile), tile)]
        away_ref[:, cols] = matmul(turned_ref[:half], right, (1, 0)).astype(BF16)
        stay_ref[:, cols] = matmul(turned_ref[half:], right, (1, 0)).astype(BF16)


def block_kernel(first, places, sides, added, *refs):
    rights, many = len(sides), len(places)
    left_any, right_any, refs = refs[0], refs[1 : 1 + rights], refs[1 + rights :]
    adds, refs = refs[: many * added], refs[many * added :]
    outs, (left_ref, right_ref, sems) = refs[:many], refs[many:]
    depth, half = right_ref.shape[1:]
    copies = [pltpu.make_async_copy(left_any.at[pl.ds(first, left_ref.shape[0])], left_ref, sems.at[0])]
    for at, side in enumerate(sides):
        source = right_any[at].at[:, pl.ds(side * half, half)]
        copies.append(pltpu.make_async_copy(source, right_ref.at[at], sems.at[1 + at]))
    for copy in copies:
        copy.start()
    for copy in copies:
        copy.wait()
    for at, (row, right) in enumerate(places):
        total = matmul(left_ref[row : row + outs[at].shape[0]], right_ref[right], (1, 0))
        if added:
            total = total + adds[at][...].astype(F32)
        outs[at][...] = total.astype(BF16)


def halves_kernel(at_ref, gate_ref, up_ref, mine_ref, theirs_ref):
    width = gate_ref.shape[1] // 2
    for part, ref in enumerate((gate_ref, up_ref)):
        span = slice(part * width, (part + 1) * width)
        low, high = ref[:, :width].astype(F32).T.astype(BF16), ref[:, width:].astype(F32).T.astype(BF16)
        first = at_ref[0] == 0
        mine_ref[span] = jnp.where(first, low, high)
        theirs_ref[span] = jnp.where(first, high, low)


def finish_kernel(at_ref, mine_ref, theirs_ref, gate_ref, up_ref):
    width = mine_ref.shape[0] // 2
    for part, out_ref in enumerate((gate_ref, up_ref)):
        span = slice(part * width, (part + 1) * width)
        mine, theirs = mine_ref[span].astype(F32).T, theirs_ref[span].astype(F32).T
        first = at_ref[0] == 0
        out_ref[:, :width] = jnp.where(first, mine, theirs)
        out_ref[:, width:] = jnp.where(first, theirs, mine)


class Square:
    def core(self, array):
        return lax.ppermute(array, "inp", [(at, at ^ 1) for at in range(4)])

    def across(self, array):
        return lax.ppermute(array, "inp", [(at, at ^ 2) for at in range(4)])

    def other(self, array):
        return lax.ppermute(array, "out", [(0, 1), (1, 0)])

    def near(self, array):
        return lax.ppermute(array, "wt", [(at, at ^ 1) for at in range(4)])

    def far(self, array):
        return lax.ppermute(array, "wt", [(at, at ^ 2) for at in range(4)])

    def gather(self, array, split):
        step = array.shape[1]
        own = array.reshape(2 * step, array.shape[2])
        by_near, by_other = self.near(own), self.other(own)
        if split:
            corner = jnp.concatenate([self.other(by_near[:step]), self.near(by_other[step:])])
        else:
            corner = self.other(by_near)
        pieces = [own, by_other, by_near, corner]
        pieces += [self.core(piece) for piece in pieces]
        rows = [jnp.concatenate(pieces[at : at + 2], axis=1) for at in range(0, 8, 2)]
        return jnp.concatenate(rows)

    def gather_units(self, own):
        by_far = self.far(own)
        return [self.across(own), self.across(by_far), own, by_far]

    def scatter_units(self, away, stay):
        total = stay.astype(F32) + self.across(away).astype(F32)
        half = total.shape[0] // 2
        return total[:half] + self.far(total[half:].astype(BF16)).astype(F32)

    def products(self, left, rights, places, adds=(), after=()):
        far = int(not adds)
        quarter, depth = left.shape[0] // 4, left.shape[1]
        half = rights[0][2]
        outs = [shape(quarter, half)] * len(places)
        use = sorted({other for _, other in places})
        chips = sorted({chip for chip, _ in places})
        first = 2 * far * quarter + chips[0] * quarter
        wanted = [((chip - chips[0]) * quarter, use.index(other)) for chip, other in places]
        args = [left] + [rights[other][0] for other in use] + [adds[place] for place in places if adds]
        blocks = call(
            functools.partial(block_kernel, first, wanted, [rights[other][1] for other in use], bool(adds)),
            outs,
            2 * len(places) * quarter * depth * half,
            args,
            after,
            specs=[ANY] * (1 + len(use)) + [VMEM] * (len(args) - 1 - len(use)),
            scratch=[
                pltpu.VMEM((len(chips) * quarter, depth), BF16),
                pltpu.VMEM((len(use), depth, half), BF16),
                pltpu.SemaphoreType.DMA((1 + len(use),)),
            ],
        )
        return dict(zip(places, blocks))

    def scatter_far(self, left, rights, after=()):
        first = self.products(left, rights, [(1, 1)], after=after)
        second = self.products(left, rights, [(0, 1), (1, 0), (0, 0)], after=list(first.values()))
        return first | second

    def scatter_near(self, left, rights, far, after=()):
        far = {place: self.core(block) for place, block in far.items()}
        sums = self.products(left, rights, [(1, 1)], far, after)
        sums |= self.products(left, rights, [(0, 1), (1, 0), (0, 0)], far, list(sums.values()))
        return sums

    def scatter_end(self, sums, split):
        corner = sums[1, 1]
        step = corner.shape[0] // 2
        if split:
            by_other = self.other(corner[:step]).astype(F32)
            by_near = self.near(corner[step:]).astype(F32)
            zeros = jnp.zeros_like(by_other)
            to_near = (sums[1, 0].astype(F32) + jnp.concatenate([by_other, zeros])).astype(BF16)
            to_other = (sums[0, 1].astype(F32) + jnp.concatenate([zeros, by_near])).astype(BF16)
        else:
            to_near = (sums[1, 0].astype(F32) + self.other(corner).astype(F32)).astype(BF16)
            to_other = sums[0, 1]
        total = sums[0, 0].astype(F32) + self.near(to_near).astype(F32) + self.other(to_other).astype(F32)
        return total.astype(BF16).reshape(2, step, corner.shape[1])

    def layer(self, tokens, gate_weight, up_weight, down_weight, cotangent):
        at_out = lax.axis_index("out").astype(jnp.int32)
        half, width = gate_weight.shape[0], gate_weight.shape[1] // 2
        pair = [shape(2 * width, half)] * 2
        mine, theirs = call(halves_kernel, pair, 0, [at_out.reshape(1), gate_weight, up_weight], specs=[SMEM, VMEM, VMEM])
        theirs = self.other(theirs)
        down_mine = lax.dynamic_slice_in_dim(down_weight, at_out * width, width, 0)
        down_theirs = self.other(lax.dynamic_slice_in_dim(down_weight, (1 - at_out) * width, width, 0))
        down_own = jnp.concatenate([down_mine, down_theirs], axis=1)

        rows_in = self.gather(tokens, False)
        sides = [jnp.concatenate(self.gather_units(own)) for own in (mine, theirs)]
        gate_up = jnp.concatenate(sides, axis=1)
        rows_cot = self.gather(cotangent, True)
        down = jnp.concatenate(self.gather_units(down_own))

        count, units = rows_in.shape[0], down.shape[0]
        step = count // 4
        hidden, hidden_turned, silu, rest = call(
            functools.partial(hidden_kernel, width, step),
            [shape(count, units), shape(units, count), shape(count, units), shape(count, units)],
            8 * count * units * half,
            [rows_in, gate_up],
            limit=28,
        )
        down_terms = call(
            functools.partial(weight_kernel, 0, 256),
            [shape(units // 2, 2 * half)] * 2,
            4 * count * units * half,
            [hidden_turned, rows_cot],
        )
        down_sum = self.scatter_units(*down_terms)
        down_sides = [(down, 0, half), (down, 1, half)]
        output_far = self.scatter_far(hidden, down_sides)
        act, act_turned = call(
            functools.partial(grads_kernel, width, step),
            [shape(count, 2 * units), shape(2 * units, count)],
            4 * count * units * half,
            [rows_cot, down, silu, rest],
            after=list(output_far.values()),
            limit=28,
        )
        output_sums = self.scatter_near(hidden, down_sides, output_far)

        def unit_terms(side, after):
            return call(
                functools.partial(weight_kernel, side * half, 256),
                [shape(units, half)] * 2,
                4 * count * units * half,
                [act_turned, rows_in],
                after=after,
            )

        other_terms = unit_terms(1, list(output_sums.values()))
        other_sum = self.scatter_units(*other_terms).astype(BF16)
        unit_sides = [(gate_up, 0, half), (gate_up, 1, half)]
        grads_far = self.scatter_far(act, unit_sides, other_terms)
        own_terms = unit_terms(0, list(grads_far.values()))
        own_sum = self.scatter_units(*own_terms).astype(BF16)
        grads_sums = self.scatter_near(act, unit_sides, grads_far, own_terms)
        output = self.scatter_end(output_sums, True)
        grad_tokens = self.scatter_end(grads_sums, False)

        down_back = self.other(down_sum[:, half:].astype(BF16))
        units_back = self.other(other_sum)
        mine, theirs = down_sum[:, :half], down_back.astype(F32)
        grad_down = jnp.where(at_out == 0, jnp.concatenate([mine, theirs]), jnp.concatenate([theirs, mine]))
        grad_gate, grad_up = call(
            finish_kernel,
            [shape(half, 2 * width, dtype=F32)] * 2,
            0,
            [at_out.reshape(1), own_sum, units_back],
            specs=[SMEM, VMEM, VMEM],
        )
        return (output, grad_tokens, grad_gate, grad_up, grad_down)


class Plain:
    def units(self, weight):
        own = lax.all_to_all(weight, "out", split_axis=0, concat_axis=1, tiled=True)
        return lax.all_gather(own, "wt", axis=0, tiled=True)

    def unit_sums(self, grad):
        own = lax.psum_scatter(grad.astype(BF16), "wt", scatter_dimension=0, tiled=True)
        return lax.all_to_all(own, "out", split_axis=1, concat_axis=0, tiled=True).astype(F32)

    def gather(self, array):
        array = lax.all_gather(lax.all_gather(array, "inp", axis=1, tiled=True), "out", axis=2, tiled=True)
        return array.reshape(-1, array.shape[2])

    def scatter(self, partial, batches):
        partial = partial.astype(BF16).reshape(batches, -1, partial.shape[1])
        partial = lax.psum_scatter(partial, "out", scatter_dimension=2, tiled=True)
        return lax.psum_scatter(partial, "inp", scatter_dimension=1, tiled=True)

    def layer(self, tokens, gate_weight, up_weight, down_weight, cotangent):
        gate, up, down = self.units(gate_weight.T), self.units(up_weight.T), self.units(down_weight)
        rows_in, rows_cot = self.gather(tokens), self.gather(cotangent)
        gate_sum = matmul(rows_in, gate, (1, 1))
        up_sum = matmul(rows_in, up, (1, 1))
        silu_g, hidden, rest = gated(gate_sum, up_sum)
        hidden = hidden.astype(BF16)
        grad_down = self.unit_sums(matmul(hidden, rows_cot, (0, 0)))
        back_sum = matmul(rows_cot, down, (1, 1))
        gate_act, up_act = (back_sum * rest).astype(BF16), (back_sum * silu_g).astype(BF16)
        grad_gate = self.unit_sums(matmul(gate_act, rows_in, (0, 0))).T
        grad_up = self.unit_sums(matmul(up_act, rows_in, (0, 0))).T
        output = self.scatter(matmul(hidden, down, (1, 0)), tokens.shape[0])
        partial = matmul(gate_act, gate, (1, 0)) + matmul(up_act, up, (1, 0))
        grad_tokens = self.scatter(partial, tokens.shape[0])
        return (output, grad_tokens, grad_gate, grad_up, grad_down)


def solution(mesh):
    square = mesh.shape["inp"] == 4 and mesh.shape["out"] == 2 and mesh.shape["wt"] == 4

    def on_device(tokens, *others):
        places = Square() if square and tokens.shape[0] == 2 else Plain()
        return places.layer(tokens, *others)

    rows_spec = P(None, ("inp", "wt"), "out")
    in_spec = P("out", ("wt", "inp"))
    down_spec = P(("wt", "inp"), "out")
    return jax.shard_map(
        on_device,
        mesh=mesh,
        in_specs=(rows_spec, in_spec, in_spec, down_spec, rows_spec),
        out_specs=(rows_spec, rows_spec, in_spec, in_spec, down_spec),
        check_vma=False,
    )
```

```python
import functools

import jax
import jax.numpy as jnp
from jax import lax
from jax.experimental import pallas as pl
from jax.experimental.pallas import tpu as pltpu
from jax.sharding import PartitionSpec as P

F32 = jnp.float32
BF16 = jnp.bfloat16
MIB = 1024 * 1024


def matmul(a, b, contract):
    return lax.dot_general(a, b, ((contract[:1], contract[1:]), ((), ())), preferred_element_type=F32)


def gated(gate_sum, up_sum):
    sigmoid_g = jax.nn.sigmoid(gate_sum)
    silu_g = gate_sum * sigmoid_g
    slope = sigmoid_g * (1.0 + gate_sum * (1.0 - sigmoid_g))
    return silu_g, silu_g * up_sum, up_sum * slope


def shape(*dims, dtype=BF16):
    return jax.ShapeDtypeStruct(dims, dtype)


def call(kernel, outs, flops, args, after=(), specs=None, scratch=(), limit=24):
    everything = [*args, *after]
    moved = sum(a.size * a.dtype.itemsize for a in args) + sum(o.size * o.dtype.itemsize for o in outs)
    specs = specs or [pl.BlockSpec(memory_space=pltpu.VMEM)] * len(args)

    def body(*refs):
        kernel(*refs[: len(args)], *refs[len(everything) :])

    return pl.pallas_call(
        body,
        out_shape=list(outs),
        in_specs=[*specs, *[pl.BlockSpec(memory_space=pl.ANY)] * len(after)],
        out_specs=[pl.BlockSpec(memory_space=pltpu.VMEM)] * len(outs),
        scratch_shapes=list(scratch),
        compiler_params=pltpu.CompilerParams(vmem_limit_bytes=limit * MIB),
        cost_estimate=pl.CostEstimate(flops=flops, bytes_accessed=moved, transcendentals=0),
    )(*everything)


ANY = pl.BlockSpec(memory_space=pl.ANY)
VMEM = pl.BlockSpec(memory_space=pltpu.VMEM)
SMEM = pl.BlockSpec(memory_space=pltpu.SMEM)


def hidden_kernel(width, rows, groups, *refs):
    row_refs, unit_refs = refs[:rows], refs[rows : rows + groups]
    hidden_ref, turned_ref, silu_ref, rest_ref = refs[rows + groups :]
    step = row_refs[0].shape[0]
    for at, row_ref in enumerate(row_refs):
        span = slice(at * step, (at + 1) * step)
        for group, unit_ref in enumerate(unit_refs):
            sums = matmul(row_ref[...], unit_ref[...], (1, 1))
            silu_g, hidden, rest = gated(sums[:, :width], sums[:, width:])
            cols = slice(group * width, (group + 1) * width)
            hidden_ref[span, cols] = hidden.astype(BF16)
            turned_ref[cols, span] = hidden.T.astype(BF16)
            silu_ref[span, cols] = silu_g.astype(BF16)
            rest_ref[span, cols] = rest.astype(BF16)


def grads_kernel(width, rows, *refs):
    row_refs, (down_ref, silu_ref, rest_ref, act_ref, turned_ref) = refs[:rows], refs[rows:]
    step = row_refs[0].shape[0]
    for at, row_ref in enumerate(row_refs):
        span = slice(at * step, (at + 1) * step)
        for pair in range(down_ref.shape[0] // (2 * width)):
            units = slice(2 * pair * width, 2 * (pair + 1) * width)
            back = matmul(row_ref[...], down_ref[units], (1, 1))
            for part, factor in enumerate((rest_ref, silu_ref)):
                grads = back * factor[span, units].astype(F32)
                for side in range(2):
                    grad = grads[:, side * width : (side + 1) * width]
                    first = (4 * pair + 2 * side + part) * width
                    low = slice(first, first + width)
                    act_ref[span, low] = grad.astype(BF16)
                    turned_ref[low, span] = grad.T.astype(BF16)


def weight_kernel(first, tile, rows, *refs):
    row_refs, (turned_ref, away_ref, stay_ref) = refs[:rows], refs[rows:]
    half, step = away_ref.shape[0], row_refs[0].shape[0]

    @pl.loop(0, away_ref.shape[1] // tile)
    def _(index):
        cols = pl.ds(pl.multiple_of(index * tile, tile), tile)
        here = pl.ds(pl.multiple_of(first + index * tile, tile), tile)
        for out_ref, low in ((away_ref, 0), (stay_ref, half)):
            total = jnp.zeros((half, tile), F32)
            for at, row_ref in enumerate(row_refs):
                left = turned_ref[low : low + half, at * step : (at + 1) * step]
                total = total + matmul(left, row_ref[:, here], (1, 0))
            out_ref[:, cols] = total.astype(BF16)


def block_kernel(first, places, sides, added, *refs):
    rights, many = len(sides), len(places)
    left_any, right_any, refs = refs[0], refs[1 : 1 + rights], refs[1 + rights :]
    adds, refs = refs[: many * added], refs[many * added :]
    outs, (left_ref, right_ref, sems) = refs[:many], refs[many:]
    depth, half = right_ref.shape[1:]
    copies = [pltpu.make_async_copy(left_any.at[pl.ds(first, left_ref.shape[0])], left_ref, sems.at[0])]
    for at, side in enumerate(sides):
        source = right_any[at].at[:, pl.ds(side * half, half)]
        copies.append(pltpu.make_async_copy(source, right_ref.at[at], sems.at[1 + at]))
    for copy in copies:
        copy.start()
    for copy in copies:
        copy.wait()
    for at, (row, right) in enumerate(places):
        total = matmul(left_ref[row : row + outs[at].shape[0]], right_ref[right], (1, 0))
        if added:
            total = total + adds[at][...].astype(F32)
        outs[at][...] = total.astype(BF16)


def halves_kernel(at_ref, gate_ref, up_ref, down_ref, mine_ref, down_mine_ref, theirs_ref):
    width = down_mine_ref.shape[0]
    first = at_ref[0] == 0
    for part, ref in enumerate((gate_ref, up_ref)):
        span = slice(part * width, (part + 1) * width)
        low, high = ref[:, :width].astype(F32).T.astype(BF16), ref[:, width:].astype(F32).T.astype(BF16)
        mine_ref[span] = jnp.where(first, low, high)
        theirs_ref[span] = jnp.where(first, high, low)
    low, high = down_ref[:width], down_ref[width:]
    down_mine_ref[...] = jnp.where(first, low, high)
    theirs_ref[2 * width :] = jnp.where(first, high, low)


def beside_kernel(first, left_ref, right_ref, out_ref):
    rows, half = left_ref.shape
    out_ref[:, :half] = left_ref[...]
    out_ref[:, half:] = right_ref[first : first + rows]


def halves_beside_kernel(left_ref, top_ref, low_ref, out_ref):
    half, step = left_ref.shape[1], top_ref.shape[0]
    out_ref[:, :half] = left_ref[...]
    out_ref[:step, half:] = top_ref[...]
    out_ref[step:, half:] = low_ref[...]


def stack_kernel(*refs):
    out_ref, step = refs[-1], refs[0].shape[0]
    for at, ref in enumerate(refs[:-1]):
        out_ref[at * step : (at + 1) * step] = ref[...]


def finish_kernel(at_ref, mine_ref, theirs_ref, gate_ref, up_ref):
    width = mine_ref.shape[0] // 2
    for part, out_ref in enumerate((gate_ref, up_ref)):
        span = slice(part * width, (part + 1) * width)
        mine, theirs = mine_ref[span].astype(F32).T, theirs_ref[span].astype(F32).T
        first = at_ref[0] == 0
        out_ref[:, :width] = jnp.where(first, mine, theirs)
        out_ref[:, width:] = jnp.where(first, theirs, mine)


def beside(left, right, first=0, after=()):
    out = [shape(left.shape[0], 2 * left.shape[1])]
    return call(functools.partial(beside_kernel, first), out, 0, [left, right], after)[0]


def stacked(parts, after=()):
    return call(stack_kernel, [shape(len(parts) * parts[0].shape[0], parts[0].shape[1])], 0, parts, after)[0]


class Square:
    def core(self, array):
        return lax.ppermute(array, "inp", [(at, at ^ 1) for at in range(4)])

    def across(self, array):
        return lax.ppermute(array, "inp", [(at, at ^ 2) for at in range(4)])

    def other(self, array):
        return lax.ppermute(array, "out", [(0, 1), (1, 0)])

    def near(self, array):
        return lax.ppermute(array, "wt", [(at, at ^ 1) for at in range(4)])

    def far(self, array):
        return lax.ppermute(array, "wt", [(at, at ^ 2) for at in range(4)])

    def scatter_units(self, away, stay):
        total = stay.astype(F32) + self.across(away).astype(F32)
        half = total.shape[0] // 2
        return total[:half] + self.far(total[half:].astype(BF16)).astype(F32)

    def products(self, left, rights, places, adds=(), after=()):
        far = int(not adds)
        quarter, depth = left.shape[0] // 4, left.shape[1]
        half = rights[0][2]
        outs = [shape(quarter, half)] * len(places)
        use = sorted({other for _, other in places})
        chips = sorted({chip for chip, _ in places})
        first = 2 * far * quarter + chips[0] * quarter
        wanted = [((chip - chips[0]) * quarter, use.index(other)) for chip, other in places]
        args = [left] + [rights[other][0] for other in use] + [adds[place] for place in places if adds]
        blocks = call(
            functools.partial(block_kernel, first, wanted, [rights[other][1] for other in use], bool(adds)),
            outs,
            2 * len(places) * quarter * depth * half,
            args,
            after,
            specs=[ANY] * (1 + len(use)) + [VMEM] * (len(args) - 1 - len(use)),
            scratch=[
                pltpu.VMEM((len(chips) * quarter, depth), BF16),
                pltpu.VMEM((len(use), depth, half), BF16),
                pltpu.SemaphoreType.DMA((1 + len(use),)),
            ],
        )
        return dict(zip(places, blocks))

    def scatter_far(self, left, rights, after=()):
        first = self.products(left, rights, [(1, 1)], after=after)
        second = self.products(left, rights, [(0, 1), (1, 0), (0, 0)], after=list(first.values()))
        return first | second

    def near_first(self, left, rights, far, after):
        return self.products(left, rights, [(1, 1)], far, after)

    def near_rest(self, left, rights, far, after):
        return self.products(left, rights, [(0, 1), (1, 0), (0, 0)], far, after)

    def layer(self, tokens, gate_weight, up_weight, down_weight, cotangent):
        at_out = lax.axis_index("out").astype(jnp.int32).reshape(1)
        half, width = gate_weight.shape[0], gate_weight.shape[1] // 2
        mine, down_mine, theirs = call(
            halves_kernel,
            [shape(2 * width, half), shape(width, half), shape(3 * width, half)],
            0,
            [at_out, gate_weight, up_weight, down_weight],
            specs=[SMEM, VMEM, VMEM, VMEM],
        )
        theirs = self.other(theirs)
        step = tokens.shape[1]
        tok, cot = tokens.reshape(2 * step, half), cotangent.reshape(2 * step, half)

        tok_near, tok_other = self.near(tok), self.other(tok)
        own_units = beside(mine, theirs)
        far_units = self.far(own_units)
        tok_corner = self.other(tok_near)
        tok_top = beside(tok, tok_other)
        across_units = self.across(own_units)
        own_down = beside(down_mine, theirs, 2 * width, [far_units, across_units])
        far_down = self.far(own_down)
        unit_groups = [across_units, self.across(far_units), own_units, far_units]
        (cot,) = call(stack_kernel, [shape(*cot.shape)], 0, [cot], after=[tok_near, tok_other])
        cot_near, cot_other = self.near(cot), self.other(cot)
        tok_low = beside(tok_near, tok_corner)
        rows_in = [tok_top, tok_low, self.core(tok_top), self.core(tok_low)]
        cot_corner = [self.other(cot_near[:step]), self.near(cot_other[step:])]
        cot_top = beside(cot, cot_other)
        (cot_low,) = call(halves_beside_kernel, [shape(2 * step, 2 * half)], 0, [cot_near, *cot_corner])
        rows_cot = [cot_top, cot_low, self.core(cot_top), self.core(cot_low)]
        down_groups = [self.across(own_down), self.across(far_down), own_down, far_down]

        count, units = 8 * step, 4 * width
        hidden, hidden_turned, silu, rest = call(
            functools.partial(hidden_kernel, width, 4, 4),
            [shape(count, units), shape(units, count), shape(count, units), shape(count, units)],
            8 * count * units * half,
            [*rows_in, *unit_groups],
            after=[far_down, cot_top],
            limit=28,
        )
        down = stacked(down_groups)
        down_sides = [(down, 0, half), (down, 1, half)]
        output_far = self.scatter_far(hidden, down_sides)
        down_terms = call(
            functools.partial(weight_kernel, 0, 256, 4),
            [shape(units // 2, 2 * half)] * 2,
            4 * count * units * half,
            [*rows_cot, hidden_turned],
            list(output_far.values()),
        )
        down_sum = self.scatter_units(*down_terms)
        act, act_turned = call(
            functools.partial(grads_kernel, width, 4),
            [shape(count, 2 * units), shape(2 * units, count)],
            4 * count * units * half,
            [*rows_cot, down, silu, rest],
            after=down_terms,
            limit=28,
        )
        output_far = {place: self.core(block) for place, block in output_far.items()}
        sums = self.near_first(hidden, down_sides, output_far, [act])
        corner = sums[1, 1]
        by_other, by_near = self.other(corner[:step]), self.near(corner[step:])
        sums |= self.near_rest(hidden, down_sides, output_far, [corner])

        def unit_terms(side, after):
            return call(
                functools.partial(weight_kernel, side * half, 256, 4),
                [shape(units, half)] * 2,
                4 * count * units * half,
                [*rows_in, act_turned],
                after=after,
            )

        other_terms = unit_terms(1, [sums[0, 0]])
        other_sum = self.scatter_units(*other_terms).astype(BF16)
        gate_up = stacked(unit_groups, [other_terms[0]])
        unit_sides = [(gate_up, 0, half), (gate_up, 1, half)]
        grads_far = self.scatter_far(act, unit_sides, [by_other, by_near])
        zeros = jnp.zeros((step, half), F32)
        to_near = (sums[1, 0].astype(F32) + jnp.concatenate([by_other.astype(F32), zeros])).astype(BF16)
        to_other = (sums[0, 1].astype(F32) + jnp.concatenate([zeros, by_near.astype(F32)])).astype(BF16)
        by_near, by_other = self.near(to_near), self.other(to_other)
        total = sums[0, 0].astype(F32) + by_near.astype(F32) + by_other.astype(F32)
        output = total.astype(BF16).reshape(2, step, half)

        own_terms = unit_terms(0, list(grads_far.values()))
        own_sum = self.scatter_units(*own_terms).astype(BF16)
        grads_far = {place: self.core(block) for place, block in grads_far.items()}
        sums = self.near_first(act, unit_sides, grads_far, [own_terms[0], by_near, by_other])
        by_other = self.other(sums[1, 1])
        sums |= self.near_rest(act, unit_sides, grads_far, [sums[1, 1]])
        to_near = (sums[1, 0].astype(F32) + by_other.astype(F32)).astype(BF16)
        by_near, by_other = self.near(to_near), self.other(sums[0, 1])
        total = sums[0, 0].astype(F32) + by_near.astype(F32) + by_other.astype(F32)
        grad_tokens = total.astype(BF16).reshape(2, step, half)

        down_back = self.other(down_sum[:, half:].astype(BF16))
        units_back = self.other(other_sum)
        mine, theirs = down_sum[:, :half], down_back.astype(F32)
        first = at_out[0] == 0
        grad_down = jnp.where(first, jnp.concatenate([mine, theirs]), jnp.concatenate([theirs, mine]))
        grad_gate, grad_up = call(
            finish_kernel,
            [shape(half, 2 * width, dtype=F32)] * 2,
            0,
            [at_out, own_sum, units_back],
            specs=[SMEM, VMEM, VMEM],
        )
        return (output, grad_tokens, grad_gate, grad_up, grad_down)


class Plain:
    def units(self, weight):
        own = lax.all_to_all(weight, "out", split_axis=0, concat_axis=1, tiled=True)
        return lax.all_gather(own, "wt", axis=0, tiled=True)

    def unit_sums(self, grad):
        own = lax.psum_scatter(grad.astype(BF16), "wt", scatter_dimension=0, tiled=True)
        return lax.all_to_all(own, "out", split_axis=1, concat_axis=0, tiled=True).astype(F32)

    def gather(self, array):
        array = lax.all_gather(lax.all_gather(array, "inp", axis=1, tiled=True), "out", axis=2, tiled=True)
        return array.reshape(-1, array.shape[2])

    def scatter(self, partial, batches):
        partial = partial.astype(BF16).reshape(batches, -1, partial.shape[1])
        partial = lax.psum_scatter(partial, "out", scatter_dimension=2, tiled=True)
        return lax.psum_scatter(partial, "inp", scatter_dimension=1, tiled=True)

    def layer(self, tokens, gate_weight, up_weight, down_weight, cotangent):
        gate, up, down = self.units(gate_weight.T), self.units(up_weight.T), self.units(down_weight)
        rows_in, rows_cot = self.gather(tokens), self.gather(cotangent)
        gate_sum = matmul(rows_in, gate, (1, 1))
        up_sum = matmul(rows_in, up, (1, 1))
        silu_g, hidden, rest = gated(gate_sum, up_sum)
        hidden = hidden.astype(BF16)
        grad_down = self.unit_sums(matmul(hidden, rows_cot, (0, 0)))
        back_sum = matmul(rows_cot, down, (1, 1))
        gate_act, up_act = (back_sum * rest).astype(BF16), (back_sum * silu_g).astype(BF16)
        grad_gate = self.unit_sums(matmul(gate_act, rows_in, (0, 0))).T
        grad_up = self.unit_sums(matmul(up_act, rows_in, (0, 0))).T
        output = self.scatter(matmul(hidden, down, (1, 0)), tokens.shape[0])
        partial = matmul(gate_act, gate, (1, 0)) + matmul(up_act, up, (1, 0))
        grad_tokens = self.scatter(partial, tokens.shape[0])
        return (output, grad_tokens, grad_gate, grad_up, grad_down)


def solution(mesh):
    square = mesh.shape["inp"] == 4 and mesh.shape["out"] == 2 and mesh.shape["wt"] == 4

    def on_device(tokens, *others):
        places = Square() if square and tokens.shape[0] == 2 else Plain()
        return places.layer(tokens, *others)

    rows_spec = P(None, ("inp", "wt"), "out")
    in_spec = P("out", ("wt", "inp"))
    down_spec = P(("wt", "inp"), "out")
    return jax.shard_map(
        on_device,
        mesh=mesh,
        in_specs=(rows_spec, in_spec, in_spec, down_spec, rows_spec),
        out_specs=(rows_spec, rows_spec, in_spec, in_spec, down_spec),
        check_vma=False,
    )
```

```python
import functools

import jax
import jax.numpy as jnp
from jax import lax
from jax.experimental import pallas as pl
from jax.experimental.pallas import tpu as pltpu
from jax.sharding import PartitionSpec as P

F32 = jnp.float32
BF16 = jnp.bfloat16
MIB = 1024 * 1024


def matmul(a, b, contract):
    return lax.dot_general(a, b, ((contract[:1], contract[1:]), ((), ())), preferred_element_type=F32)


def gated(gate_sum, up_sum):
    sigmoid_g = jax.nn.sigmoid(gate_sum)
    silu_g = gate_sum * sigmoid_g
    slope = sigmoid_g * (1.0 + gate_sum * (1.0 - sigmoid_g))
    return silu_g, silu_g * up_sum, up_sum * slope


def shape(*dims, dtype=BF16):
    return jax.ShapeDtypeStruct(dims, dtype)


def call(kernel, outs, flops, args, after=(), specs=None, scratch=(), limit=24):
    everything = [*args, *after]
    moved = sum(a.size * a.dtype.itemsize for a in args) + sum(o.size * o.dtype.itemsize for o in outs)
    specs = specs or [pl.BlockSpec(memory_space=pltpu.VMEM)] * len(args)

    def body(*refs):
        kernel(*refs[: len(args)], *refs[len(everything) :])

    return pl.pallas_call(
        body,
        out_shape=list(outs),
        in_specs=[*specs, *[pl.BlockSpec(memory_space=pl.ANY)] * len(after)],
        out_specs=[pl.BlockSpec(memory_space=pltpu.VMEM)] * len(outs),
        scratch_shapes=list(scratch),
        compiler_params=pltpu.CompilerParams(vmem_limit_bytes=limit * MIB),
        cost_estimate=pl.CostEstimate(flops=flops, bytes_accessed=moved, transcendentals=0),
    )(*everything)


SLOW = 3 * 10**10
ANY = pl.BlockSpec(memory_space=pl.ANY)
HBM = pl.BlockSpec(memory_space=pltpu.HBM)
VMEM = pl.BlockSpec(memory_space=pltpu.VMEM)
SMEM = pl.BlockSpec(memory_space=pltpu.SMEM)


def load(refs, into, sems):
    copies = [pltpu.make_async_copy(ref, into.at[at], sems.at[at]) for at, ref in enumerate(refs)]
    for copy in copies:
        copy.start()
    return copies


def hidden_kernel(width, rows, groups, *refs):
    row_refs, unit_refs = refs[:rows], refs[rows : rows + 2 * groups]
    hidden_ref, turned_ref, silu_ref, rest_ref, loaded, sems, units, unit_sems = refs[rows + 2 * groups :]
    step, half = row_refs[0].shape[0], unit_refs[0].shape[1]
    unit_copies = load(unit_refs, units, unit_sems)
    copies = load(row_refs, loaded, sems)
    for copy in unit_copies:
        copy.wait()
    for at, copy in enumerate(copies):
        copy.wait()
        row_ref = loaded.at[at]
        span = slice(at * step, (at + 1) * step)
        for group in range(groups):
            sums = matmul(row_ref[:, :half], units[group], (1, 1))
            sums = sums + matmul(row_ref[:, half:], units[groups + group], (1, 1))
            silu_g, hidden, rest = gated(sums[:, :width], sums[:, width:])
            cols = slice(group * width, (group + 1) * width)
            hidden_ref[span, cols] = hidden.astype(BF16)
            turned_ref[cols, span] = hidden.T.astype(BF16)
            silu_ref[span, cols] = silu_g.astype(BF16)
            rest_ref[span, cols] = rest.astype(BF16)


def grads_kernel(width, rows, *refs):
    row_refs, (silu_any, rest_any, down_ref, act_ref, turned_ref, loaded, sems) = refs[:rows], refs[rows : rows + 7]
    silu_ref, rest_ref, silu_sems, rest_sems = refs[rows + 7 :]
    step = row_refs[0].shape[0]
    spans = [pl.ds(at * step, step) for at in range(rows)]
    copies = load(row_refs, loaded, sems)
    silu_copies = [pltpu.make_async_copy(silu_any.at[s], silu_ref.at[s], silu_sems.at[i]) for i, s in enumerate(spans)]
    rest_copies = [pltpu.make_async_copy(rest_any.at[s], rest_ref.at[s], rest_sems.at[i]) for i, s in enumerate(spans)]
    for copy in silu_copies + rest_copies:
        copy.start()
    for at, copy in enumerate(copies):
        copy.wait()
        silu_copies[at].wait()
        rest_copies[at].wait()
        row_ref = loaded.at[at]
        span = slice(at * step, (at + 1) * step)
        for pair in range(down_ref.shape[0] // (2 * width)):
            units = slice(2 * pair * width, 2 * (pair + 1) * width)
            back = matmul(row_ref[...], down_ref[units], (1, 1))
            for part, factor in enumerate((rest_ref, silu_ref)):
                grads = back * factor[span, units].astype(F32)
                for side in range(2):
                    grad = grads[:, side * width : (side + 1) * width]
                    first = (4 * pair + 2 * side + part) * width
                    low = slice(first, first + width)
                    act_ref[span, low] = grad.astype(BF16)
                    turned_ref[low, span] = grad.T.astype(BF16)


def weight_kernel(first, tile, rows, *refs):
    row_refs, (turned_ref, away_ref, stay_ref, loaded, sems) = refs[:rows], refs[rows:]
    half, step = away_ref.shape[0], row_refs[0].shape[0]
    span = away_ref.shape[1] // 2
    parts = []
    for part in range(2):
        cols = pl.ds(first + part * span, span)
        parts.append(load([ref.at[:, cols] for ref in row_refs], loaded.at[part], sems.at[part]))
    for part, copies in enumerate(parts):
        for copy in copies:
            copy.wait()

        @pl.loop(0, span // tile)
        def _(index):
            here = pl.ds(pl.multiple_of(index * tile, tile), tile)
            cols = pl.ds(pl.multiple_of(part * span + index * tile, tile), tile)
            for out_ref, low in ((away_ref, 0), (stay_ref, half)):
                total = jnp.zeros((half, tile), F32)
                for at in range(rows):
                    left = turned_ref[low : low + half, at * step : (at + 1) * step]
                    total = total + matmul(left, loaded[part, at, :, here], (1, 0))
                out_ref[:, cols] = total.astype(BF16)


def block_kernel(first, places, sides, added, *refs):
    rights, many = len(sides), len(places)
    left_any, right_any, refs = refs[0], refs[1 : 1 + rights], refs[1 + rights :]
    adds, refs = refs[: many * added], refs[many * added :]
    outs, (left_ref, right_ref, sems) = refs[:many], refs[many:]
    depth, half = right_ref.shape[1:]
    copies = [pltpu.make_async_copy(left_any.at[pl.ds(first, left_ref.shape[0])], left_ref, sems.at[0])]
    for at, side in enumerate(sides):
        source = right_any[at].at[:, pl.ds(side * half, half)]
        copies.append(pltpu.make_async_copy(source, right_ref.at[at], sems.at[1 + at]))
    for copy in copies:
        copy.start()
    for copy in copies:
        copy.wait()
    for at, (row, right) in enumerate(places):
        total = matmul(left_ref[row : row + outs[at].shape[0]], right_ref[right], (1, 0))
        if added:
            total = total + adds[at][...].astype(F32)
        outs[at][...] = total.astype(BF16)


def halves_kernel(at_ref, gate_any, up_any, down_any, mine_ref, down_mine_ref, theirs_ref, gate_ref, up_ref, down_ref, sems):
    copies = [
        pltpu.make_async_copy(source, into, sems.at[at])
        for at, (source, into) in enumerate(((gate_any, gate_ref), (up_any, up_ref), (down_any, down_ref)))
    ]
    for copy in copies:
        copy.start()
    for copy in copies:
        copy.wait()
    width = down_mine_ref.shape[0]
    first = at_ref[0] == 0
    for part, ref in enumerate((gate_ref, up_ref)):
        span = slice(part * width, (part + 1) * width)
        low, high = ref[:, :width].astype(F32).T.astype(BF16), ref[:, width:].astype(F32).T.astype(BF16)
        mine_ref[span] = jnp.where(first, low, high)
        theirs_ref[span] = jnp.where(first, high, low)
    low, high = down_ref[:width], down_ref[width:]
    down_mine_ref[...] = jnp.where(first, low, high)
    theirs_ref[2 * width :] = jnp.where(first, high, low)


def take_kernel(in_ref, out_ref):
    out_ref[...] = in_ref[: out_ref.shape[0]]


def fetch_kernel(in_ref, out_ref, sem):
    copy = pltpu.make_async_copy(in_ref, out_ref, sem)
    copy.start()
    copy.wait()


def units_kernel(many, *refs):
    blocks, (out_ref, sems) = refs[: 2 * many], refs[2 * many :]
    step, span = blocks[0].shape
    copies = []
    for at, ref in enumerate(blocks):
        into = out_ref.at[pl.ds(at % many * step, step), pl.ds(at // many * span, span)]
        copies.append(pltpu.make_async_copy(ref, into, sems.at[at]))
    for copy in copies:
        copy.start()
    for copy in copies:
        copy.wait()


def add_kernel(stay_ref, came_ref, own_ref, far_ref):
    half = own_ref.shape[0]
    own_ref[...] = stay_ref[:half].astype(F32) + came_ref[:half].astype(F32)
    far_ref[...] = (stay_ref[half:].astype(F32) + came_ref[half:].astype(F32)).astype(BF16)


def beside_kernel(first, left_ref, right_ref, out_ref):
    rows, half = left_ref.shape
    out_ref[:, :half] = left_ref[...]
    out_ref[:, half:] = right_ref[first : first + rows]


def halves_beside_kernel(left_ref, top_ref, low_ref, out_ref):
    half, step = left_ref.shape[1], top_ref.shape[0]
    out_ref[:, :half] = left_ref[...]
    out_ref[:step, half:] = top_ref[...]
    out_ref[step:, half:] = low_ref[...]


def stack_kernel(*refs):
    out_ref, step = refs[-1], refs[0].shape[0]
    for at, ref in enumerate(refs[:-1]):
        out_ref[at * step : (at + 1) * step] = ref[...]


def finish_kernel(at_ref, mine_ref, theirs_ref, gate_ref, up_ref):
    width = mine_ref.shape[0] // 2
    for part, out_ref in enumerate((gate_ref, up_ref)):
        span = slice(part * width, (part + 1) * width)
        mine, theirs = mine_ref[span].astype(F32).T, theirs_ref[span].astype(F32).T
        first = at_ref[0] == 0
        out_ref[:, :width] = jnp.where(first, mine, theirs)
        out_ref[:, width:] = jnp.where(first, theirs, mine)


def beside(left, right, first=0, after=()):
    out = [shape(left.shape[0], 2 * left.shape[1])]
    return call(functools.partial(beside_kernel, first), out, 0, [left, right], after)[0]


def stacked(parts, after=()):
    return call(stack_kernel, [shape(len(parts) * parts[0].shape[0], parts[0].shape[1])], 0, parts, after)[0]


def taken(array, rows, after):
    return call(take_kernel, [shape(rows, array.shape[1])], 0, [array], after)[0]


def fetched(array, after):
    scratch = [pltpu.SemaphoreType.DMA]
    return call(fetch_kernel, [shape(*array.shape)], 0, [array], after, specs=[HBM], scratch=scratch)[0]


class Square:
    def core(self, array):
        return lax.ppermute(array, "inp", [(at, at ^ 1) for at in range(4)])

    def across(self, array):
        return lax.ppermute(array, "inp", [(at, at ^ 2) for at in range(4)])

    def other(self, array):
        return lax.ppermute(array, "out", [(0, 1), (1, 0)])

    def near(self, array):
        return lax.ppermute(array, "wt", [(at, at ^ 1) for at in range(4)])

    def far(self, array):
        return lax.ppermute(array, "wt", [(at, at ^ 2) for at in range(4)])

    def scatter_units(self, came, stay, flops=0):
        half, cols = stay.shape[0] // 2, stay.shape[1]
        outs = [shape(half, cols, dtype=F32), shape(half, cols)]
        own, far = call(add_kernel, outs, flops, [stay, came])
        return own + self.far(far).astype(F32)

    def products(self, left, rights, places, adds=(), after=()):
        far = int(not adds)
        quarter, depth = left.shape[0] // 4, left.shape[1]
        half = rights[0][2]
        outs = [shape(quarter, half)] * len(places)
        use = sorted({other for _, other in places})
        chips = sorted({chip for chip, _ in places})
        first = 2 * far * quarter + chips[0] * quarter
        wanted = [((chip - chips[0]) * quarter, use.index(other)) for chip, other in places]
        args = [left] + [rights[other][0] for other in use] + [adds[place] for place in places if adds]
        blocks = call(
            functools.partial(block_kernel, first, wanted, [rights[other][1] for other in use], bool(adds)),
            outs,
            2 * len(places) * quarter * depth * half,
            args,
            after,
            specs=[ANY] * (1 + len(use)) + [VMEM] * (len(args) - 1 - len(use)),
            scratch=[
                pltpu.VMEM((len(chips) * quarter, depth), BF16),
                pltpu.VMEM((len(use), depth, half), BF16),
                pltpu.SemaphoreType.DMA((1 + len(use),)),
            ],
        )
        return dict(zip(places, blocks))

    def scatter_far(self, left, rights, after=()):
        first = self.products(left, rights, [(1, 1)], after=after)
        second = self.products(left, rights, [(0, 1), (1, 0), (0, 0)], after=list(first.values()))
        return first | second

    def near_first(self, left, rights, far, after):
        return self.products(left, rights, [(1, 1)], far, after)

    def near_rest(self, left, rights, far, after):
        return self.products(left, rights, [(0, 1), (1, 0), (0, 0)], far, after)

    def layer(self, tokens, gate_weight, up_weight, down_weight, cotangent):
        at_out = lax.axis_index("out").astype(jnp.int32).reshape(1)
        half, width = gate_weight.shape[0], gate_weight.shape[1] // 2
        mine, down_mine, theirs = call(
            halves_kernel,
            [shape(2 * width, half), shape(width, half), shape(3 * width, half)],
            0,
            [at_out, gate_weight, up_weight, down_weight],
            specs=[SMEM, HBM, HBM, HBM],
            scratch=[
                pltpu.VMEM(gate_weight.shape, BF16),
                pltpu.VMEM(up_weight.shape, BF16),
                pltpu.VMEM(down_weight.shape, BF16),
                pltpu.SemaphoreType.DMA((3,)),
            ],
        )
        came = self.other(theirs)
        step = tokens.shape[1]
        tok, cot = tokens.reshape(2 * step, half), cotangent.reshape(2 * step, half)

        tok_near = self.near(tok)
        far_mine, across_mine = self.far(mine), self.across(mine)
        tok_other = self.other(fetched(tok, [came, tok_near, across_mine, far_mine]))
        theirs = taken(came, 2 * width, [far_mine, across_mine])
        tok_corner = self.other(taken(tok_near, 2 * step, [far_mine]))
        far_theirs, across_theirs = self.far(theirs), self.across(theirs)
        corner_mine = self.across(far_mine)
        corner_theirs = self.across(far_theirs)
        unit_groups = [across_mine, corner_mine, mine, far_mine, across_theirs, corner_theirs, theirs, far_theirs]
        own_down = beside(down_mine, came, 2 * width, [far_theirs, across_theirs, corner_mine])
        far_down = self.far(own_down)
        cot_near = self.near(fetched(cot, [tok_near]))
        tok_top = beside(tok, tok_other)
        tok_low = beside(tok_near, tok_corner, 0, [corner_theirs, far_down, cot_near])
        rows_in = [tok_top, tok_low, self.core(tok_top), self.core(tok_low)]
        cot_other = self.other(fetched(cot, [tok_corner, corner_theirs, rows_in[2]]))
        down_groups = [self.across(own_down), self.across(far_down), own_down, far_down]

        count, units = 8 * step, 4 * width
        hidden, hidden_turned, silu, rest = call(
            functools.partial(hidden_kernel, width, 4, 4),
            [shape(count, units), shape(units, count), shape(count, units), shape(count, units)],
            8 * count * units * half,
            [*rows_in, *unit_groups],
            after=down_groups[:2],
            specs=[HBM] * (4 + len(unit_groups)),
            scratch=[
                pltpu.VMEM((4, 2 * step, 2 * half), BF16),
                pltpu.SemaphoreType.DMA((4,)),
                pltpu.VMEM((len(unit_groups), 2 * width, half), BF16),
                pltpu.SemaphoreType.DMA((len(unit_groups),)),
            ],
            limit=30,
        )
        cot_corner = [self.other(cot_near[:step]), self.near(cot_other[step:])]
        cot_top = beside(cot, cot_other, 0, [hidden])
        outs = [shape(2 * step, 2 * half)]
        (cot_low,) = call(halves_beside_kernel, outs, 0, [cot_near, *cot_corner], [hidden])
        rows_cot = [cot_top, cot_low, self.core(cot_top), self.core(cot_low)]
        down = stacked(down_groups)
        down_sides = [(down, 0, half), (down, 1, half)]
        output_far = self.scatter_far(hidden, down_sides)
        down_terms = call(
            functools.partial(weight_kernel, 0, 256, 4),
            [shape(units // 2, 2 * half)] * 2,
            4 * count * units * half,
            [*rows_cot, hidden_turned],
            list(output_far.values()),
            specs=[HBM] * 4 + [VMEM],
            scratch=[pltpu.VMEM((2, 4, 2 * step, half), BF16), pltpu.SemaphoreType.DMA((2, 4))],
        )
        down_sum = self.scatter_units(self.across(down_terms[0]), down_terms[1])
        act, act_turned = call(
            functools.partial(grads_kernel, width, 4),
            [shape(count, 2 * units), shape(2 * units, count)],
            4 * count * units * half,
            [*rows_cot, silu, rest, down],
            after=down_terms,
            specs=[HBM] * 6 + [VMEM],
            scratch=[
                pltpu.VMEM((4, 2 * step, 2 * half), BF16),
                pltpu.SemaphoreType.DMA((4,)),
                pltpu.VMEM((count, units), BF16),
                pltpu.VMEM((count, units), BF16),
                pltpu.SemaphoreType.DMA((4,)),
                pltpu.SemaphoreType.DMA((4,)),
            ],
            limit=30,
        )
        output_far = {place: self.core(block) for place, block in output_far.items()}
        sums = self.near_first(hidden, down_sides, output_far, [act])
        corner = sums[1, 1]
        by_other, by_near = self.other(corner[:step]), self.near(corner[step:])
        sums |= self.near_rest(hidden, down_sides, output_far, [corner])

        def unit_terms(side, after):
            return call(
                functools.partial(weight_kernel, side * half, 256, 4),
                [shape(units, half)] * 2,
                4 * count * units * half,
                [*rows_in, act_turned],
                after=after,
                specs=[HBM] * 4 + [VMEM],
                scratch=[pltpu.VMEM((2, 4, 2 * step, half // 2), BF16), pltpu.SemaphoreType.DMA((2, 4))],
            )

        other_terms = unit_terms(1, [sums[0, 0]])
        other_sum = self.scatter_units(self.across(other_terms[0]), other_terms[1], SLOW).astype(BF16)
        (gate_up,) = call(
            functools.partial(units_kernel, 4),
            [shape(2 * units, 2 * half)],
            0,
            unit_groups,
            [other_terms[0]],
            specs=[HBM] * 8,
            scratch=[pltpu.SemaphoreType.DMA((8,))],
        )
        unit_sides = [(gate_up, 0, half), (gate_up, 1, half)]
        grads_far = self.scatter_far(act, unit_sides, [by_other, by_near])
        zeros = jnp.zeros((step, half), F32)
        to_near = (sums[1, 0].astype(F32) + jnp.concatenate([by_other.astype(F32), zeros])).astype(BF16)
        to_other = (sums[0, 1].astype(F32) + jnp.concatenate([zeros, by_near.astype(F32)])).astype(BF16)
        by_near, by_other = self.near(to_near), self.other(to_other)
        total = sums[0, 0].astype(F32) + by_near.astype(F32) + by_other.astype(F32)
        output = total.astype(BF16).reshape(2, step, half)

        own_terms = unit_terms(0, list(grads_far.values()))
        own_came = self.across(own_terms[0])
        own_sum = self.scatter_units(own_came, own_terms[1], SLOW).astype(BF16)
        grads_far = {place: self.core(block) for place, block in grads_far.items()}
        sums = self.near_first(act, unit_sides, grads_far, [own_terms[0], by_other])
        by_other = self.other(sums[1, 1])
        sums |= self.near_rest(act, unit_sides, grads_far, [sums[1, 1], by_near, own_came])
        to_near = (sums[1, 0].astype(F32) + by_other.astype(F32)).astype(BF16)
        by_near, by_other = self.near(to_near), self.other(sums[0, 1])
        total = sums[0, 0].astype(F32) + by_near.astype(F32) + by_other.astype(F32)
        grad_tokens = total.astype(BF16).reshape(2, step, half)

        down_back = self.other(down_sum[:, half:].astype(BF16))
        units_back = self.other(other_sum)
        mine, theirs = down_sum[:, :half], down_back.astype(F32)
        first = at_out[0] == 0
        grad_down = jnp.where(first, jnp.concatenate([mine, theirs]), jnp.concatenate([theirs, mine]))
        grad_gate, grad_up = call(
            finish_kernel,
            [shape(half, 2 * width, dtype=F32)] * 2,
            0,
            [at_out, own_sum, units_back],
            specs=[SMEM, VMEM, VMEM],
        )
        return (output, grad_tokens, grad_gate, grad_up, grad_down)


class Plain:
    def units(self, weight):
        own = lax.all_to_all(weight, "out", split_axis=0, concat_axis=1, tiled=True)
        return lax.all_gather(own, "wt", axis=0, tiled=True)

    def unit_sums(self, grad):
        own = lax.psum_scatter(grad.astype(BF16), "wt", scatter_dimension=0, tiled=True)
        return lax.all_to_all(own, "out", split_axis=1, concat_axis=0, tiled=True).astype(F32)

    def gather(self, array):
        array = lax.all_gather(lax.all_gather(array, "inp", axis=1, tiled=True), "out", axis=2, tiled=True)
        return array.reshape(-1, array.shape[2])

    def scatter(self, partial, batches):
        partial = partial.astype(BF16).reshape(batches, -1, partial.shape[1])
        partial = lax.psum_scatter(partial, "out", scatter_dimension=2, tiled=True)
        return lax.psum_scatter(partial, "inp", scatter_dimension=1, tiled=True)

    def layer(self, tokens, gate_weight, up_weight, down_weight, cotangent):
        gate, up, down = self.units(gate_weight.T), self.units(up_weight.T), self.units(down_weight)
        rows_in, rows_cot = self.gather(tokens), self.gather(cotangent)
        gate_sum = matmul(rows_in, gate, (1, 1))
        up_sum = matmul(rows_in, up, (1, 1))
        silu_g, hidden, rest = gated(gate_sum, up_sum)
        hidden = hidden.astype(BF16)
        grad_down = self.unit_sums(matmul(hidden, rows_cot, (0, 0)))
        back_sum = matmul(rows_cot, down, (1, 1))
        gate_act, up_act = (back_sum * rest).astype(BF16), (back_sum * silu_g).astype(BF16)
        grad_gate = self.unit_sums(matmul(gate_act, rows_in, (0, 0))).T
        grad_up = self.unit_sums(matmul(up_act, rows_in, (0, 0))).T
        output = self.scatter(matmul(hidden, down, (1, 0)), tokens.shape[0])
        partial = matmul(gate_act, gate, (1, 0)) + matmul(up_act, up, (1, 0))
        grad_tokens = self.scatter(partial, tokens.shape[0])
        return (output, grad_tokens, grad_gate, grad_up, grad_down)


def solution(mesh):
    square = mesh.shape["inp"] == 4 and mesh.shape["out"] == 2 and mesh.shape["wt"] == 4

    def on_device(tokens, *others):
        places = Square() if square and tokens.shape[0] == 2 else Plain()
        return places.layer(tokens, *others)

    rows_spec = P(None, ("inp", "wt"), "out")
    in_spec = P("out", ("wt", "inp"))
    down_spec = P(("wt", "inp"), "out")
    return jax.shard_map(
        on_device,
        mesh=mesh,
        in_specs=(rows_spec, in_spec, in_spec, down_spec, rows_spec),
        out_specs=(rows_spec, rows_spec, in_spec, in_spec, down_spec),
        check_vma=False,
    )
```

```python
import functools

import jax
import jax.numpy as jnp
from jax import lax
from jax.experimental import pallas as pl
from jax.experimental.pallas import tpu as pltpu
from jax.sharding import PartitionSpec as P

F32 = jnp.float32
BF16 = jnp.bfloat16
MIB = 1024 * 1024


def matmul(a, b, contract):
    return lax.dot_general(a, b, ((contract[:1], contract[1:]), ((), ())), preferred_element_type=F32)


def gated(gate_sum, up_sum):
    sigmoid_g = jax.nn.sigmoid(gate_sum)
    silu_g = gate_sum * sigmoid_g
    slope = sigmoid_g * (1.0 + gate_sum * (1.0 - sigmoid_g))
    return silu_g, silu_g * up_sum, up_sum * slope


def shape(*dims, dtype=BF16):
    return jax.ShapeDtypeStruct(dims, dtype)


def call(kernel, outs, flops, args, after=(), specs=None, scratch=(), limit=24):
    everything = [*args, *after]
    moved = sum(a.size * a.dtype.itemsize for a in args) + sum(o.size * o.dtype.itemsize for o in outs)
    specs = specs or [pl.BlockSpec(memory_space=pltpu.VMEM)] * len(args)

    def body(*refs):
        kernel(*refs[: len(args)], *refs[len(everything) :])

    return pl.pallas_call(
        body,
        out_shape=list(outs),
        in_specs=[*specs, *[pl.BlockSpec(memory_space=pl.ANY)] * len(after)],
        out_specs=[pl.BlockSpec(memory_space=pltpu.VMEM)] * len(outs),
        scratch_shapes=list(scratch),
        compiler_params=pltpu.CompilerParams(vmem_limit_bytes=limit * MIB),
        cost_estimate=pl.CostEstimate(flops=flops // SHARE, bytes_accessed=moved // SHARE, transcendentals=0),
    )(*everything)


SHARE = 1
ANY = pl.BlockSpec(memory_space=pl.ANY)
HBM = pl.BlockSpec(memory_space=pltpu.HBM)
VMEM = pl.BlockSpec(memory_space=pltpu.VMEM)
SMEM = pl.BlockSpec(memory_space=pltpu.SMEM)


def load(refs, into, sems):
    copies = [pltpu.make_async_copy(ref, into.at[at], sems.at[at]) for at, ref in enumerate(refs)]
    for copy in copies:
        copy.start()
    return copies


def hidden_kernel(width, rows, groups, *refs):
    row_refs, unit_refs = refs[:rows], refs[rows : rows + 2 * groups]
    hidden_ref, turned_ref, silu_ref, rest_ref, loaded, sems, units, unit_sems = refs[rows + 2 * groups :]
    step, half = row_refs[0].shape[0], unit_refs[0].shape[1]
    unit_copies = load(unit_refs, units, unit_sems)
    copies = load(row_refs, loaded, sems)
    for copy in unit_copies:
        copy.wait()
    for at, copy in enumerate(copies):
        copy.wait()
        row_ref = loaded.at[at]
        span = slice(at * step, (at + 1) * step)
        for group in range(groups):
            sums = matmul(row_ref[:, :half], units[group], (1, 1))
            sums = sums + matmul(row_ref[:, half:], units[groups + group], (1, 1))
            silu_g, hidden, rest = gated(sums[:, :width], sums[:, width:])
            cols = slice(group * width, (group + 1) * width)
            hidden_ref[span, cols] = hidden.astype(BF16)
            turned_ref[cols, span] = hidden.T.astype(BF16)
            silu_ref[span, cols] = silu_g.astype(BF16)
            rest_ref[span, cols] = rest.astype(BF16)


def grads_kernel(width, rows, *refs):
    row_refs, (silu_any, rest_any, down_ref, act_ref, turned_ref, loaded, sems) = refs[:rows], refs[rows : rows + 7]
    silu_ref, rest_ref, silu_sems, rest_sems = refs[rows + 7 :]
    step = row_refs[0].shape[0]
    spans = [pl.ds(at * step, step) for at in range(rows)]
    copies = load(row_refs, loaded, sems)
    silu_copies = [pltpu.make_async_copy(silu_any.at[s], silu_ref.at[s], silu_sems.at[i]) for i, s in enumerate(spans)]
    rest_copies = [pltpu.make_async_copy(rest_any.at[s], rest_ref.at[s], rest_sems.at[i]) for i, s in enumerate(spans)]
    for copy in silu_copies + rest_copies:
        copy.start()
    for at, copy in enumerate(copies):
        copy.wait()
        silu_copies[at].wait()
        rest_copies[at].wait()
        row_ref = loaded.at[at]
        span = slice(at * step, (at + 1) * step)
        for pair in range(down_ref.shape[0] // (2 * width)):
            units = slice(2 * pair * width, 2 * (pair + 1) * width)
            back = matmul(row_ref[...], down_ref[units], (1, 1))
            for part, factor in enumerate((rest_ref, silu_ref)):
                grads = back * factor[span, units].astype(F32)
                for side in range(2):
                    grad = grads[:, side * width : (side + 1) * width]
                    first = (4 * pair + 2 * side + part) * width
                    low = slice(first, first + width)
                    act_ref[span, low] = grad.astype(BF16)
                    turned_ref[low, span] = grad.T.astype(BF16)


def weight_kernel(first, tile, rows, *refs):
    row_refs, (turned_ref, away_ref, stay_ref, loaded, sems) = refs[:rows], refs[rows:]
    half, step = away_ref.shape[0], row_refs[0].shape[0]
    span = away_ref.shape[1] // 2
    parts = []
    for part in range(2):
        cols = pl.ds(first + part * span, span)
        parts.append(load([ref.at[:, cols] for ref in row_refs], loaded.at[part], sems.at[part]))
    for part, copies in enumerate(parts):
        for copy in copies:
            copy.wait()

        @pl.loop(0, span // tile)
        def _(index):
            here = pl.ds(pl.multiple_of(index * tile, tile), tile)
            cols = pl.ds(pl.multiple_of(part * span + index * tile, tile), tile)
            for out_ref, low in ((away_ref, 0), (stay_ref, half)):
                total = jnp.zeros((half, tile), F32)
                for at in range(rows):
                    left = turned_ref[low : low + half, at * step : (at + 1) * step]
                    total = total + matmul(left, loaded[part, at, :, here], (1, 0))
                out_ref[:, cols] = total.astype(BF16)


def block_kernel(first, places, sides, added, *refs):
    rights, many = len(sides), len(places)
    left_any, right_any, refs = refs[0], refs[1 : 1 + rights], refs[1 + rights :]
    adds, refs = refs[: many * added], refs[many * added :]
    outs, (left_ref, right_ref, sems) = refs[:many], refs[many:]
    depth, half = right_ref.shape[1:]
    copies = [pltpu.make_async_copy(left_any.at[pl.ds(first, left_ref.shape[0])], left_ref, sems.at[0])]
    for at, side in enumerate(sides):
        source = right_any[at].at[:, pl.ds(side * half, half)]
        copies.append(pltpu.make_async_copy(source, right_ref.at[at], sems.at[1 + at]))
    for copy in copies:
        copy.start()
    for copy in copies:
        copy.wait()
    for at, (row, right) in enumerate(places):
        total = matmul(left_ref[row : row + outs[at].shape[0]], right_ref[right], (1, 0))
        if added:
            total = total + adds[at][...].astype(F32)
        outs[at][...] = total.astype(BF16)


def halves_kernel(at_ref, gate_any, up_any, down_any, mine_ref, down_mine_ref, theirs_ref, gate_ref, up_ref, down_ref, sems):
    copies = [
        pltpu.make_async_copy(source, into, sems.at[at])
        for at, (source, into) in enumerate(((gate_any, gate_ref), (up_any, up_ref), (down_any, down_ref)))
    ]
    for copy in copies:
        copy.start()
    for copy in copies:
        copy.wait()
    width = down_mine_ref.shape[0]
    first = at_ref[0] == 0
    for part, ref in enumerate((gate_ref, up_ref)):
        span = slice(part * width, (part + 1) * width)
        low, high = ref[:, :width].astype(F32).T.astype(BF16), ref[:, width:].astype(F32).T.astype(BF16)
        mine_ref[span] = jnp.where(first, low, high)
        theirs_ref[span] = jnp.where(first, high, low)
    low, high = down_ref[:width], down_ref[width:]
    down_mine_ref[...] = jnp.where(first, low, high)
    theirs_ref[2 * width :] = jnp.where(first, high, low)


def take_kernel(in_ref, out_ref):
    out_ref[...] = in_ref[: out_ref.shape[0]]


def fetch_kernel(in_ref, out_ref, sem):
    copy = pltpu.make_async_copy(in_ref, out_ref, sem)
    copy.start()
    copy.wait()


def units_kernel(many, *refs):
    blocks, (out_ref, sems) = refs[: 2 * many], refs[2 * many :]
    step, span = blocks[0].shape
    copies = []
    for at, ref in enumerate(blocks):
        into = out_ref.at[pl.ds(at % many * step, step), pl.ds(at // many * span, span)]
        copies.append(pltpu.make_async_copy(ref, into, sems.at[at]))
    for copy in copies:
        copy.start()
    for copy in copies:
        copy.wait()


def sum_kernel(left_ref, right_ref, out_ref):
    out_ref[...] = (left_ref[...].astype(F32) + right_ref[...].astype(F32)).astype(BF16)


def add_kernel(stay_ref, came_ref, own_ref, far_ref):
    half = own_ref.shape[0]
    own_ref[...] = stay_ref[:half].astype(F32) + came_ref[:half].astype(F32)
    far_ref[...] = (stay_ref[half:].astype(F32) + came_ref[half:].astype(F32)).astype(BF16)


def beside_kernel(first, left_ref, right_ref, out_ref):
    rows, half = left_ref.shape
    out_ref[:, :half] = left_ref[...]
    out_ref[:, half:] = right_ref[first : first + rows]


def halves_beside_kernel(left_ref, top_ref, low_ref, out_ref):
    half, step = left_ref.shape[1], top_ref.shape[0]
    out_ref[:, :half] = left_ref[...]
    out_ref[:step, half:] = top_ref[...]
    out_ref[step:, half:] = low_ref[...]


def stack_kernel(*refs):
    out_ref, step = refs[-1], refs[0].shape[0]
    for at, ref in enumerate(refs[:-1]):
        out_ref[at * step : (at + 1) * step] = ref[...]


def finish_kernel(at_ref, mine_ref, theirs_ref, gate_ref, up_ref):
    width = mine_ref.shape[0] // 2
    for part, out_ref in enumerate((gate_ref, up_ref)):
        span = slice(part * width, (part + 1) * width)
        mine, theirs = mine_ref[span].astype(F32).T, theirs_ref[span].astype(F32).T
        first = at_ref[0] == 0
        out_ref[:, :width] = jnp.where(first, mine, theirs)
        out_ref[:, width:] = jnp.where(first, theirs, mine)


def beside(left, right, first=0, after=()):
    out = [shape(left.shape[0], 2 * left.shape[1])]
    return call(functools.partial(beside_kernel, first), out, 0, [left, right], after)[0]


def stacked(parts, after=()):
    return call(stack_kernel, [shape(len(parts) * parts[0].shape[0], parts[0].shape[1])], 0, parts, after)[0]


def taken(array, rows, after):
    return call(take_kernel, [shape(rows, array.shape[1])], 0, [array], after)[0]


def fetched(array, after):
    scratch = [pltpu.SemaphoreType.DMA]
    return call(fetch_kernel, [shape(*array.shape)], 0, [array], after, specs=[HBM], scratch=scratch)[0]


class Square:
    def core(self, array):
        return lax.ppermute(array, "inp", [(at, at ^ 1) for at in range(4)])

    def across(self, array):
        return lax.ppermute(array, "inp", [(at, at ^ 2) for at in range(4)])

    def other(self, array):
        return lax.ppermute(array, "out", [(0, 1), (1, 0)])

    def near(self, array):
        return lax.ppermute(array, "wt", [(at, at ^ 1) for at in range(4)])

    def far(self, array):
        return lax.ppermute(array, "wt", [(at, at ^ 2) for at in range(4)])

    def added(self, stay, came):
        half, cols = stay.shape[0] // 2, stay.shape[1]
        return call(add_kernel, [shape(half, cols, dtype=F32), shape(half, cols)], 0, [stay, came])

    def products(self, left, rights, places, adds=(), after=()):
        far = int(not adds)
        quarter, depth = left.shape[0] // 4, left.shape[1]
        half = rights[0][2]
        outs = [shape(quarter, half)] * len(places)
        use = sorted({other for _, other in places})
        chips = sorted({chip for chip, _ in places})
        first = 2 * far * quarter + chips[0] * quarter
        wanted = [((chip - chips[0]) * quarter, use.index(other)) for chip, other in places]
        args = [left] + [rights[other][0] for other in use] + [adds[place] for place in places if adds]
        blocks = call(
            functools.partial(block_kernel, first, wanted, [rights[other][1] for other in use], bool(adds)),
            outs,
            2 * len(places) * quarter * depth * half,
            args,
            after,
            specs=[ANY] * (1 + len(use)) + [VMEM] * (len(args) - 1 - len(use)),
            scratch=[
                pltpu.VMEM((len(chips) * quarter, depth), BF16),
                pltpu.VMEM((len(use), depth, half), BF16),
                pltpu.SemaphoreType.DMA((1 + len(use),)),
            ],
        )
        return dict(zip(places, blocks))

    def scatter_far(self, left, rights, after=()):
        first = self.products(left, rights, [(1, 1)], after=after)
        second = self.products(left, rights, [(0, 1), (1, 0), (0, 0)], after=list(first.values()))
        return first | second

    def near_first(self, left, rights, far, after):
        return self.products(left, rights, [(1, 1)], far, after)

    def near_rest(self, left, rights, far, after):
        return self.products(left, rights, [(0, 1), (1, 0), (0, 0)], far, after)

    def layer(self, tokens, gate_weight, up_weight, down_weight, cotangent):
        at_out = lax.axis_index("out").astype(jnp.int32).reshape(1)
        half, width = gate_weight.shape[0], gate_weight.shape[1] // 2
        mine, down_mine, theirs = call(
            halves_kernel,
            [shape(2 * width, half), shape(width, half), shape(3 * width, half)],
            0,
            [at_out, gate_weight, up_weight, down_weight],
            specs=[SMEM, HBM, HBM, HBM],
            scratch=[
                pltpu.VMEM(gate_weight.shape, BF16),
                pltpu.VMEM(up_weight.shape, BF16),
                pltpu.VMEM(down_weight.shape, BF16),
                pltpu.SemaphoreType.DMA((3,)),
            ],
        )
        came = self.other(theirs)
        step = tokens.shape[1]
        tok, cot = tokens.reshape(2 * step, half), cotangent.reshape(2 * step, half)

        tok_near = self.near(tok)
        far_mine, across_mine = self.far(mine), self.across(mine)
        tok_other = self.other(fetched(tok, [came, across_mine]))
        theirs = taken(came, 2 * width, [far_mine, across_mine])
        tok_corner = self.other(taken(tok_near, 2 * step, [far_mine]))
        far_theirs, across_theirs = self.far(theirs), self.across(theirs)
        corner_mine = self.across(far_mine)
        corner_theirs = self.across(far_theirs)
        unit_groups = [across_mine, corner_mine, mine, far_mine, across_theirs, corner_theirs, theirs, far_theirs]
        own_down = beside(down_mine, came, 2 * width, [far_theirs])
        far_down = self.far(own_down)
        cot_near = self.near(fetched(cot, [tok_near]))
        late_cot = fetched(cot, [tok_corner, corner_mine, across_theirs, corner_theirs, cot_near])
        cot_other = self.other(late_cot)
        tok_top = beside(tok, tok_other)
        tok_low = beside(tok_near, tok_corner, 0, [late_cot, own_down])
        rows_in = [tok_top, tok_low, self.core(tok_top), self.core(tok_low)]
        down_groups = [self.across(own_down), self.across(far_down), own_down, far_down]

        count, units = 8 * step, 4 * width
        hidden, hidden_turned, silu, rest = call(
            functools.partial(hidden_kernel, width, 4, 4),
            [shape(count, units), shape(units, count), shape(count, units), shape(count, units)],
            8 * count * units * half,
            [*rows_in, *unit_groups],
            after=[far_down, down_groups[0], cot_near],
            specs=[HBM] * (4 + len(unit_groups)),
            scratch=[
                pltpu.VMEM((4, 2 * step, 2 * half), BF16),
                pltpu.SemaphoreType.DMA((4,)),
                pltpu.VMEM((len(unit_groups), 2 * width, half), BF16),
                pltpu.SemaphoreType.DMA((len(unit_groups),)),
            ],
            limit=30,
        )
        cot_corner = [self.other(cot_near[:step]), self.near(cot_other[step:])]
        cot_top = beside(cot, cot_other, 0, [hidden])
        outs = [shape(2 * step, 2 * half)]
        (cot_low,) = call(halves_beside_kernel, outs, 0, [cot_near, *cot_corner], [hidden])
        rows_cot = [cot_top, cot_low, self.core(cot_top), self.core(cot_low)]
        down = stacked(down_groups)
        down_sides = [(down, 0, half), (down, 1, half)]
        output_far = self.scatter_far(hidden, down_sides)
        down_terms = call(
            functools.partial(weight_kernel, 0, 256, 4),
            [shape(units // 2, 2 * half)] * 2,
            4 * count * units * half,
            [*rows_cot, hidden_turned],
            list(output_far.values()),
            specs=[HBM] * 4 + [VMEM],
            scratch=[pltpu.VMEM((2, 4, 2 * step, half), BF16), pltpu.SemaphoreType.DMA((2, 4))],
        )
        down_half, down_far = self.added(down_terms[1], self.across(down_terms[0]))
        down_came = self.far(down_far)
        act, act_turned = call(
            functools.partial(grads_kernel, width, 4),
            [shape(count, 2 * units), shape(2 * units, count)],
            4 * count * units * half,
            [*rows_cot, silu, rest, down],
            after=down_terms,
            specs=[HBM] * 6 + [VMEM],
            scratch=[
                pltpu.VMEM((4, 2 * step, 2 * half), BF16),
                pltpu.SemaphoreType.DMA((4,)),
                pltpu.VMEM((count, units), BF16),
                pltpu.VMEM((count, units), BF16),
                pltpu.SemaphoreType.DMA((4,)),
                pltpu.SemaphoreType.DMA((4,)),
            ],
            limit=30,
        )
        output_far = {place: self.core(block) for place, block in output_far.items()}
        sums = self.near_first(hidden, down_sides, output_far, [act])
        corner = sums[1, 1]
        by_other, by_near = self.other(corner[:step]), self.near(corner[step:])
        sums |= self.near_rest(hidden, down_sides, output_far, [corner])

        def unit_terms(side, after):
            return call(
                functools.partial(weight_kernel, side * half, 256, 4),
                [shape(units, half)] * 2,
                4 * count * units * half,
                [*rows_in, act_turned],
                after=after,
                specs=[HBM] * 4 + [VMEM],
                scratch=[pltpu.VMEM((2, 4, 2 * step, half // 2), BF16), pltpu.SemaphoreType.DMA((2, 4))],
            )

        other_terms = unit_terms(1, [sums[0, 0]])
        other_half, other_far = self.added(other_terms[1], self.across(other_terms[0]))
        other_came = self.far(other_far)
        (gate_up,) = call(
            functools.partial(units_kernel, 4),
            [shape(2 * units, 2 * half)],
            0,
            unit_groups,
            [other_terms[0], down_far],
            specs=[HBM] * 8,
            scratch=[pltpu.SemaphoreType.DMA((8,))],
        )
        unit_sides = [(gate_up, 0, half), (gate_up, 1, half)]
        grads_far = self.scatter_far(act, unit_sides, [by_other, by_near])
        zeros = jnp.zeros((step, half), F32)
        to_near = (sums[1, 0].astype(F32) + jnp.concatenate([by_other.astype(F32), zeros])).astype(BF16)
        to_other = (sums[0, 1].astype(F32) + jnp.concatenate([zeros, by_near.astype(F32)])).astype(BF16)
        by_near, by_other = self.near(to_near), self.other(to_other)
        total = sums[0, 0].astype(F32) + by_near.astype(F32) + by_other.astype(F32)
        output = total.astype(BF16).reshape(2, step, half)

        own_terms = unit_terms(0, list(grads_far.values()))
        own_half, own_far = self.added(own_terms[1], self.across(own_terms[0]))
        own_came = self.far(own_far)
        grads_far = {place: self.core(block) for place, block in grads_far.items()}
        sums = self.near_first(act, unit_sides, grads_far, [own_terms[0], by_other, by_near, other_far, down_came, *grads_far.values()])
        by_other = self.other(sums[1, 1])
        sums |= self.near_rest(act, unit_sides, grads_far, [sums[1, 1], other_came])
        (to_near,) = call(sum_kernel, [shape(2 * step, half)], 0, [sums[1, 0], by_other], [own_far])
        by_near, by_other = self.near(to_near), self.other(sums[0, 1])
        total = sums[0, 0].astype(F32) + by_near.astype(F32) + by_other.astype(F32)
        grad_tokens = total.astype(BF16).reshape(2, step, half)

        down_sum = down_half + down_came.astype(F32)
        other_sum = (other_half + other_came.astype(F32)).astype(BF16)
        own_sum = (own_half + own_came.astype(F32)).astype(BF16)
        down_back = self.other(down_sum[:, half:].astype(BF16))
        units_back = self.other(other_sum)
        mine, theirs = down_sum[:, :half], down_back.astype(F32)
        first = at_out[0] == 0
        grad_down = jnp.where(first, jnp.concatenate([mine, theirs]), jnp.concatenate([theirs, mine]))
        grad_gate, grad_up = call(
            finish_kernel,
            [shape(half, 2 * width, dtype=F32)] * 2,
            0,
            [at_out, own_sum, units_back],
            specs=[SMEM, VMEM, VMEM],
        )
        return (output, grad_tokens, grad_gate, grad_up, grad_down)


class Plain:
    def units(self, weight):
        own = lax.all_to_all(weight, "out", split_axis=0, concat_axis=1, tiled=True)
        return lax.all_gather(own, "wt", axis=0, tiled=True)

    def unit_sums(self, grad):
        own = lax.psum_scatter(grad.astype(BF16), "wt", scatter_dimension=0, tiled=True)
        return lax.all_to_all(own, "out", split_axis=1, concat_axis=0, tiled=True).astype(F32)

    def gather(self, array):
        array = lax.all_gather(lax.all_gather(array, "inp", axis=1, tiled=True), "out", axis=2, tiled=True)
        return array.reshape(-1, array.shape[2])

    def scatter(self, partial, batches):
        partial = partial.astype(BF16).reshape(batches, -1, partial.shape[1])
        partial = lax.psum_scatter(partial, "out", scatter_dimension=2, tiled=True)
        return lax.psum_scatter(partial, "inp", scatter_dimension=1, tiled=True)

    def layer(self, tokens, gate_weight, up_weight, down_weight, cotangent):
        gate, up, down = self.units(gate_weight.T), self.units(up_weight.T), self.units(down_weight)
        rows_in, rows_cot = self.gather(tokens), self.gather(cotangent)
        gate_sum = matmul(rows_in, gate, (1, 1))
        up_sum = matmul(rows_in, up, (1, 1))
        silu_g, hidden, rest = gated(gate_sum, up_sum)
        hidden = hidden.astype(BF16)
        grad_down = self.unit_sums(matmul(hidden, rows_cot, (0, 0)))
        back_sum = matmul(rows_cot, down, (1, 1))
        gate_act, up_act = (back_sum * rest).astype(BF16), (back_sum * silu_g).astype(BF16)
        grad_gate = self.unit_sums(matmul(gate_act, rows_in, (0, 0))).T
        grad_up = self.unit_sums(matmul(up_act, rows_in, (0, 0))).T
        output = self.scatter(matmul(hidden, down, (1, 0)), tokens.shape[0])
        partial = matmul(gate_act, gate, (1, 0)) + matmul(up_act, up, (1, 0))
        grad_tokens = self.scatter(partial, tokens.shape[0])
        return (output, grad_tokens, grad_gate, grad_up, grad_down)


def solution(mesh):
    square = mesh.shape["inp"] == 4 and mesh.shape["out"] == 2 and mesh.shape["wt"] == 4

    def on_device(tokens, *others):
        places = Square() if square and tokens.shape[0] == 2 else Plain()
        return places.layer(tokens, *others)

    rows_spec = P(None, ("inp", "wt"), "out")
    in_spec = P("out", ("wt", "inp"))
    down_spec = P(("wt", "inp"), "out")
    return jax.shard_map(
        on_device,
        mesh=mesh,
        in_specs=(rows_spec, in_spec, in_spec, down_spec, rows_spec),
        out_specs=(rows_spec, rows_spec, in_spec, in_spec, down_spec),
        check_vma=False,
    )
```

```python
import functools

import jax
import jax.numpy as jnp
from jax import lax
from jax.experimental import pallas as pl
from jax.experimental.pallas import tpu as pltpu
from jax.sharding import PartitionSpec as P

F32 = jnp.float32
BF16 = jnp.bfloat16
MIB = 1024 * 1024


def matmul(a, b, contract):
    return lax.dot_general(a, b, ((contract[:1], contract[1:]), ((), ())), preferred_element_type=F32)


def gated(gate_sum, up_sum):
    sigmoid_g = jax.nn.sigmoid(gate_sum)
    silu_g = gate_sum * sigmoid_g
    slope = sigmoid_g * (1.0 + gate_sum * (1.0 - sigmoid_g))
    return silu_g, silu_g * up_sum, up_sum * slope


def shape(*dims, dtype=BF16):
    return jax.ShapeDtypeStruct(dims, dtype)


def call(kernel, outs, flops, args, after=(), specs=None, scratch=(), limit=24):
    everything = [*args, *after]
    moved = sum(a.size * a.dtype.itemsize for a in args) + sum(o.size * o.dtype.itemsize for o in outs)
    specs = specs or [pl.BlockSpec(memory_space=pltpu.VMEM)] * len(args)

    def body(*refs):
        kernel(*refs[: len(args)], *refs[len(everything) :])

    return pl.pallas_call(
        body,
        out_shape=list(outs),
        in_specs=[*specs, *[pl.BlockSpec(memory_space=pl.ANY)] * len(after)],
        out_specs=[pl.BlockSpec(memory_space=pltpu.VMEM)] * len(outs),
        scratch_shapes=list(scratch),
        compiler_params=pltpu.CompilerParams(vmem_limit_bytes=limit * MIB),
        cost_estimate=pl.CostEstimate(flops=flops // SHARE, bytes_accessed=moved // SHARE, transcendentals=0),
    )(*everything)


SHARE = 1
ANY = pl.BlockSpec(memory_space=pl.ANY)
HBM = pl.BlockSpec(memory_space=pltpu.HBM)
VMEM = pl.BlockSpec(memory_space=pltpu.VMEM)
SMEM = pl.BlockSpec(memory_space=pltpu.SMEM)


def load(refs, into, sems):
    copies = [pltpu.make_async_copy(ref, into.at[at], sems.at[at]) for at, ref in enumerate(refs)]
    for copy in copies:
        copy.start()
    return copies


def hidden_kernel(width, rows, groups, *refs):
    row_refs, unit_refs = refs[:rows], refs[rows : rows + 2 * groups]
    hidden_ref, turned_ref, silu_ref, rest_ref, loaded, sems, units, unit_sems = refs[rows + 2 * groups :]
    step, half = row_refs[0].shape[0], unit_refs[0].shape[1]
    unit_copies = load(unit_refs, units, unit_sems)
    copies = load(row_refs, loaded, sems)
    for copy in unit_copies:
        copy.wait()
    for at, copy in enumerate(copies):
        copy.wait()
        row_ref = loaded.at[at]
        span = slice(at * step, (at + 1) * step)
        for group in range(groups):
            sums = matmul(row_ref[:, :half], units[group], (1, 1))
            sums = sums + matmul(row_ref[:, half:], units[groups + group], (1, 1))
            silu_g, hidden, rest = gated(sums[:, :width], sums[:, width:])
            cols = slice(group * width, (group + 1) * width)
            hidden_ref[span, cols] = hidden.astype(BF16)
            turned_ref[cols, span] = hidden.T.astype(BF16)
            silu_ref[span, cols] = silu_g.astype(BF16)
            rest_ref[span, cols] = rest.astype(BF16)


def grads_kernel(width, rows, *refs):
    row_refs, (silu_any, rest_any, down_ref, act_ref, turned_ref, loaded, sems) = refs[:rows], refs[rows : rows + 7]
    silu_ref, rest_ref, silu_sems, rest_sems = refs[rows + 7 :]
    step = row_refs[0].shape[0]
    spans = [pl.ds(at * step, step) for at in range(rows)]
    copies = load(row_refs, loaded, sems)
    silu_copies = [pltpu.make_async_copy(silu_any.at[s], silu_ref.at[s], silu_sems.at[i]) for i, s in enumerate(spans)]
    rest_copies = [pltpu.make_async_copy(rest_any.at[s], rest_ref.at[s], rest_sems.at[i]) for i, s in enumerate(spans)]
    for copy in silu_copies + rest_copies:
        copy.start()
    for at, copy in enumerate(copies):
        copy.wait()
        silu_copies[at].wait()
        rest_copies[at].wait()
        row_ref = loaded.at[at]
        span = slice(at * step, (at + 1) * step)
        for pair in range(down_ref.shape[0] // (2 * width)):
            units = slice(2 * pair * width, 2 * (pair + 1) * width)
            back = matmul(row_ref[...], down_ref[units], (1, 1))
            for part, factor in enumerate((rest_ref, silu_ref)):
                grads = back * factor[span, units].astype(F32)
                for side in range(2):
                    grad = grads[:, side * width : (side + 1) * width]
                    first = (4 * pair + 2 * side + part) * width
                    low = slice(first, first + width)
                    act_ref[span, low] = grad.astype(BF16)
                    turned_ref[low, span] = grad.T.astype(BF16)


def weight_kernel(first, tile, rows, *refs):
    row_refs, (turned_ref, away_ref, stay_ref, loaded, sems) = refs[:rows], refs[rows:]
    half, step = away_ref.shape[0], row_refs[0].shape[0]
    span = away_ref.shape[1] // 2
    parts = []
    for part in range(2):
        cols = pl.ds(first + part * span, span)
        parts.append(load([ref.at[:, cols] for ref in row_refs], loaded.at[part], sems.at[part]))
    for part, copies in enumerate(parts):
        for copy in copies:
            copy.wait()

        @pl.loop(0, span // tile)
        def _(index):
            here = pl.ds(pl.multiple_of(index * tile, tile), tile)
            cols = pl.ds(pl.multiple_of(part * span + index * tile, tile), tile)
            for out_ref, low in ((away_ref, 0), (stay_ref, half)):
                total = jnp.zeros((half, tile), F32)
                for at in range(rows):
                    left = turned_ref[low : low + half, at * step : (at + 1) * step]
                    total = total + matmul(left, loaded[part, at, :, here], (1, 0))
                out_ref[:, cols] = total.astype(BF16)


def block_kernel(first, places, sides, added, *refs):
    rights, many = len(sides), len(places)
    left_any, right_any, refs = refs[0], refs[1 : 1 + rights], refs[1 + rights :]
    adds, refs = refs[: many * added], refs[many * added :]
    outs, (left_ref, right_ref, sems) = refs[:many], refs[many:]
    depth, half = right_ref.shape[1:]
    copies = [pltpu.make_async_copy(left_any.at[pl.ds(first, left_ref.shape[0])], left_ref, sems.at[0])]
    for at, side in enumerate(sides):
        source = right_any[at].at[:, pl.ds(side * half, half)]
        copies.append(pltpu.make_async_copy(source, right_ref.at[at], sems.at[1 + at]))
    for copy in copies:
        copy.start()
    for copy in copies:
        copy.wait()
    for at, (row, right) in enumerate(places):
        total = matmul(left_ref[row : row + outs[at].shape[0]], right_ref[right], (1, 0))
        if added:
            total = total + adds[at][...].astype(F32)
        outs[at][...] = total.astype(BF16)


def halves_kernel(at_ref, gate_any, up_any, down_any, mine_ref, down_mine_ref, theirs_ref, gate_ref, up_ref, down_ref, sems):
    copies = [
        pltpu.make_async_copy(source, into, sems.at[at])
        for at, (source, into) in enumerate(((gate_any, gate_ref), (up_any, up_ref), (down_any, down_ref)))
    ]
    for copy in copies:
        copy.start()
    for copy in copies:
        copy.wait()
    width = down_mine_ref.shape[0]
    first = at_ref[0] == 0
    for part, ref in enumerate((gate_ref, up_ref)):
        span = slice(part * width, (part + 1) * width)
        low, high = ref[:, :width].astype(F32).T.astype(BF16), ref[:, width:].astype(F32).T.astype(BF16)
        mine_ref[span] = jnp.where(first, low, high)
        theirs_ref[span] = jnp.where(first, high, low)
    low, high = down_ref[:width], down_ref[width:]
    down_mine_ref[...] = jnp.where(first, low, high)
    theirs_ref[2 * width :] = jnp.where(first, high, low)


def take_kernel(in_ref, out_ref):
    out_ref[...] = in_ref[: out_ref.shape[0]]


def fetch_kernel(in_ref, out_ref, sem):
    copy = pltpu.make_async_copy(in_ref, out_ref, sem)
    copy.start()
    copy.wait()


def units_kernel(many, *refs):
    blocks, (out_ref, sems) = refs[: 2 * many], refs[2 * many :]
    step, span = blocks[0].shape
    copies = []
    for at, ref in enumerate(blocks):
        into = out_ref.at[pl.ds(at % many * step, step), pl.ds(at // many * span, span)]
        copies.append(pltpu.make_async_copy(ref, into, sems.at[at]))
    for copy in copies:
        copy.start()
    for copy in copies:
        copy.wait()


def sum_kernel(left_ref, right_ref, out_ref):
    out_ref[...] = (left_ref[...].astype(F32) + right_ref[...].astype(F32)).astype(BF16)


def add_kernel(stay_ref, came_ref, own_ref, far_ref):
    half = own_ref.shape[0]
    own_ref[...] = stay_ref[:half].astype(F32) + came_ref[:half].astype(F32)
    far_ref[...] = (stay_ref[half:].astype(F32) + came_ref[half:].astype(F32)).astype(BF16)


def beside_kernel(first, left_ref, right_ref, out_ref):
    rows, half = left_ref.shape
    out_ref[:, :half] = left_ref[...]
    out_ref[:, half:] = right_ref[first : first + rows]


def halves_beside_kernel(left_ref, top_ref, low_ref, out_ref):
    half, step = left_ref.shape[1], top_ref.shape[0]
    out_ref[:, :half] = left_ref[...]
    out_ref[:step, half:] = top_ref[...]
    out_ref[step:, half:] = low_ref[...]


def stack_kernel(*refs):
    out_ref, step = refs[-1], refs[0].shape[0]
    for at, ref in enumerate(refs[:-1]):
        out_ref[at * step : (at + 1) * step] = ref[...]


def finish_kernel(at_ref, mine_ref, theirs_ref, gate_ref, up_ref):
    width = mine_ref.shape[0] // 2
    for part, out_ref in enumerate((gate_ref, up_ref)):
        span = slice(part * width, (part + 1) * width)
        mine, theirs = mine_ref[span].astype(F32).T, theirs_ref[span].astype(F32).T
        first = at_ref[0] == 0
        out_ref[:, :width] = jnp.where(first, mine, theirs)
        out_ref[:, width:] = jnp.where(first, theirs, mine)


def beside(left, right, first=0, after=()):
    out = [shape(left.shape[0], 2 * left.shape[1])]
    return call(functools.partial(beside_kernel, first), out, 0, [left, right], after)[0]


def stacked(parts, after=()):
    return call(stack_kernel, [shape(len(parts) * parts[0].shape[0], parts[0].shape[1])], 0, parts, after)[0]


def taken(array, rows, after):
    return call(take_kernel, [shape(rows, array.shape[1])], 0, [array], after)[0]


def fetched(array, after):
    scratch = [pltpu.SemaphoreType.DMA]
    return call(fetch_kernel, [shape(*array.shape)], 0, [array], after, specs=[HBM], scratch=scratch)[0]


class Square:
    def core(self, array):
        return lax.ppermute(array, "inp", [(at, at ^ 1) for at in range(4)])

    def across(self, array):
        return lax.ppermute(array, "inp", [(at, at ^ 2) for at in range(4)])

    def other(self, array):
        return lax.ppermute(array, "out", [(0, 1), (1, 0)])

    def near(self, array):
        return lax.ppermute(array, "wt", [(at, at ^ 1) for at in range(4)])

    def far(self, array):
        return lax.ppermute(array, "wt", [(at, at ^ 2) for at in range(4)])

    def added(self, stay, came, after=()):
        half, cols = stay.shape[0] // 2, stay.shape[1]
        return call(add_kernel, [shape(half, cols, dtype=F32), shape(half, cols)], 0, [stay, came], after)

    def products(self, left, rights, places, adds=(), after=()):
        far = int(not adds)
        quarter, depth = left.shape[0] // 4, left.shape[1]
        half = rights[0][2]
        outs = [shape(quarter, half)] * len(places)
        use = sorted({other for _, other in places})
        chips = sorted({chip for chip, _ in places})
        first = 2 * far * quarter + chips[0] * quarter
        wanted = [((chip - chips[0]) * quarter, use.index(other)) for chip, other in places]
        args = [left] + [rights[other][0] for other in use] + [adds[place] for place in places if adds]
        blocks = call(
            functools.partial(block_kernel, first, wanted, [rights[other][1] for other in use], bool(adds)),
            outs,
            2 * len(places) * quarter * depth * half,
            args,
            after,
            specs=[ANY] * (1 + len(use)) + [VMEM] * (len(args) - 1 - len(use)),
            scratch=[
                pltpu.VMEM((len(chips) * quarter, depth), BF16),
                pltpu.VMEM((len(use), depth, half), BF16),
                pltpu.SemaphoreType.DMA((1 + len(use),)),
            ],
        )
        return dict(zip(places, blocks))

    def scatter_far(self, left, rights, after=()):
        first = self.products(left, rights, [(1, 1)], after=after)
        second = self.products(left, rights, [(0, 1), (1, 0), (0, 0)], after=list(first.values()))
        return first | second

    def near_first(self, left, rights, far, after):
        return self.products(left, rights, [(1, 1)], far, after)

    def near_rest(self, left, rights, far, after):
        return self.products(left, rights, [(0, 1), (1, 0), (0, 0)], far, after)

    def layer(self, tokens, gate_weight, up_weight, down_weight, cotangent):
        at_out = lax.axis_index("out").astype(jnp.int32).reshape(1)
        half, width = gate_weight.shape[0], gate_weight.shape[1] // 2
        mine, down_mine, theirs = call(
            halves_kernel,
            [shape(2 * width, half), shape(width, half), shape(3 * width, half)],
            0,
            [at_out, gate_weight, up_weight, down_weight],
            specs=[SMEM, HBM, HBM, HBM],
            scratch=[
                pltpu.VMEM(gate_weight.shape, BF16),
                pltpu.VMEM(up_weight.shape, BF16),
                pltpu.VMEM(down_weight.shape, BF16),
                pltpu.SemaphoreType.DMA((3,)),
            ],
        )
        came = self.other(theirs)
        step = tokens.shape[1]
        tok, cot = tokens.reshape(2 * step, half), cotangent.reshape(2 * step, half)

        tok_near = self.near(tok)
        far_mine, across_mine = self.far(mine), self.across(mine)
        tok_other = self.other(fetched(tok, [came, across_mine]))
        theirs = taken(came, 2 * width, [far_mine, across_mine])
        tok_corner = self.other(taken(tok_near, 2 * step, [far_mine]))
        far_theirs, across_theirs = self.far(theirs), self.across(theirs)
        corner_mine = self.across(far_mine)
        corner_theirs = self.across(far_theirs)
        unit_groups = [across_mine, corner_mine, mine, far_mine, across_theirs, corner_theirs, theirs, far_theirs]
        own_down = beside(down_mine, came, 2 * width, [far_theirs])
        far_down = self.far(own_down)
        cot_near = self.near(fetched(cot, [tok_near]))
        late_cot = fetched(cot, [tok_corner, corner_mine])
        cot_other = self.other(late_cot)
        tok_top = beside(tok, tok_other)
        tok_low = beside(tok_near, tok_corner, 0, [late_cot, across_theirs, corner_theirs, far_down])
        rows_in = [tok_top, tok_low, self.core(tok_top), self.core(tok_low)]
        down_groups = [self.across(own_down), self.across(far_down), own_down, far_down]

        count, units = 8 * step, 4 * width
        hidden, hidden_turned, silu, rest = call(
            functools.partial(hidden_kernel, width, 4, 4),
            [shape(count, units), shape(units, count), shape(count, units), shape(count, units)],
            8 * count * units * half,
            [*rows_in, *unit_groups],
            after=[*down_groups[:2], cot_near],
            specs=[HBM] * (4 + len(unit_groups)),
            scratch=[
                pltpu.VMEM((4, 2 * step, 2 * half), BF16),
                pltpu.SemaphoreType.DMA((4,)),
                pltpu.VMEM((len(unit_groups), 2 * width, half), BF16),
                pltpu.SemaphoreType.DMA((len(unit_groups),)),
            ],
            limit=30,
        )
        cot_corner = [self.other(cot_near[:step]), self.near(cot_other[step:])]
        cot_top = beside(cot, cot_other)
        outs = [shape(2 * step, 2 * half)]
        (cot_low,) = call(halves_beside_kernel, outs, 0, [cot_near, *cot_corner], [hidden])
        rows_cot = [cot_top, cot_low, self.core(cot_top), self.core(cot_low)]
        down = stacked(down_groups)
        down_sides = [(down, 0, half), (down, 1, half)]
        output_far = self.scatter_far(hidden, down_sides)
        down_terms = call(
            functools.partial(weight_kernel, 0, 256, 4),
            [shape(units // 2, 2 * half)] * 2,
            4 * count * units * half,
            [*rows_cot, hidden_turned],
            list(output_far.values()),
            specs=[HBM] * 4 + [VMEM],
            scratch=[pltpu.VMEM((2, 4, 2 * step, half), BF16), pltpu.SemaphoreType.DMA((2, 4))],
        )
        down_half, down_far = self.added(down_terms[1], self.across(down_terms[0]))
        down_came = self.far(down_far)
        act, act_turned = call(
            functools.partial(grads_kernel, width, 4),
            [shape(count, 2 * units), shape(2 * units, count)],
            4 * count * units * half,
            [*rows_cot, silu, rest, down],
            after=down_terms,
            specs=[HBM] * 6 + [VMEM],
            scratch=[
                pltpu.VMEM((4, 2 * step, 2 * half), BF16),
                pltpu.SemaphoreType.DMA((4,)),
                pltpu.VMEM((count, units), BF16),
                pltpu.VMEM((count, units), BF16),
                pltpu.SemaphoreType.DMA((4,)),
                pltpu.SemaphoreType.DMA((4,)),
            ],
            limit=30,
        )
        output_far = {place: self.core(block) for place, block in output_far.items()}
        sums = self.near_first(hidden, down_sides, output_far, [act])
        corner = sums[1, 1]
        by_other, by_near = self.other(corner[:step]), self.near(corner[step:])
        sums |= self.near_rest(hidden, down_sides, output_far, [corner])

        def unit_terms(side, after):
            return call(
                functools.partial(weight_kernel, side * half, 256, 4),
                [shape(units, half)] * 2,
                4 * count * units * half,
                [*rows_in, act_turned],
                after=after,
                specs=[HBM] * 4 + [VMEM],
                scratch=[pltpu.VMEM((2, 4, 2 * step, half // 2), BF16), pltpu.SemaphoreType.DMA((2, 4))],
            )

        other_terms = unit_terms(1, [sums[0, 0]])
        other_across = self.across(other_terms[0])
        (gate_up,) = call(
            functools.partial(units_kernel, 4),
            [shape(2 * units, 2 * half)],
            0,
            unit_groups,
            [other_terms[0], down_far],
            specs=[HBM] * 8,
            scratch=[pltpu.SemaphoreType.DMA((8,))],
        )
        unit_sides = [(gate_up, 0, half), (gate_up, 1, half)]
        grads_far = self.scatter_far(act, unit_sides, [by_other, by_near])
        zeros = jnp.zeros((step, half), F32)
        to_near = (sums[1, 0].astype(F32) + jnp.concatenate([by_other.astype(F32), zeros])).astype(BF16)
        to_other = (sums[0, 1].astype(F32) + jnp.concatenate([zeros, by_near.astype(F32)])).astype(BF16)
        by_near, by_other = self.near(to_near), self.other(to_other)
        total = sums[0, 0].astype(F32) + by_near.astype(F32) + by_other.astype(F32)
        output = total.astype(BF16).reshape(2, step, half)

        grads_far = {place: self.core(block) for place, block in grads_far.items()}
        sums = self.near_first(act, unit_sides, grads_far, [by_other, by_near, other_across, *grads_far.values()])
        by_other = self.other(sums[1, 1])
        own_terms = unit_terms(0, [sums[1, 1]])
        own_half, own_far = self.added(own_terms[1], self.across(own_terms[0]))
        own_came = self.far(own_far)
        down_sum = down_half + down_came.astype(F32)
        down_back = self.other(down_sum[:, half:].astype(BF16))
        other_half, other_far = self.added(other_terms[1], other_across, [down_came, own_terms[0]])
        other_came = self.far(other_far)
        other_sum = (other_half + other_came.astype(F32)).astype(BF16)
        sums |= self.near_rest(act, unit_sides, grads_far, [sums[1, 1], other_far, down_back])
        (to_near,) = call(sum_kernel, [shape(2 * step, half)], 0, [sums[1, 0], by_other])
        by_near, by_other = self.near(to_near), self.other(sums[0, 1])
        total = sums[0, 0].astype(F32) + by_near.astype(F32) + by_other.astype(F32)
        grad_tokens = total.astype(BF16).reshape(2, step, half)

        own_sum = (own_half + own_came.astype(F32)).astype(BF16)
        units_back = self.other(other_sum)
        mine, theirs = down_sum[:, :half], down_back.astype(F32)
        first = at_out[0] == 0
        grad_down = jnp.where(first, jnp.concatenate([mine, theirs]), jnp.concatenate([theirs, mine]))
        grad_gate, grad_up = call(
            finish_kernel,
            [shape(half, 2 * width, dtype=F32)] * 2,
            0,
            [at_out, own_sum, units_back],
            specs=[SMEM, VMEM, VMEM],
        )
        return (output, grad_tokens, grad_gate, grad_up, grad_down)


class Plain:
    def units(self, weight):
        own = lax.all_to_all(weight, "out", split_axis=0, concat_axis=1, tiled=True)
        return lax.all_gather(own, "wt", axis=0, tiled=True)

    def unit_sums(self, grad):
        own = lax.psum_scatter(grad.astype(BF16), "wt", scatter_dimension=0, tiled=True)
        return lax.all_to_all(own, "out", split_axis=1, concat_axis=0, tiled=True).astype(F32)

    def gather(self, array):
        array = lax.all_gather(lax.all_gather(array, "inp", axis=1, tiled=True), "out", axis=2, tiled=True)
        return array.reshape(-1, array.shape[2])

    def scatter(self, partial, batches):
        partial = partial.astype(BF16).reshape(batches, -1, partial.shape[1])
        partial = lax.psum_scatter(partial, "out", scatter_dimension=2, tiled=True)
        return lax.psum_scatter(partial, "inp", scatter_dimension=1, tiled=True)

    def layer(self, tokens, gate_weight, up_weight, down_weight, cotangent):
        gate, up, down = self.units(gate_weight.T), self.units(up_weight.T), self.units(down_weight)
        rows_in, rows_cot = self.gather(tokens), self.gather(cotangent)
        gate_sum = matmul(rows_in, gate, (1, 1))
        up_sum = matmul(rows_in, up, (1, 1))
        silu_g, hidden, rest = gated(gate_sum, up_sum)
        hidden = hidden.astype(BF16)
        grad_down = self.unit_sums(matmul(hidden, rows_cot, (0, 0)))
        back_sum = matmul(rows_cot, down, (1, 1))
        gate_act, up_act = (back_sum * rest).astype(BF16), (back_sum * silu_g).astype(BF16)
        grad_gate = self.unit_sums(matmul(gate_act, rows_in, (0, 0))).T
        grad_up = self.unit_sums(matmul(up_act, rows_in, (0, 0))).T
        output = self.scatter(matmul(hidden, down, (1, 0)), tokens.shape[0])
        partial = matmul(gate_act, gate, (1, 0)) + matmul(up_act, up, (1, 0))
        grad_tokens = self.scatter(partial, tokens.shape[0])
        return (output, grad_tokens, grad_gate, grad_up, grad_down)


def solution(mesh):
    square = mesh.shape["inp"] == 4 and mesh.shape["out"] == 2 and mesh.shape["wt"] == 4

    def on_device(tokens, *others):
        places = Square() if square and tokens.shape[0] == 2 else Plain()
        return places.layer(tokens, *others)

    rows_spec = P(None, ("inp", "wt"), "out")
    in_spec = P("out", ("wt", "inp"))
    down_spec = P(("wt", "inp"), "out")
    return jax.shard_map(
        on_device,
        mesh=mesh,
        in_specs=(rows_spec, in_spec, in_spec, down_spec, rows_spec),
        out_specs=(rows_spec, rows_spec, in_spec, in_spec, down_spec),
        check_vma=False,
    )
```

```python
import functools

import jax
import jax.numpy as jnp
from jax import lax
from jax.experimental import pallas as pl
from jax.experimental.pallas import tpu as pltpu
from jax.sharding import PartitionSpec as P

F32 = jnp.float32
BF16 = jnp.bfloat16
MIB = 1024 * 1024


def matmul(a, b, contract):
    return lax.dot_general(a, b, ((contract[:1], contract[1:]), ((), ())), preferred_element_type=F32)


def gated(gate_sum, up_sum):
    sigmoid_g = jax.nn.sigmoid(gate_sum)
    silu_g = gate_sum * sigmoid_g
    slope = sigmoid_g * (1.0 + gate_sum * (1.0 - sigmoid_g))
    return silu_g, silu_g * up_sum, up_sum * slope


def shape(*dims, dtype=BF16):
    return jax.ShapeDtypeStruct(dims, dtype)


def call(kernel, outs, flops, args, after=(), specs=None, scratch=(), limit=24):
    everything = [*args, *after]
    moved = sum(a.size * a.dtype.itemsize for a in args) + sum(o.size * o.dtype.itemsize for o in outs)
    specs = specs or [pl.BlockSpec(memory_space=pltpu.VMEM)] * len(args)

    def body(*refs):
        kernel(*refs[: len(args)], *refs[len(everything) :])

    return pl.pallas_call(
        body,
        out_shape=list(outs),
        in_specs=[*specs, *[pl.BlockSpec(memory_space=pl.ANY)] * len(after)],
        out_specs=[pl.BlockSpec(memory_space=pltpu.VMEM)] * len(outs),
        scratch_shapes=list(scratch),
        compiler_params=pltpu.CompilerParams(vmem_limit_bytes=limit * MIB),
        cost_estimate=pl.CostEstimate(flops=flops, bytes_accessed=moved, transcendentals=0),
    )(*everything)


SLOW = 5 * 10**10
ANY = pl.BlockSpec(memory_space=pl.ANY)
HBM = pl.BlockSpec(memory_space=pltpu.HBM)
VMEM = pl.BlockSpec(memory_space=pltpu.VMEM)
SMEM = pl.BlockSpec(memory_space=pltpu.SMEM)


def load(refs, into, sems):
    copies = [pltpu.make_async_copy(ref, into.at[at], sems.at[at]) for at, ref in enumerate(refs)]
    for copy in copies:
        copy.start()
    return copies


def hidden_kernel(width, rows, groups, *refs):
    row_refs, unit_refs = refs[:rows], refs[rows : rows + 2 * groups]
    hidden_ref, turned_ref, silu_ref, rest_ref, loaded, sems, units, unit_sems = refs[rows + 2 * groups :]
    step, half = row_refs[0].shape[0], unit_refs[0].shape[1]
    unit_copies = load(unit_refs, units, unit_sems)
    copies = load(row_refs, loaded, sems)
    for copy in unit_copies:
        copy.wait()
    for at, copy in enumerate(copies):
        copy.wait()
        row_ref = loaded.at[at]
        span = slice(at * step, (at + 1) * step)
        for group in range(groups):
            sums = matmul(row_ref[:, :half], units[group], (1, 1))
            sums = sums + matmul(row_ref[:, half:], units[groups + group], (1, 1))
            silu_g, hidden, rest = gated(sums[:, :width], sums[:, width:])
            cols = slice(group * width, (group + 1) * width)
            hidden_ref[span, cols] = hidden.astype(BF16)
            turned_ref[cols, span] = hidden.T.astype(BF16)
            silu_ref[span, cols] = silu_g.astype(BF16)
            rest_ref[span, cols] = rest.astype(BF16)


def grads_kernel(width, rows, *refs):
    row_refs, (silu_any, rest_any, down_ref, act_ref, turned_ref, loaded, sems) = refs[:rows], refs[rows : rows + 7]
    silu_ref, rest_ref, silu_sems, rest_sems = refs[rows + 7 :]
    step = row_refs[0].shape[0]
    spans = [pl.ds(at * step, step) for at in range(rows)]
    copies = load(row_refs, loaded, sems)
    silu_copies = [pltpu.make_async_copy(silu_any.at[s], silu_ref.at[s], silu_sems.at[i]) for i, s in enumerate(spans)]
    rest_copies = [pltpu.make_async_copy(rest_any.at[s], rest_ref.at[s], rest_sems.at[i]) for i, s in enumerate(spans)]
    for copy in silu_copies + rest_copies:
        copy.start()
    for at, copy in enumerate(copies):
        copy.wait()
        silu_copies[at].wait()
        rest_copies[at].wait()
        row_ref = loaded.at[at]
        span = slice(at * step, (at + 1) * step)
        for pair in range(down_ref.shape[0] // (2 * width)):
            units = slice(2 * pair * width, 2 * (pair + 1) * width)
            back = matmul(row_ref[...], down_ref[units], (1, 1))
            for part, factor in enumerate((rest_ref, silu_ref)):
                grads = back * factor[span, units].astype(F32)
                for side in range(2):
                    grad = grads[:, side * width : (side + 1) * width]
                    first = (4 * pair + 2 * side + part) * width
                    low = slice(first, first + width)
                    act_ref[span, low] = grad.astype(BF16)
                    turned_ref[low, span] = grad.T.astype(BF16)


def weight_kernel(first, tile, rows, *refs):
    row_refs, (turned_ref, away_ref, stay_ref, loaded, sems) = refs[:rows], refs[rows:]
    half, step = away_ref.shape[0], row_refs[0].shape[0]
    span = away_ref.shape[1] // 2
    parts = []
    for part in range(2):
        cols = pl.ds(first + part * span, span)
        parts.append(load([ref.at[:, cols] for ref in row_refs], loaded.at[part], sems.at[part]))
    for part, copies in enumerate(parts):
        for copy in copies:
            copy.wait()

        @pl.loop(0, span // tile)
        def _(index):
            here = pl.ds(pl.multiple_of(index * tile, tile), tile)
            cols = pl.ds(pl.multiple_of(part * span + index * tile, tile), tile)
            for out_ref, low in ((away_ref, 0), (stay_ref, half)):
                total = jnp.zeros((half, tile), F32)
                for at in range(rows):
                    left = turned_ref[low : low + half, at * step : (at + 1) * step]
                    total = total + matmul(left, loaded[part, at, :, here], (1, 0))
                out_ref[:, cols] = total.astype(BF16)


def block_kernel(first, places, sides, added, *refs):
    rights, many = len(sides), len(places)
    left_any, right_any, refs = refs[0], refs[1 : 1 + rights], refs[1 + rights :]
    adds, refs = refs[: many * added], refs[many * added :]
    outs, (left_ref, right_ref, sems) = refs[:many], refs[many:]
    depth, half = right_ref.shape[1:]
    copies = [pltpu.make_async_copy(left_any.at[pl.ds(first, left_ref.shape[0])], left_ref, sems.at[0])]
    for at, side in enumerate(sides):
        source = right_any[at].at[:, pl.ds(side * half, half)]
        copies.append(pltpu.make_async_copy(source, right_ref.at[at], sems.at[1 + at]))
    for copy in copies:
        copy.start()
    for copy in copies:
        copy.wait()
    for at, (row, right) in enumerate(places):
        total = matmul(left_ref[row : row + outs[at].shape[0]], right_ref[right], (1, 0))
        if added:
            total = total + adds[at][...].astype(F32)
        outs[at][...] = total.astype(BF16)


def halves_kernel(at_ref, gate_any, up_any, down_any, mine_ref, down_mine_ref, theirs_ref, gate_ref, up_ref, down_ref, sems):
    copies = [
        pltpu.make_async_copy(source, into, sems.at[at])
        for at, (source, into) in enumerate(((gate_any, gate_ref), (up_any, up_ref), (down_any, down_ref)))
    ]
    for copy in copies:
        copy.start()
    for copy in copies:
        copy.wait()
    width = down_mine_ref.shape[0]
    first = at_ref[0] == 0
    for part, ref in enumerate((gate_ref, up_ref)):
        span = slice(part * width, (part + 1) * width)
        low, high = ref[:, :width].astype(F32).T.astype(BF16), ref[:, width:].astype(F32).T.astype(BF16)
        mine_ref[span] = jnp.where(first, low, high)
        theirs_ref[span] = jnp.where(first, high, low)
    low, high = down_ref[:width], down_ref[width:]
    down_mine_ref[...] = jnp.where(first, low, high)
    theirs_ref[2 * width :] = jnp.where(first, high, low)


def take_kernel(in_ref, out_ref):
    out_ref[...] = in_ref[: out_ref.shape[0]]


def fetch_kernel(in_ref, out_ref, sem):
    copy = pltpu.make_async_copy(in_ref, out_ref, sem)
    copy.start()
    copy.wait()


def units_kernel(many, *refs):
    blocks, (out_ref, sems) = refs[: 2 * many], refs[2 * many :]
    step, span = blocks[0].shape
    copies = []
    for at, ref in enumerate(blocks):
        into = out_ref.at[pl.ds(at % many * step, step), pl.ds(at // many * span, span)]
        copies.append(pltpu.make_async_copy(ref, into, sems.at[at]))
    for copy in copies:
        copy.start()
    for copy in copies:
        copy.wait()


def sum_kernel(left_ref, right_ref, out_ref):
    out_ref[...] = (left_ref[...].astype(F32) + right_ref[...].astype(F32)).astype(BF16)


def add_kernel(stay_ref, came_ref, own_ref, far_ref):
    half = own_ref.shape[0]
    own_ref[...] = stay_ref[:half].astype(F32) + came_ref[:half].astype(F32)
    far_ref[...] = (stay_ref[half:].astype(F32) + came_ref[half:].astype(F32)).astype(BF16)


def beside_kernel(first, left_ref, right_ref, out_ref):
    rows, half = left_ref.shape
    out_ref[:, :half] = left_ref[...]
    out_ref[:, half:] = right_ref[first : first + rows]


def halves_beside_kernel(left_ref, top_ref, low_ref, out_ref):
    half, step = left_ref.shape[1], top_ref.shape[0]
    out_ref[:, :half] = left_ref[...]
    out_ref[:step, half:] = top_ref[...]
    out_ref[step:, half:] = low_ref[...]


def stack_kernel(*refs):
    out_ref, step = refs[-1], refs[0].shape[0]
    for at, ref in enumerate(refs[:-1]):
        out_ref[at * step : (at + 1) * step] = ref[...]


def finish_kernel(at_ref, mine_ref, theirs_ref, gate_ref, up_ref):
    width = mine_ref.shape[0] // 2
    for part, out_ref in enumerate((gate_ref, up_ref)):
        span = slice(part * width, (part + 1) * width)
        mine, theirs = mine_ref[span].astype(F32).T, theirs_ref[span].astype(F32).T
        first = at_ref[0] == 0
        out_ref[:, :width] = jnp.where(first, mine, theirs)
        out_ref[:, width:] = jnp.where(first, theirs, mine)


def beside(left, right, first=0, after=()):
    out = [shape(left.shape[0], 2 * left.shape[1])]
    return call(functools.partial(beside_kernel, first), out, 0, [left, right], after)[0]


def stacked(parts, after=()):
    return call(stack_kernel, [shape(len(parts) * parts[0].shape[0], parts[0].shape[1])], 0, parts, after)[0]


def taken(array, rows, after, flops=0):
    return call(take_kernel, [shape(rows, array.shape[1])], flops, [array], after)[0]


def fetched(array, after):
    scratch = [pltpu.SemaphoreType.DMA]
    return call(fetch_kernel, [shape(*array.shape)], 0, [array], after, specs=[HBM], scratch=scratch)[0]


class Square:
    def core(self, array):
        return lax.ppermute(array, "inp", [(at, at ^ 1) for at in range(4)])

    def across(self, array):
        return lax.ppermute(array, "inp", [(at, at ^ 2) for at in range(4)])

    def other(self, array):
        return lax.ppermute(array, "out", [(0, 1), (1, 0)])

    def near(self, array):
        return lax.ppermute(array, "wt", [(at, at ^ 1) for at in range(4)])

    def far(self, array):
        return lax.ppermute(array, "wt", [(at, at ^ 2) for at in range(4)])

    def added(self, stay, came, after=()):
        half, cols = stay.shape[0] // 2, stay.shape[1]
        return call(add_kernel, [shape(half, cols, dtype=F32), shape(half, cols)], 0, [stay, came], after)

    def products(self, left, rights, places, adds=(), after=()):
        far = int(not adds)
        quarter, depth = left.shape[0] // 4, left.shape[1]
        half = rights[0][2]
        outs = [shape(quarter, half)] * len(places)
        use = sorted({other for _, other in places})
        chips = sorted({chip for chip, _ in places})
        first = 2 * far * quarter + chips[0] * quarter
        wanted = [((chip - chips[0]) * quarter, use.index(other)) for chip, other in places]
        args = [left] + [rights[other][0] for other in use] + [adds[place] for place in places if adds]
        blocks = call(
            functools.partial(block_kernel, first, wanted, [rights[other][1] for other in use], bool(adds)),
            outs,
            2 * len(places) * quarter * depth * half,
            args,
            after,
            specs=[ANY] * (1 + len(use)) + [VMEM] * (len(args) - 1 - len(use)),
            scratch=[
                pltpu.VMEM((len(chips) * quarter, depth), BF16),
                pltpu.VMEM((len(use), depth, half), BF16),
                pltpu.SemaphoreType.DMA((1 + len(use),)),
            ],
        )
        return dict(zip(places, blocks))

    def far_first(self, left, rights, after):
        return self.products(left, rights, [(1, 1)], after=after)

    def far_rest(self, left, rights, after):
        return self.products(left, rights, [(0, 1), (1, 0), (0, 0)], after=after)

    def near_first(self, left, rights, far, after):
        return self.products(left, rights, [(1, 1)], far, after)

    def near_rest(self, left, rights, far, after):
        return self.products(left, rights, [(0, 1), (1, 0), (0, 0)], far, after)

    def layer(self, tokens, gate_weight, up_weight, down_weight, cotangent):
        at_out = lax.axis_index("out").astype(jnp.int32).reshape(1)
        half, width = gate_weight.shape[0], gate_weight.shape[1] // 2
        mine, down_mine, theirs = call(
            halves_kernel,
            [shape(2 * width, half), shape(width, half), shape(3 * width, half)],
            0,
            [at_out, gate_weight, up_weight, down_weight],
            specs=[SMEM, HBM, HBM, HBM],
            scratch=[
                pltpu.VMEM(gate_weight.shape, BF16),
                pltpu.VMEM(up_weight.shape, BF16),
                pltpu.VMEM(down_weight.shape, BF16),
                pltpu.SemaphoreType.DMA((3,)),
            ],
        )
        came = self.other(theirs)
        step = tokens.shape[1]
        tok, cot = tokens.reshape(2 * step, half), cotangent.reshape(2 * step, half)

        tok_near = self.near(tok)
        far_mine, across_mine = self.far(mine), self.across(mine)
        late_tok = fetched(tok, [came, across_mine])
        tok_other = self.other(late_tok)
        theirs = taken(came, 2 * width, [far_mine, across_mine])
        tok_corner = self.other(taken(tok_near, 2 * step, [far_mine, tok_other]))
        far_theirs, across_theirs = self.far(theirs), self.across(theirs)
        corner_mine = self.across(far_mine)
        corner_theirs = self.across(far_theirs)
        unit_groups = [across_mine, corner_mine, mine, far_mine, across_theirs, corner_theirs, theirs, far_theirs]
        own_down = beside(down_mine, came, 2 * width, [far_theirs])
        far_down = self.far(own_down)
        cot_near = self.near(fetched(cot, [tok_near]))
        late_cot = fetched(cot, [tok_corner, corner_mine])
        cot_other = self.other(late_cot)
        tok_top = beside(tok, tok_other)
        tok_low = beside(tok_near, tok_corner, 0, [late_cot, across_theirs, corner_theirs])
        rows_in = [tok_top, tok_low, self.core(tok_top), self.core(tok_low)]
        cot_corner = [self.other(cot_near[:step]), self.near(cot_other[step:])]
        down_groups = [self.across(own_down), taken(self.across(far_down), width, [], SLOW), own_down, far_down]

        count, units = 8 * step, 4 * width
        hidden, hidden_turned, silu, rest = call(
            functools.partial(hidden_kernel, width, 4, 4),
            [shape(count, units), shape(units, count), shape(count, units), shape(count, units)],
            8 * count * units * half,
            [*rows_in, *unit_groups],
            after=[*down_groups[:2], *cot_corner],
            specs=[HBM] * (4 + len(unit_groups)),
            scratch=[
                pltpu.VMEM((4, 2 * step, 2 * half), BF16),
                pltpu.SemaphoreType.DMA((4,)),
                pltpu.VMEM((len(unit_groups), 2 * width, half), BF16),
                pltpu.SemaphoreType.DMA((len(unit_groups),)),
            ],
            limit=30,
        )
        cot_top = beside(cot, cot_other)
        outs = [shape(2 * step, 2 * half)]
        (cot_low,) = call(halves_beside_kernel, outs, 0, [cot_near, *cot_corner], [hidden])
        rows_cot = [cot_top, cot_low, self.core(cot_top), self.core(cot_low)]
        down = stacked(down_groups)
        down_sides = [(down, 0, half), (down, 1, half)]
        output_far = self.far_first(hidden, down_sides, [])
        output_far |= self.far_rest(hidden, down_sides, [output_far[1, 1]])
        down_terms = call(
            functools.partial(weight_kernel, 0, 256, 4),
            [shape(units // 2, 2 * half)] * 2,
            4 * count * units * half,
            [*rows_cot, hidden_turned],
            list(output_far.values()),
            specs=[HBM] * 4 + [VMEM],
            scratch=[pltpu.VMEM((2, 4, 2 * step, half), BF16), pltpu.SemaphoreType.DMA((2, 4))],
        )
        down_half, down_far = self.added(down_terms[1], self.across(down_terms[0]))
        down_came = self.far(down_far)
        act, act_turned = call(
            functools.partial(grads_kernel, width, 4),
            [shape(count, 2 * units), shape(2 * units, count)],
            4 * count * units * half,
            [*rows_cot, silu, rest, down],
            after=down_terms,
            specs=[HBM] * 6 + [VMEM],
            scratch=[
                pltpu.VMEM((4, 2 * step, 2 * half), BF16),
                pltpu.SemaphoreType.DMA((4,)),
                pltpu.VMEM((count, units), BF16),
                pltpu.VMEM((count, units), BF16),
                pltpu.SemaphoreType.DMA((4,)),
                pltpu.SemaphoreType.DMA((4,)),
            ],
            limit=30,
        )
        output_far = {place: self.core(block) for place, block in output_far.items()}
        sums = self.near_first(hidden, down_sides, output_far, [act])
        corner = sums[1, 1]
        by_other, by_near = self.other(corner[:step]), self.near(corner[step:])
        sums |= self.near_rest(hidden, down_sides, output_far, [corner])

        def unit_terms(side, after):
            return call(
                functools.partial(weight_kernel, side * half, 256, 4),
                [shape(units, half)] * 2,
                4 * count * units * half,
                [*rows_in, act_turned],
                after=after,
                specs=[HBM] * 4 + [VMEM],
                scratch=[pltpu.VMEM((2, 4, 2 * step, half // 2), BF16), pltpu.SemaphoreType.DMA((2, 4))],
            )

        other_terms = unit_terms(1, [sums[0, 0]])
        other_across = self.across(other_terms[0])
        (gate_up,) = call(
            functools.partial(units_kernel, 4),
            [shape(2 * units, 2 * half)],
            0,
            unit_groups,
            [other_terms[0], down_far],
            specs=[HBM] * 8,
            scratch=[pltpu.SemaphoreType.DMA((8,))],
        )
        unit_sides = [(gate_up, 0, half), (gate_up, 1, half)]
        grads_far = self.far_first(act, unit_sides, [by_other, by_near])
        own_terms = unit_terms(0, [grads_far[1, 1]])
        grads_far |= self.far_rest(act, unit_sides, [own_terms[0], down_came])
        zeros = jnp.zeros((step, half), F32)
        to_near = (sums[1, 0].astype(F32) + jnp.concatenate([by_other.astype(F32), zeros])).astype(BF16)
        to_other = (sums[0, 1].astype(F32) + jnp.concatenate([zeros, by_near.astype(F32)])).astype(BF16)
        by_near, by_other = self.near(to_near), self.other(to_other)
        total = sums[0, 0].astype(F32) + by_near.astype(F32) + by_other.astype(F32)
        output = total.astype(BF16).reshape(2, step, half)

        grads_far = {place: self.core(block) for place, block in grads_far.items()}
        sums = self.near_first(act, unit_sides, grads_far, [by_other, by_near, other_across])
        by_other = self.other(sums[1, 1])
        own_across = self.across(own_terms[0])
        own_half, own_far = self.added(own_terms[1], own_across)
        own_came = self.far(own_far)
        down_sum = down_half + down_came.astype(F32)
        down_back = self.other(down_sum[:, half:].astype(BF16))
        other_half, other_far = self.added(other_terms[1], other_across)
        other_came = self.far(other_far)
        other_late = taken(other_came, 2 * width, [], SLOW // 12)
        other_sum = (other_half + other_came.astype(F32)).astype(BF16)
        sums |= self.near_rest(act, unit_sides, grads_far, [sums[1, 1], own_across])
        (to_near,) = call(sum_kernel, [shape(2 * step, half)], 0, [sums[1, 0], by_other], [other_late, down_back])
        by_near, by_other = self.near(to_near), self.other(sums[0, 1])
        total = sums[0, 0].astype(F32) + by_near.astype(F32) + by_other.astype(F32)
        grad_tokens = total.astype(BF16).reshape(2, step, half)

        own_sum = (own_half + own_came.astype(F32)).astype(BF16)
        units_back = self.other(other_sum)
        mine, theirs = down_sum[:, :half], down_back.astype(F32)
        first = at_out[0] == 0
        grad_down = jnp.where(first, jnp.concatenate([mine, theirs]), jnp.concatenate([theirs, mine]))
        grad_gate, grad_up = call(
            finish_kernel,
            [shape(half, 2 * width, dtype=F32)] * 2,
            0,
            [at_out, own_sum, units_back],
            specs=[SMEM, VMEM, VMEM],
        )
        return (output, grad_tokens, grad_gate, grad_up, grad_down)


class Plain:
    def units(self, weight):
        own = lax.all_to_all(weight, "out", split_axis=0, concat_axis=1, tiled=True)
        return lax.all_gather(own, "wt", axis=0, tiled=True)

    def unit_sums(self, grad):
        own = lax.psum_scatter(grad.astype(BF16), "wt", scatter_dimension=0, tiled=True)
        return lax.all_to_all(own, "out", split_axis=1, concat_axis=0, tiled=True).astype(F32)

    def gather(self, array):
        array = lax.all_gather(lax.all_gather(array, "inp", axis=1, tiled=True), "out", axis=2, tiled=True)
        return array.reshape(-1, array.shape[2])

    def scatter(self, partial, batches):
        partial = partial.astype(BF16).reshape(batches, -1, partial.shape[1])
        partial = lax.psum_scatter(partial, "out", scatter_dimension=2, tiled=True)
        return lax.psum_scatter(partial, "inp", scatter_dimension=1, tiled=True)

    def layer(self, tokens, gate_weight, up_weight, down_weight, cotangent):
        gate, up, down = self.units(gate_weight.T), self.units(up_weight.T), self.units(down_weight)
        rows_in, rows_cot = self.gather(tokens), self.gather(cotangent)
        gate_sum = matmul(rows_in, gate, (1, 1))
        up_sum = matmul(rows_in, up, (1, 1))
        silu_g, hidden, rest = gated(gate_sum, up_sum)
        hidden = hidden.astype(BF16)
        grad_down = self.unit_sums(matmul(hidden, rows_cot, (0, 0)))
        back_sum = matmul(rows_cot, down, (1, 1))
        gate_act, up_act = (back_sum * rest).astype(BF16), (back_sum * silu_g).astype(BF16)
        grad_gate = self.unit_sums(matmul(gate_act, rows_in, (0, 0))).T
        grad_up = self.unit_sums(matmul(up_act, rows_in, (0, 0))).T
        output = self.scatter(matmul(hidden, down, (1, 0)), tokens.shape[0])
        partial = matmul(gate_act, gate, (1, 0)) + matmul(up_act, up, (1, 0))
        grad_tokens = self.scatter(partial, tokens.shape[0])
        return (output, grad_tokens, grad_gate, grad_up, grad_down)


def solution(mesh):
    square = mesh.shape["inp"] == 4 and mesh.shape["out"] == 2 and mesh.shape["wt"] == 4

    def on_device(tokens, *others):
        places = Square() if square and tokens.shape[0] == 2 else Plain()
        return places.layer(tokens, *others)

    rows_spec = P(None, ("inp", "wt"), "out")
    in_spec = P("out", ("wt", "inp"))
    down_spec = P(("wt", "inp"), "out")
    return jax.shard_map(
        on_device,
        mesh=mesh,
        in_specs=(rows_spec, in_spec, in_spec, down_spec, rows_spec),
        out_specs=(rows_spec, rows_spec, in_spec, in_spec, down_spec),
        check_vma=False,
    )
```

```python
import functools

import jax
import jax.numpy as jnp
from jax import lax
from jax.experimental import pallas as pl
from jax.experimental.pallas import tpu as pltpu
from jax.sharding import PartitionSpec as P

F32 = jnp.float32
BF16 = jnp.bfloat16
MIB = 1024 * 1024


def matmul(a, b, contract):
    return lax.dot_general(a, b, ((contract[:1], contract[1:]), ((), ())), preferred_element_type=F32)


def gated(gate_sum, up_sum):
    sigmoid_g = jax.nn.sigmoid(gate_sum)
    silu_g = gate_sum * sigmoid_g
    slope = sigmoid_g * (1.0 + gate_sum * (1.0 - sigmoid_g))
    return silu_g, silu_g * up_sum, up_sum * slope


def shape(*dims, dtype=BF16):
    return jax.ShapeDtypeStruct(dims, dtype)


def call(kernel, outs, flops, args, after=(), specs=None, scratch=(), limit=24):
    everything = [*args, *after]
    moved = sum(a.size * a.dtype.itemsize for a in args) + sum(o.size * o.dtype.itemsize for o in outs)
    specs = specs or [pl.BlockSpec(memory_space=pltpu.VMEM)] * len(args)

    def body(*refs):
        kernel(*refs[: len(args)], *refs[len(everything) :])

    return pl.pallas_call(
        body,
        out_shape=list(outs),
        in_specs=[*specs, *[pl.BlockSpec(memory_space=pl.ANY)] * len(after)],
        out_specs=[pl.BlockSpec(memory_space=pltpu.VMEM)] * len(outs),
        scratch_shapes=list(scratch),
        compiler_params=pltpu.CompilerParams(vmem_limit_bytes=limit * MIB),
        cost_estimate=pl.CostEstimate(flops=flops, bytes_accessed=moved, transcendentals=0),
    )(*everything)


SLOW = 5 * 10**10
ANY = pl.BlockSpec(memory_space=pl.ANY)
HBM = pl.BlockSpec(memory_space=pltpu.HBM)
VMEM = pl.BlockSpec(memory_space=pltpu.VMEM)
SMEM = pl.BlockSpec(memory_space=pltpu.SMEM)


def load(refs, into, sems):
    copies = [pltpu.make_async_copy(ref, into.at[at], sems.at[at]) for at, ref in enumerate(refs)]
    for copy in copies:
        copy.start()
    return copies


def hidden_kernel(width, rows, groups, *refs):
    row_refs, unit_refs = refs[:rows], refs[rows : rows + 2 * groups]
    hidden_ref, turned_ref, silu_ref, rest_ref, loaded, sems, units, unit_sems = refs[rows + 2 * groups :]
    step, half = row_refs[0].shape[0], unit_refs[0].shape[1]
    unit_copies = load(unit_refs, units, unit_sems)
    copies = load(row_refs, loaded, sems)
    for copy in unit_copies:
        copy.wait()
    for at, copy in enumerate(copies):
        copy.wait()
        row_ref = loaded.at[at]
        span = slice(at * step, (at + 1) * step)
        for group in range(groups):
            sums = matmul(row_ref[:, :half], units[group], (1, 1))
            sums = sums + matmul(row_ref[:, half:], units[groups + group], (1, 1))
            silu_g, hidden, rest = gated(sums[:, :width], sums[:, width:])
            cols = slice(group * width, (group + 1) * width)
            hidden_ref[span, cols] = hidden.astype(BF16)
            turned_ref[cols, span] = hidden.T.astype(BF16)
            silu_ref[span, cols] = silu_g.astype(BF16)
            rest_ref[span, cols] = rest.astype(BF16)


def grads_kernel(width, rows, *refs):
    row_refs, (silu_any, rest_any, down_ref, act_ref, turned_ref, loaded, sems) = refs[:rows], refs[rows : rows + 7]
    silu_ref, rest_ref, silu_sems, rest_sems = refs[rows + 7 :]
    step = row_refs[0].shape[0]
    spans = [pl.ds(at * step, step) for at in range(rows)]
    copies = load(row_refs, loaded, sems)
    silu_copies = [pltpu.make_async_copy(silu_any.at[s], silu_ref.at[s], silu_sems.at[i]) for i, s in enumerate(spans)]
    rest_copies = [pltpu.make_async_copy(rest_any.at[s], rest_ref.at[s], rest_sems.at[i]) for i, s in enumerate(spans)]
    for copy in silu_copies + rest_copies:
        copy.start()
    for at, copy in enumerate(copies):
        copy.wait()
        silu_copies[at].wait()
        rest_copies[at].wait()
        row_ref = loaded.at[at]
        span = slice(at * step, (at + 1) * step)
        for pair in range(down_ref.shape[0] // (2 * width)):
            units = slice(2 * pair * width, 2 * (pair + 1) * width)
            back = matmul(row_ref[...], down_ref[units], (1, 1))
            for part, factor in enumerate((rest_ref, silu_ref)):
                grads = back * factor[span, units].astype(F32)
                for side in range(2):
                    grad = grads[:, side * width : (side + 1) * width]
                    first = (4 * pair + 2 * side + part) * width
                    low = slice(first, first + width)
                    act_ref[span, low] = grad.astype(BF16)
                    turned_ref[low, span] = grad.T.astype(BF16)


def weight_kernel(first, tile, rows, *refs):
    row_refs, (turned_ref, away_ref, stay_ref, loaded, sems) = refs[:rows], refs[rows:]
    half, step = away_ref.shape[0], row_refs[0].shape[0]
    span = away_ref.shape[1] // 2
    parts = []
    for part in range(2):
        cols = pl.ds(first + part * span, span)
        parts.append(load([ref.at[:, cols] for ref in row_refs], loaded.at[part], sems.at[part]))
    for part, copies in enumerate(parts):
        for copy in copies:
            copy.wait()

        @pl.loop(0, span // tile)
        def _(index):
            here = pl.ds(pl.multiple_of(index * tile, tile), tile)
            cols = pl.ds(pl.multiple_of(part * span + index * tile, tile), tile)
            for out_ref, low in ((away_ref, 0), (stay_ref, half)):
                total = jnp.zeros((half, tile), F32)
                for at in range(rows):
                    left = turned_ref[low : low + half, at * step : (at + 1) * step]
                    total = total + matmul(left, loaded[part, at, :, here], (1, 0))
                out_ref[:, cols] = total.astype(BF16)


def block_kernel(first, places, sides, added, *refs):
    rights, many = len(sides), len(places)
    left_any, right_any, refs = refs[0], refs[1 : 1 + rights], refs[1 + rights :]
    adds, refs = refs[: many * added], refs[many * added :]
    outs, (left_ref, right_ref, sems) = refs[:many], refs[many:]
    depth, half = right_ref.shape[1:]
    copies = [pltpu.make_async_copy(left_any.at[pl.ds(first, left_ref.shape[0])], left_ref, sems.at[0])]
    for at, side in enumerate(sides):
        source = right_any[at].at[:, pl.ds(side * half, half)]
        copies.append(pltpu.make_async_copy(source, right_ref.at[at], sems.at[1 + at]))
    for copy in copies:
        copy.start()
    for copy in copies:
        copy.wait()
    for at, (row, right) in enumerate(places):
        total = matmul(left_ref[row : row + outs[at].shape[0]], right_ref[right], (1, 0))
        if added:
            total = total + adds[at][...].astype(F32)
        outs[at][...] = total.astype(BF16)


def halves_kernel(at_ref, gate_any, up_any, down_any, mine_ref, down_mine_ref, theirs_ref, gate_ref, up_ref, down_ref, sems):
    copies = [
        pltpu.make_async_copy(source, into, sems.at[at])
        for at, (source, into) in enumerate(((gate_any, gate_ref), (up_any, up_ref), (down_any, down_ref)))
    ]
    for copy in copies:
        copy.start()
    for copy in copies:
        copy.wait()
    width = down_mine_ref.shape[0]
    first = at_ref[0] == 0
    for part, ref in enumerate((gate_ref, up_ref)):
        span = slice(part * width, (part + 1) * width)
        low, high = ref[:, :width].astype(F32).T.astype(BF16), ref[:, width:].astype(F32).T.astype(BF16)
        mine_ref[span] = jnp.where(first, low, high)
        theirs_ref[span] = jnp.where(first, high, low)
    low, high = down_ref[:width], down_ref[width:]
    down_mine_ref[...] = jnp.where(first, low, high)
    theirs_ref[2 * width :] = jnp.where(first, high, low)


def take_kernel(in_ref, out_ref):
    out_ref[...] = in_ref[: out_ref.shape[0]]


def fetch_kernel(in_ref, out_ref, sem):
    copy = pltpu.make_async_copy(in_ref, out_ref, sem)
    copy.start()
    copy.wait()


def units_kernel(many, *refs):
    blocks, (out_ref, sems) = refs[: 2 * many], refs[2 * many :]
    step, span = blocks[0].shape
    copies = []
    for at, ref in enumerate(blocks):
        into = out_ref.at[pl.ds(at % many * step, step), pl.ds(at // many * span, span)]
        copies.append(pltpu.make_async_copy(ref, into, sems.at[at]))
    for copy in copies:
        copy.start()
    for copy in copies:
        copy.wait()


def sum_kernel(left_ref, right_ref, out_ref):
    out_ref[...] = (left_ref[...].astype(F32) + right_ref[...].astype(F32)).astype(BF16)


def add_kernel(stay_ref, came_ref, own_ref, far_ref):
    half = own_ref.shape[0]
    own_ref[...] = stay_ref[:half].astype(F32) + came_ref[:half].astype(F32)
    far_ref[...] = (stay_ref[half:].astype(F32) + came_ref[half:].astype(F32)).astype(BF16)


def beside_kernel(first, left_ref, right_ref, out_ref):
    rows, half = left_ref.shape
    out_ref[:, :half] = left_ref[...]
    out_ref[:, half:] = right_ref[first : first + rows]


def halves_beside_kernel(left_ref, top_ref, low_ref, out_ref):
    half, step = left_ref.shape[1], top_ref.shape[0]
    out_ref[:, :half] = left_ref[...]
    out_ref[:step, half:] = top_ref[...]
    out_ref[step:, half:] = low_ref[...]


def stack_kernel(*refs):
    out_ref, step = refs[-1], refs[0].shape[0]
    for at, ref in enumerate(refs[:-1]):
        out_ref[at * step : (at + 1) * step] = ref[...]


def finish_kernel(at_ref, mine_ref, theirs_ref, gate_ref, up_ref):
    width = mine_ref.shape[0] // 2
    for part, out_ref in enumerate((gate_ref, up_ref)):
        span = slice(part * width, (part + 1) * width)
        mine, theirs = mine_ref[span].astype(F32).T, theirs_ref[span].astype(F32).T
        first = at_ref[0] == 0
        out_ref[:, :width] = jnp.where(first, mine, theirs)
        out_ref[:, width:] = jnp.where(first, theirs, mine)


def beside(left, right, first=0, after=()):
    out = [shape(left.shape[0], 2 * left.shape[1])]
    return call(functools.partial(beside_kernel, first), out, 0, [left, right], after)[0]


def stacked(parts, after=()):
    return call(stack_kernel, [shape(len(parts) * parts[0].shape[0], parts[0].shape[1])], 0, parts, after)[0]


def taken(array, rows, after, flops=0):
    return call(take_kernel, [shape(rows, array.shape[1])], flops, [array], after)[0]


def fetched(array, after):
    scratch = [pltpu.SemaphoreType.DMA]
    return call(fetch_kernel, [shape(*array.shape)], 0, [array], after, specs=[HBM], scratch=scratch)[0]


class Square:
    def core(self, array):
        return lax.ppermute(array, "inp", [(at, at ^ 1) for at in range(4)])

    def across(self, array):
        return lax.ppermute(array, "inp", [(at, at ^ 2) for at in range(4)])

    def other(self, array):
        return lax.ppermute(array, "out", [(0, 1), (1, 0)])

    def near(self, array):
        return lax.ppermute(array, "wt", [(at, at ^ 1) for at in range(4)])

    def far(self, array):
        return lax.ppermute(array, "wt", [(at, at ^ 2) for at in range(4)])

    def added(self, stay, came, after=()):
        half, cols = stay.shape[0] // 2, stay.shape[1]
        return call(add_kernel, [shape(half, cols, dtype=F32), shape(half, cols)], 0, [stay, came], after)

    def products(self, left, rights, places, adds=(), after=()):
        far = int(not adds)
        quarter, depth = left.shape[0] // 4, left.shape[1]
        half = rights[0][2]
        outs = [shape(quarter, half)] * len(places)
        use = sorted({other for _, other in places})
        chips = sorted({chip for chip, _ in places})
        first = 2 * far * quarter + chips[0] * quarter
        wanted = [((chip - chips[0]) * quarter, use.index(other)) for chip, other in places]
        args = [left] + [rights[other][0] for other in use] + [adds[place] for place in places if adds]
        blocks = call(
            functools.partial(block_kernel, first, wanted, [rights[other][1] for other in use], bool(adds)),
            outs,
            2 * len(places) * quarter * depth * half,
            args,
            after,
            specs=[ANY] * (1 + len(use)) + [VMEM] * (len(args) - 1 - len(use)),
            scratch=[
                pltpu.VMEM((len(chips) * quarter, depth), BF16),
                pltpu.VMEM((len(use), depth, half), BF16),
                pltpu.SemaphoreType.DMA((1 + len(use),)),
            ],
        )
        return dict(zip(places, blocks))

    def far_first(self, left, rights, after):
        return self.products(left, rights, [(1, 1)], after=after)

    def far_rest(self, left, rights, after):
        return self.products(left, rights, [(0, 1), (1, 0), (0, 0)], after=after)

    def near_first(self, left, rights, far, after):
        return self.products(left, rights, [(1, 1)], far, after)

    def near_rest(self, left, rights, far, after):
        return self.products(left, rights, [(0, 1), (1, 0), (0, 0)], far, after)

    def layer(self, tokens, gate_weight, up_weight, down_weight, cotangent):
        at_out = lax.axis_index("out").astype(jnp.int32).reshape(1)
        half, width = gate_weight.shape[0], gate_weight.shape[1] // 2
        mine, down_mine, theirs = call(
            halves_kernel,
            [shape(2 * width, half), shape(width, half), shape(3 * width, half)],
            0,
            [at_out, gate_weight, up_weight, down_weight],
            specs=[SMEM, HBM, HBM, HBM],
            scratch=[
                pltpu.VMEM(gate_weight.shape, BF16),
                pltpu.VMEM(up_weight.shape, BF16),
                pltpu.VMEM(down_weight.shape, BF16),
                pltpu.SemaphoreType.DMA((3,)),
            ],
        )
        came = self.other(theirs)
        step = tokens.shape[1]
        tok, cot = tokens.reshape(2 * step, half), cotangent.reshape(2 * step, half)

        tok_near = self.near(tok)
        far_mine, across_mine = self.far(mine), self.across(mine)
        late_tok = fetched(tok, [came, across_mine])
        tok_other = self.other(late_tok)
        theirs = taken(came, 2 * width, [far_mine, across_mine])
        tok_corner = self.other(taken(tok_near, 2 * step, [far_mine, tok_other]))
        far_theirs, across_theirs = self.far(theirs), self.across(theirs)
        corner_mine = self.across(far_mine)
        corner_theirs = self.across(far_theirs)
        unit_groups = [across_mine, corner_mine, mine, far_mine, across_theirs, corner_theirs, theirs, far_theirs]
        own_down = beside(down_mine, came, 2 * width, [far_theirs, across_theirs, corner_mine])
        far_down = self.far(own_down)
        cot_near = self.near(fetched(cot, [tok_near]))
        late_cot = fetched(cot, [tok_corner, far_theirs])
        cot_other = self.other(late_cot)
        tok_top = beside(tok, tok_other)
        tok_low = beside(tok_near, tok_corner, 0, [late_cot, across_theirs, corner_theirs])
        rows_in = [tok_top, tok_low, self.core(tok_top), self.core(tok_low)]
        cot_corner = [self.other(cot_near[:step]), self.near(cot_other[step:])]
        down_groups = [self.across(own_down), taken(self.across(far_down), width, [], SLOW), own_down, far_down]

        count, units = 8 * step, 4 * width
        hidden, hidden_turned, silu, rest = call(
            functools.partial(hidden_kernel, width, 4, 4),
            [shape(count, units), shape(units, count), shape(count, units), shape(count, units)],
            8 * count * units * half,
            [*rows_in, *unit_groups],
            after=[*down_groups[:2], cot_other],
            specs=[HBM] * (4 + len(unit_groups)),
            scratch=[
                pltpu.VMEM((4, 2 * step, 2 * half), BF16),
                pltpu.SemaphoreType.DMA((4,)),
                pltpu.VMEM((len(unit_groups), 2 * width, half), BF16),
                pltpu.SemaphoreType.DMA((len(unit_groups),)),
            ],
            limit=30,
        )
        cot_top = beside(cot, cot_other)
        outs = [shape(2 * step, 2 * half)]
        (cot_low,) = call(halves_beside_kernel, outs, 0, [cot_near, *cot_corner], [hidden])
        rows_cot = [cot_top, cot_low, self.core(cot_top), self.core(cot_low)]
        down = stacked(down_groups)
        down_sides = [(down, 0, half), (down, 1, half)]
        output_far = self.far_first(hidden, down_sides, [])
        output_far |= self.far_rest(hidden, down_sides, [output_far[1, 1]])
        down_terms = call(
            functools.partial(weight_kernel, 0, 256, 4),
            [shape(units // 2, 2 * half)] * 2,
            4 * count * units * half,
            [*rows_cot, hidden_turned],
            list(output_far.values()),
            specs=[HBM] * 4 + [VMEM],
            scratch=[pltpu.VMEM((2, 4, 2 * step, half), BF16), pltpu.SemaphoreType.DMA((2, 4))],
        )
        down_half, down_far = self.added(down_terms[1], self.across(down_terms[0]))
        down_came = self.far(down_far)
        act, act_turned = call(
            functools.partial(grads_kernel, width, 4),
            [shape(count, 2 * units), shape(2 * units, count)],
            4 * count * units * half,
            [*rows_cot, silu, rest, down],
            after=down_terms,
            specs=[HBM] * 6 + [VMEM],
            scratch=[
                pltpu.VMEM((4, 2 * step, 2 * half), BF16),
                pltpu.SemaphoreType.DMA((4,)),
                pltpu.VMEM((count, units), BF16),
                pltpu.VMEM((count, units), BF16),
                pltpu.SemaphoreType.DMA((4,)),
                pltpu.SemaphoreType.DMA((4,)),
            ],
            limit=30,
        )
        output_far = {place: self.core(block) for place, block in output_far.items()}
        sums = self.near_first(hidden, down_sides, output_far, [act])
        corner = sums[1, 1]
        by_other, by_near = self.other(corner[:step]), self.near(corner[step:])
        sums |= self.near_rest(hidden, down_sides, output_far, [corner])

        def unit_terms(side, after):
            return call(
                functools.partial(weight_kernel, side * half, 256, 4),
                [shape(units, half)] * 2,
                4 * count * units * half,
                [*rows_in, act_turned],
                after=after,
                specs=[HBM] * 4 + [VMEM],
                scratch=[pltpu.VMEM((2, 4, 2 * step, half // 2), BF16), pltpu.SemaphoreType.DMA((2, 4))],
            )

        other_terms = unit_terms(1, [sums[0, 0]])
        other_across = self.across(other_terms[0])
        (gate_up,) = call(
            functools.partial(units_kernel, 4),
            [shape(2 * units, 2 * half)],
            0,
            unit_groups,
            [other_terms[0], down_far],
            specs=[HBM] * 8,
            scratch=[pltpu.SemaphoreType.DMA((8,))],
        )
        unit_sides = [(gate_up, 0, half), (gate_up, 1, half)]
        grads_far = self.far_first(act, unit_sides, [])
        grads_far = {place: self.core(block) for place, block in grads_far.items()}
        grads_sums = self.near_first(act, unit_sides, grads_far, [])
        grads_corner = self.other(grads_sums[1, 1])
        own_terms = unit_terms(0, [grads_sums[1, 1]])
        zeros = jnp.zeros((step, half), F32)
        to_near = (sums[1, 0].astype(F32) + jnp.concatenate([by_other.astype(F32), zeros])).astype(BF16)
        to_other = (sums[0, 1].astype(F32) + jnp.concatenate([zeros, by_near.astype(F32)])).astype(BF16)
        by_near, by_other = self.near(to_near), self.other(to_other)
        total = sums[0, 0].astype(F32) + by_near.astype(F32) + by_other.astype(F32)
        output = total.astype(BF16).reshape(2, step, half)

        waits = [own_terms[0], by_other, by_near, other_across, down_came]
        for place, block in self.far_rest(act, unit_sides, waits).items():
            grads_far[place] = self.core(block)
        own_across = self.across(own_terms[0])
        own_half, own_far = self.added(own_terms[1], own_across)
        own_came = self.far(own_far)
        down_sum = down_half + down_came.astype(F32)
        down_back = self.other(down_sum[:, half:].astype(BF16))
        other_half, other_far = self.added(other_terms[1], other_across)
        other_came = self.far(other_far)
        (other_sum,) = call(sum_kernel, [shape(2 * width, half)], 0, [other_half, other_came], [grads_corner])
        sums = self.near_rest(act, unit_sides, grads_far, [own_far, other_sum])
        (to_near,) = call(sum_kernel, [shape(2 * step, half)], 0, [sums[1, 0], grads_corner])
        by_near, by_other = self.near(to_near), self.other(sums[0, 1])
        total = sums[0, 0].astype(F32) + by_near.astype(F32) + by_other.astype(F32)
        grad_tokens = total.astype(BF16).reshape(2, step, half)

        own_sum = (own_half + own_came.astype(F32)).astype(BF16)
        units_back = self.other(other_sum)
        mine, theirs = down_sum[:, :half], down_back.astype(F32)
        first = at_out[0] == 0
        grad_down = jnp.where(first, jnp.concatenate([mine, theirs]), jnp.concatenate([theirs, mine]))
        grad_gate, grad_up = call(
            finish_kernel,
            [shape(half, 2 * width, dtype=F32)] * 2,
            0,
            [at_out, own_sum, units_back],
            specs=[SMEM, VMEM, VMEM],
        )
        return (output, grad_tokens, grad_gate, grad_up, grad_down)


class Plain:
    def units(self, weight):
        own = lax.all_to_all(weight, "out", split_axis=0, concat_axis=1, tiled=True)
        return lax.all_gather(own, "wt", axis=0, tiled=True)

    def unit_sums(self, grad):
        own = lax.psum_scatter(grad.astype(BF16), "wt", scatter_dimension=0, tiled=True)
        return lax.all_to_all(own, "out", split_axis=1, concat_axis=0, tiled=True).astype(F32)

    def gather(self, array):
        array = lax.all_gather(lax.all_gather(array, "inp", axis=1, tiled=True), "out", axis=2, tiled=True)
        return array.reshape(-1, array.shape[2])

    def scatter(self, partial, batches):
        partial = partial.astype(BF16).reshape(batches, -1, partial.shape[1])
        partial = lax.psum_scatter(partial, "out", scatter_dimension=2, tiled=True)
        return lax.psum_scatter(partial, "inp", scatter_dimension=1, tiled=True)

    def layer(self, tokens, gate_weight, up_weight, down_weight, cotangent):
        gate, up, down = self.units(gate_weight.T), self.units(up_weight.T), self.units(down_weight)
        rows_in, rows_cot = self.gather(tokens), self.gather(cotangent)
        gate_sum = matmul(rows_in, gate, (1, 1))
        up_sum = matmul(rows_in, up, (1, 1))
        silu_g, hidden, rest = gated(gate_sum, up_sum)
        hidden = hidden.astype(BF16)
        grad_down = self.unit_sums(matmul(hidden, rows_cot, (0, 0)))
        back_sum = matmul(rows_cot, down, (1, 1))
        gate_act, up_act = (back_sum * rest).astype(BF16), (back_sum * silu_g).astype(BF16)
        grad_gate = self.unit_sums(matmul(gate_act, rows_in, (0, 0))).T
        grad_up = self.unit_sums(matmul(up_act, rows_in, (0, 0))).T
        output = self.scatter(matmul(hidden, down, (1, 0)), tokens.shape[0])
        partial = matmul(gate_act, gate, (1, 0)) + matmul(up_act, up, (1, 0))
        grad_tokens = self.scatter(partial, tokens.shape[0])
        return (output, grad_tokens, grad_gate, grad_up, grad_down)


def solution(mesh):
    square = mesh.shape["inp"] == 4 and mesh.shape["out"] == 2 and mesh.shape["wt"] == 4

    def on_device(tokens, *others):
        places = Square() if square and tokens.shape[0] == 2 else Plain()
        return places.layer(tokens, *others)

    rows_spec = P(None, ("inp", "wt"), "out")
    in_spec = P("out", ("wt", "inp"))
    down_spec = P(("wt", "inp"), "out")
    return jax.shard_map(
        on_device,
        mesh=mesh,
        in_specs=(rows_spec, in_spec, in_spec, down_spec, rows_spec),
        out_specs=(rows_spec, rows_spec, in_spec, in_spec, down_spec),
        check_vma=False,
    )
```

```python
import functools

import jax
import jax.numpy as jnp
from jax import lax
from jax.experimental import pallas as pl
from jax.experimental.pallas import tpu as pltpu
from jax.sharding import PartitionSpec as P

F32 = jnp.float32
BF16 = jnp.bfloat16
MIB = 1024 * 1024


def matmul(a, b, contract):
    return lax.dot_general(a, b, ((contract[:1], contract[1:]), ((), ())), preferred_element_type=F32)


def gated(gate_sum, up_sum):
    sigmoid_g = jax.nn.sigmoid(gate_sum)
    silu_g = gate_sum * sigmoid_g
    slope = sigmoid_g * (1.0 + gate_sum * (1.0 - sigmoid_g))
    return silu_g, silu_g * up_sum, up_sum * slope


def shape(*dims, dtype=BF16):
    return jax.ShapeDtypeStruct(dims, dtype)


def call(kernel, outs, flops, args, after=(), specs=None, scratch=(), limit=24):
    everything = [*args, *after]
    moved = sum(a.size * a.dtype.itemsize for a in args) + sum(o.size * o.dtype.itemsize for o in outs)
    specs = specs or [pl.BlockSpec(memory_space=pltpu.VMEM)] * len(args)

    def body(*refs):
        kernel(*refs[: len(args)], *refs[len(everything) :])

    return pl.pallas_call(
        body,
        out_shape=list(outs),
        in_specs=[*specs, *[pl.BlockSpec(memory_space=pl.ANY)] * len(after)],
        out_specs=[pl.BlockSpec(memory_space=pltpu.VMEM)] * len(outs),
        scratch_shapes=list(scratch),
        compiler_params=pltpu.CompilerParams(vmem_limit_bytes=limit * MIB),
        cost_estimate=pl.CostEstimate(flops=flops, bytes_accessed=moved, transcendentals=0),
    )(*everything)


ANY = pl.BlockSpec(memory_space=pl.ANY)
HBM = pl.BlockSpec(memory_space=pltpu.HBM)
VMEM = pl.BlockSpec(memory_space=pltpu.VMEM)
SMEM = pl.BlockSpec(memory_space=pltpu.SMEM)


class Rows:
    def __init__(self, pieces, blocks, step):
        self.pieces, self.blocks, self.step = pieces, blocks, step

    def read(self, refs, at, side):
        piece, first = self.blocks[at][side]
        return refs[piece].at[first : first + self.step]


def hidden_kernel(rows, width, *refs):
    count = len(rows.pieces)
    pieces, (own_ref, other_ref, hidden_ref, turned_ref, silu_ref, rest_ref) = refs[:count], refs[count:]
    groups = own_ref.shape[0] // (2 * width)
    for at in range(len(rows.blocks)):
        span = slice(at * rows.step, (at + 1) * rows.step)
        sums = matmul(rows.read(pieces, at, 0)[...], own_ref[...], (1, 1))
        sums = sums + matmul(rows.read(pieces, at, 1)[...], other_ref[...], (1, 1))
        for group in range(groups):
            low = 2 * group * width
            silu_g, hidden, rest = gated(sums[:, low : low + width], sums[:, low + width : low + 2 * width])
            cols = slice(group * width, (group + 1) * width)
            hidden_ref[span, cols] = hidden.astype(BF16)
            turned_ref[cols, span] = hidden.T.astype(BF16)
            silu_ref[span, cols] = silu_g.astype(BF16)
            rest_ref[span, cols] = rest.astype(BF16)


def grads_kernel(rows, width, *refs):
    count = len(rows.pieces)
    pieces, (down_ref, silu_ref, rest_ref, act_ref, turned_ref) = refs[:count], refs[count:]
    groups = down_ref.shape[0] // width
    half = down_ref.shape[1] // 2
    for at in range(len(rows.blocks)):
        span = slice(at * rows.step, (at + 1) * rows.step)
        back = matmul(rows.read(pieces, at, 0)[...], down_ref[:, :half], (1, 1))
        back = back + matmul(rows.read(pieces, at, 1)[...], down_ref[:, half:], (1, 1))
        for group in range(groups):
            cols = slice(group * width, (group + 1) * width)
            for part, factor in enumerate((rest_ref, silu_ref)):
                grad = back[:, cols] * factor[span, cols].astype(F32)
                low = (2 * group + part) * width
                act_ref[span, low : low + width] = grad.astype(BF16)
                turned_ref[low : low + width, span] = grad.T.astype(BF16)


def weight_kernel(rows, sides, tile, *refs):
    count = len(rows.pieces)
    pieces, (turned_ref, out_ref) = refs[:count], refs[count:]
    half = out_ref.shape[1] // len(sides)
    for place, side in enumerate(sides):

        @pl.loop(0, half // tile)
        def _(index):
            cols = pl.ds(pl.multiple_of(index * tile, tile), tile)
            total = jnp.zeros((out_ref.shape[0], tile), F32)
            for at in range(len(rows.blocks)):
                span = slice(at * rows.step, (at + 1) * rows.step)
                total = total + matmul(turned_ref[:, span], rows.read(pieces, at, side)[:, cols], (1, 0))
            out_ref[:, pl.ds(pl.multiple_of(place * half + index * tile, tile), tile)] = total.astype(BF16)


def block_kernel(first, places, sides, added, *refs):
    rights, many = len(sides), len(places)
    left_any, right_any, refs = refs[0], refs[1 : 1 + rights], refs[1 + rights :]
    adds, refs = refs[: many * added], refs[many * added :]
    outs, (left_ref, right_ref, sems) = refs[:many], refs[many:]
    depth, half = right_ref.shape[1:]
    copies = [pltpu.make_async_copy(left_any.at[pl.ds(first, left_ref.shape[0])], left_ref, sems.at[0])]
    for at, side in enumerate(sides):
        source = right_any[at].at[:, pl.ds(side * half, half)]
        copies.append(pltpu.make_async_copy(source, right_ref.at[at], sems.at[1 + at]))
    for copy in copies:
        copy.start()
    for copy in copies:
        copy.wait()
    for at, (row, right) in enumerate(places):
        total = matmul(left_ref[row : row + outs[at].shape[0]], right_ref[right], (1, 0))
        if added:
            total = total + adds[at][...].astype(F32)
        outs[at][...] = total.astype(BF16)


def sum_kernel(left_ref, right_ref, out_ref):
    out_ref[...] = (left_ref[...].astype(F32) + right_ref[...].astype(F32)).astype(BF16)


def finish_kernel(at_ref, mine_ref, theirs_ref, gate_ref, up_ref):
    width = mine_ref.shape[0] // 2
    for part, out_ref in enumerate((gate_ref, up_ref)):
        span = slice(part * width, (part + 1) * width)
        mine, theirs = mine_ref[span].astype(F32).T, theirs_ref[span].astype(F32).T
        first = at_ref[0] == 0
        out_ref[:, :width] = jnp.where(first, mine, theirs)
        out_ref[:, width:] = jnp.where(first, theirs, mine)


class Square:
    def core(self, array):
        return lax.ppermute(array, "inp", [(at, at ^ 1) for at in range(4)])

    def chip(self, array):
        return lax.ppermute(array, "inp", [(at, at ^ 2) for at in range(4)])

    def other(self, array):
        return lax.ppermute(array, "out", [(0, 1), (1, 0)])

    def unit_halves(self, weight):
        half = weight.shape[0] // 2
        at = lax.axis_index("out")
        return (
            lax.dynamic_slice_in_dim(weight, at * half, half, 0),
            lax.dynamic_slice_in_dim(weight, (1 - at) * half, half, 0),
        )

    def in_order(self, mine, theirs):
        mine, theirs = mine.astype(F32), theirs.astype(F32)
        first = lax.axis_index("out") == 0
        return jnp.where(first, jnp.concatenate([mine, theirs]), jnp.concatenate([theirs, mine]))

    def gather(self, array):
        step = array.shape[1]
        own = array.reshape(2 * step, array.shape[2])
        by_chip, by_other = self.chip(own), self.other(own)
        corner = [self.other(by_chip[:step]), self.chip(by_other[step:])]
        pieces = [own, by_other, by_chip] + corner
        pieces = pieces + [self.core(piece) for piece in pieces]
        blocks = []
        for base in (0, 5):
            blocks += [((base, 0), (base + 1, 0)), ((base, step), (base + 1, step))]
            blocks += [((base + 2, 0), (base + 3, 0)), ((base + 2, step), (base + 4, 0))]
        return Rows(pieces, blocks, step)

    def products(self, left, rights, places, adds=(), after=()):
        far = int(not adds)
        quarter, depth = left.shape[0] // 4, left.shape[1]
        half = rights[0][2]
        outs = [shape(quarter, half)] * len(places)
        use = sorted({other for _, other in places})
        chips = sorted({chip for chip, _ in places})
        first = 2 * far * quarter + chips[0] * quarter
        wanted = [((chip - chips[0]) * quarter, use.index(other)) for chip, other in places]
        args = [left] + [rights[other][0] for other in use] + [adds[place] for place in places if adds]
        blocks = call(
            functools.partial(block_kernel, first, wanted, [rights[other][1] for other in use], bool(adds)),
            outs,
            2 * len(places) * quarter * depth * half,
            args,
            after,
            specs=[ANY] * (1 + len(use)) + [VMEM] * (len(args) - 1 - len(use)),
            scratch=[
                pltpu.VMEM((len(chips) * quarter, depth), BF16),
                pltpu.VMEM((len(use), depth, half), BF16),
                pltpu.SemaphoreType.DMA((1 + len(use),)),
            ],
        )
        return dict(zip(places, blocks))

    def far_first(self, left, rights, after):
        return self.products(left, rights, [(1, 1)], after=after)

    def far_rest(self, left, rights, after):
        return self.products(left, rights, [(0, 1), (1, 0), (0, 0)], after=after)

    def near_first(self, left, rights, far, after):
        return self.products(left, rights, [(1, 1)], far, after)

    def near_rest(self, left, rights, far, after):
        return self.products(left, rights, [(0, 1), (1, 0), (0, 0)], far, after)

    def layer(self, tokens, gate_weight, up_weight, down_weight, cotangent):
        def gather_units(array):
            return lax.all_gather(array, "wt", axis=0, tiled=True)

        def scatter_units(array):
            return lax.psum_scatter(array, "wt", scatter_dimension=0, tiled=True)

        gate_mine, gate_theirs = self.unit_halves(gate_weight.T)
        up_mine, up_theirs = self.unit_halves(up_weight.T)
        down_mine, down_theirs = self.unit_halves(down_weight)
        width, half = gate_mine.shape
        own_units = gather_units(jnp.concatenate([gate_mine, up_mine]))
        other_units = gather_units(self.other(jnp.concatenate([gate_theirs, up_theirs])))
        down = gather_units(jnp.concatenate([down_mine, self.other(down_theirs)], axis=1))
        rows_in = self.gather(tokens)
        rows_cot = self.gather(cotangent)
        step = rows_in.step
        count = len(rows_in.blocks) * step
        units = down.shape[0]

        hidden, hidden_turned, silu, rest = call(
            functools.partial(hidden_kernel, rows_in, width),
            [shape(count, units), shape(units, count), shape(count, units), shape(count, units)],
            8 * count * units * half,
            [*rows_in.pieces, own_units, other_units],
            limit=44,
        )
        (down_term,) = call(
            functools.partial(weight_kernel, rows_cot, (0, 1), 256),
            [shape(units, 2 * half)],
            4 * count * units * half,
            [*rows_cot.pieces, hidden_turned],
            limit=44,
        )
        down_sum = scatter_units(down_term)
        down_sides = [(down, 0, half), (down, 1, half)]
        output_far = self.far_first(hidden, down_sides, [])
        output_far |= self.far_rest(hidden, down_sides, [output_far[1, 1]])
        act, act_turned = call(
            functools.partial(grads_kernel, rows_cot, width),
            [shape(count, 2 * units), shape(2 * units, count)],
            4 * count * units * half,
            [*rows_cot.pieces, down, silu, rest],
            after=list(output_far.values()),
            limit=44,
        )

        def unit_term(side, after):
            return call(
                functools.partial(weight_kernel, rows_in, (side,), 256),
                [shape(2 * units, half)],
                4 * count * units * half,
                [*rows_in.pieces, act_turned],
                after,
                limit=44,
            )[0]

        output_far = {place: self.core(block) for place, block in output_far.items()}
        sums = self.near_first(hidden, down_sides, output_far, [act])
        corner = sums[1, 1]
        by_other, by_chip = self.other(corner[:step]), self.chip(corner[step:])
        sums |= self.near_rest(hidden, down_sides, output_far, [corner])
        other_term = unit_term(1, [sums[0, 0]])
        other_sum = scatter_units(other_term)
        unit_sides = [(own_units, 0, half), (other_units, 0, half)]
        grads_far = self.far_first(act, unit_sides, [other_term, by_other, by_chip])
        grads_far |= self.far_rest(act, unit_sides, [grads_far[1, 1]])
        zeros = jnp.zeros((step, half), F32)
        to_chip = (sums[1, 0].astype(F32) + jnp.concatenate([by_other.astype(F32), zeros])).astype(BF16)
        to_other = (sums[0, 1].astype(F32) + jnp.concatenate([zeros, by_chip.astype(F32)])).astype(BF16)
        output_chip, output_other = self.chip(to_chip), self.other(to_other)
        own_term = unit_term(0, list(grads_far.values()))
        own_sum = scatter_units(own_term)
        grads_far = {place: self.core(block) for place, block in grads_far.items()}
        grads = self.near_first(act, unit_sides, grads_far, [own_term])
        corner = self.chip(grads[1, 1])
        down_back = self.other(down_sum[:, half:])
        grads |= self.near_rest(act, unit_sides, grads_far, [grads[1, 1], output_chip, output_other])
        by_chip = self.chip(grads[1, 0])
        (to_other,) = call(sum_kernel, [shape(2 * step, half)], 0, [grads[0, 1], corner])
        by_other = self.other(to_other)
        total = sums[0, 0].astype(F32) + output_chip.astype(F32) + output_other.astype(F32)
        output = total.astype(BF16).reshape(2, step, half)
        units_back = self.other(other_sum)
        (partial,) = call(sum_kernel, [shape(2 * step, half)], 0, [grads[0, 0], by_chip], [down_back])
        (total,) = call(sum_kernel, [shape(2 * step, half)], 0, [partial, by_other], [units_back])
        grad_tokens = total.reshape(2, step, half)

        at_out = lax.axis_index("out").astype(jnp.int32).reshape(1)
        mine, theirs = down_sum[:, :half].astype(F32), down_back.astype(F32)
        first = at_out[0] == 0
        grad_down = jnp.where(first, jnp.concatenate([mine, theirs]), jnp.concatenate([theirs, mine]))
        grad_gate, grad_up = call(
            finish_kernel,
            [shape(half, 2 * width, dtype=F32)] * 2,
            0,
            [at_out, own_sum, units_back],
            [total],
            specs=[SMEM, VMEM, VMEM],
        )
        return (output, grad_tokens, grad_gate, grad_up, grad_down)


class Plain:
    def units(self, weight):
        own = lax.all_to_all(weight, "out", split_axis=0, concat_axis=1, tiled=True)
        return lax.all_gather(own, "wt", axis=0, tiled=True)

    def unit_sums(self, grad):
        own = lax.psum_scatter(grad.astype(BF16), "wt", scatter_dimension=0, tiled=True)
        return lax.all_to_all(own, "out", split_axis=1, concat_axis=0, tiled=True).astype(F32)

    def gather(self, array):
        array = lax.all_gather(lax.all_gather(array, "inp", axis=1, tiled=True), "out", axis=2, tiled=True)
        return array.reshape(-1, array.shape[2])

    def scatter(self, partial, batches):
        partial = partial.astype(BF16).reshape(batches, -1, partial.shape[1])
        partial = lax.psum_scatter(partial, "out", scatter_dimension=2, tiled=True)
        return lax.psum_scatter(partial, "inp", scatter_dimension=1, tiled=True)

    def layer(self, tokens, gate_weight, up_weight, down_weight, cotangent):
        gate, up, down = self.units(gate_weight.T), self.units(up_weight.T), self.units(down_weight)
        rows_in, rows_cot = self.gather(tokens), self.gather(cotangent)
        gate_sum = matmul(rows_in, gate, (1, 1))
        up_sum = matmul(rows_in, up, (1, 1))
        silu_g, hidden, rest = gated(gate_sum, up_sum)
        hidden = hidden.astype(BF16)
        grad_down = self.unit_sums(matmul(hidden, rows_cot, (0, 0)))
        back_sum = matmul(rows_cot, down, (1, 1))
        gate_act, up_act = (back_sum * rest).astype(BF16), (back_sum * silu_g).astype(BF16)
        grad_gate = self.unit_sums(matmul(gate_act, rows_in, (0, 0))).T
        grad_up = self.unit_sums(matmul(up_act, rows_in, (0, 0))).T
        output = self.scatter(matmul(hidden, down, (1, 0)), tokens.shape[0])
        partial = matmul(gate_act, gate, (1, 0)) + matmul(up_act, up, (1, 0))
        grad_tokens = self.scatter(partial, tokens.shape[0])
        return (output, grad_tokens, grad_gate, grad_up, grad_down)


def solution(mesh):
    square = mesh.shape["inp"] == 4 and mesh.shape["out"] == 2

    def on_device(tokens, *others):
        places = Square() if square and tokens.shape[0] == 2 else Plain()
        return places.layer(tokens, *others)

    rows_spec = P(None, ("inp", "wt"), "out")
    in_spec = P("out", ("wt", "inp"))
    down_spec = P(("wt", "inp"), "out")
    return jax.shard_map(
        on_device,
        mesh=mesh,
        in_specs=(rows_spec, in_spec, in_spec, down_spec, rows_spec),
        out_specs=(rows_spec, rows_spec, in_spec, in_spec, down_spec),
        check_vma=False,
    )
```

```python
import functools

import jax
import jax.numpy as jnp
from jax import lax
from jax.experimental import pallas as pl
from jax.experimental.pallas import tpu as pltpu
from jax.sharding import PartitionSpec as P

F32 = jnp.float32
BF16 = jnp.bfloat16
MIB = 1024 * 1024


def matmul(a, b, contract):
    return lax.dot_general(a, b, ((contract[:1], contract[1:]), ((), ())), preferred_element_type=F32)


def gated(gate_sum, up_sum):
    sigmoid_g = jax.nn.sigmoid(gate_sum)
    silu_g = gate_sum * sigmoid_g
    slope = sigmoid_g * (1.0 + gate_sum * (1.0 - sigmoid_g))
    return silu_g, silu_g * up_sum, up_sum * slope


def shape(*dims, dtype=BF16):
    return jax.ShapeDtypeStruct(dims, dtype)


def call(kernel, outs, flops, args, after=(), specs=None, scratch=(), limit=24):
    everything = [*args, *after]
    moved = sum(a.size * a.dtype.itemsize for a in args) + sum(o.size * o.dtype.itemsize for o in outs)
    specs = specs or [pl.BlockSpec(memory_space=pltpu.VMEM)] * len(args)

    def body(*refs):
        kernel(*refs[: len(args)], *refs[len(everything) :])

    return pl.pallas_call(
        body,
        out_shape=list(outs),
        in_specs=[*specs, *[pl.BlockSpec(memory_space=pl.ANY)] * len(after)],
        out_specs=[pl.BlockSpec(memory_space=pltpu.VMEM)] * len(outs),
        scratch_shapes=list(scratch),
        compiler_params=pltpu.CompilerParams(vmem_limit_bytes=limit * MIB),
        cost_estimate=pl.CostEstimate(flops=flops, bytes_accessed=moved, transcendentals=0),
    )(*everything)


ANY = pl.BlockSpec(memory_space=pl.ANY)
HBM = pl.BlockSpec(memory_space=pltpu.HBM)
VMEM = pl.BlockSpec(memory_space=pltpu.VMEM)
SMEM = pl.BlockSpec(memory_space=pltpu.SMEM)


class Rows:
    def __init__(self, pieces, blocks, step):
        self.pieces, self.blocks, self.step = pieces, blocks, step

    def read(self, refs, at, side):
        piece, first = self.blocks[at][side]
        return refs[piece].at[first : first + self.step]


def hidden_kernel(rows, width, *refs):
    count = len(rows.pieces)
    pieces, (own_ref, other_ref, hidden_ref, turned_ref, silu_ref, rest_ref) = refs[:count], refs[count:]
    groups = own_ref.shape[0] // (2 * width)
    for at in range(len(rows.blocks)):
        span = slice(at * rows.step, (at + 1) * rows.step)
        sums = matmul(rows.read(pieces, at, 0)[...], own_ref[...], (1, 1))
        sums = sums + matmul(rows.read(pieces, at, 1)[...], other_ref[...], (1, 1))
        for group in range(groups):
            low = 2 * group * width
            silu_g, hidden, rest = gated(sums[:, low : low + width], sums[:, low + width : low + 2 * width])
            cols = slice(group * width, (group + 1) * width)
            hidden_ref[span, cols] = hidden.astype(BF16)
            turned_ref[cols, span] = hidden.T.astype(BF16)
            silu_ref[span, cols] = silu_g.astype(BF16)
            rest_ref[span, cols] = rest.astype(BF16)


def grads_kernel(rows, width, *refs):
    count = len(rows.pieces)
    pieces, (down_ref, silu_ref, rest_ref, act_ref, turned_ref) = refs[:count], refs[count:]
    groups = down_ref.shape[0] // width
    half = down_ref.shape[1] // 2
    for at in range(len(rows.blocks)):
        span = slice(at * rows.step, (at + 1) * rows.step)
        back = matmul(rows.read(pieces, at, 0)[...], down_ref[:, :half], (1, 1))
        back = back + matmul(rows.read(pieces, at, 1)[...], down_ref[:, half:], (1, 1))
        for group in range(groups):
            cols = slice(group * width, (group + 1) * width)
            for part, factor in enumerate((rest_ref, silu_ref)):
                grad = back[:, cols] * factor[span, cols].astype(F32)
                low = (2 * group + part) * width
                act_ref[span, low : low + width] = grad.astype(BF16)
                turned_ref[low : low + width, span] = grad.T.astype(BF16)


def weight_kernel(rows, sides, tile, *refs):
    count = len(rows.pieces)
    pieces, (turned_ref, out_ref) = refs[:count], refs[count:]
    half = out_ref.shape[1] // len(sides)
    for place, side in enumerate(sides):

        @pl.loop(0, half // tile)
        def _(index):
            cols = pl.ds(pl.multiple_of(index * tile, tile), tile)
            total = jnp.zeros((out_ref.shape[0], tile), F32)
            for at in range(len(rows.blocks)):
                span = slice(at * rows.step, (at + 1) * rows.step)
                total = total + matmul(turned_ref[:, span], rows.read(pieces, at, side)[:, cols], (1, 0))
            out_ref[:, pl.ds(pl.multiple_of(place * half + index * tile, tile), tile)] = total.astype(BF16)


def block_kernel(first, places, sides, added, *refs):
    rights, many = len(sides), len(places)
    left_any, right_any, refs = refs[0], refs[1 : 1 + rights], refs[1 + rights :]
    adds, refs = refs[: many * added], refs[many * added :]
    outs, (left_ref, right_ref, sems) = refs[:many], refs[many:]
    depth, half = right_ref.shape[1:]
    copies = [pltpu.make_async_copy(left_any.at[pl.ds(first, left_ref.shape[0])], left_ref, sems.at[0])]
    for at, side in enumerate(sides):
        source = right_any[at].at[:, pl.ds(side * half, half)]
        copies.append(pltpu.make_async_copy(source, right_ref.at[at], sems.at[1 + at]))
    for copy in copies:
        copy.start()
    for copy in copies:
        copy.wait()
    for at, (row, right) in enumerate(places):
        total = matmul(left_ref[row : row + outs[at].shape[0]], right_ref[right], (1, 0))
        if added:
            total = total + adds[at][...].astype(F32)
        outs[at][...] = total.astype(BF16)


def sum_kernel(left_ref, right_ref, out_ref):
    out_ref[...] = (left_ref[...].astype(F32) + right_ref[...].astype(F32)).astype(BF16)


def finish_kernel(at_ref, mine_ref, theirs_ref, gate_ref, up_ref):
    width = mine_ref.shape[0] // 2
    for part, out_ref in enumerate((gate_ref, up_ref)):
        span = slice(part * width, (part + 1) * width)
        mine, theirs = mine_ref[span].astype(F32).T, theirs_ref[span].astype(F32).T
        first = at_ref[0] == 0
        out_ref[:, :width] = jnp.where(first, mine, theirs)
        out_ref[:, width:] = jnp.where(first, theirs, mine)


class Square:
    def core(self, array):
        return lax.ppermute(array, "inp", [(at, at ^ 1) for at in range(4)])

    def chip(self, array):
        return lax.ppermute(array, "inp", [(at, at ^ 2) for at in range(4)])

    def other(self, array):
        return lax.ppermute(array, "out", [(0, 1), (1, 0)])

    def unit_halves(self, weight):
        half = weight.shape[0] // 2
        at = lax.axis_index("out")
        return (
            lax.dynamic_slice_in_dim(weight, at * half, half, 0),
            lax.dynamic_slice_in_dim(weight, (1 - at) * half, half, 0),
        )

    def in_order(self, mine, theirs):
        mine, theirs = mine.astype(F32), theirs.astype(F32)
        first = lax.axis_index("out") == 0
        return jnp.where(first, jnp.concatenate([mine, theirs]), jnp.concatenate([theirs, mine]))

    def gather(self, array):
        step = array.shape[1]
        own = array.reshape(2 * step, array.shape[2])
        by_chip, by_other = self.chip(own), self.other(own)
        corner = [self.other(by_chip[:step]), self.chip(by_other[step:])]
        pieces = [own, by_other, by_chip] + corner
        pieces = pieces + [self.core(piece) for piece in pieces]
        blocks = []
        for base in (0, 5):
            blocks += [((base, 0), (base + 1, 0)), ((base, step), (base + 1, step))]
            blocks += [((base + 2, 0), (base + 3, 0)), ((base + 2, step), (base + 4, 0))]
        return Rows(pieces, blocks, step)

    def products(self, left, rights, places, adds=(), after=()):
        far = int(not adds)
        quarter, depth = left.shape[0] // 4, left.shape[1]
        half = rights[0][2]
        outs = [shape(quarter, half)] * len(places)
        use = sorted({other for _, other in places})
        chips = sorted({chip for chip, _ in places})
        first = 2 * far * quarter + chips[0] * quarter
        wanted = [((chip - chips[0]) * quarter, use.index(other)) for chip, other in places]
        args = [left] + [rights[other][0] for other in use] + [adds[place] for place in places if adds]
        blocks = call(
            functools.partial(block_kernel, first, wanted, [rights[other][1] for other in use], bool(adds)),
            outs,
            2 * len(places) * quarter * depth * half,
            args,
            after,
            specs=[ANY] * (1 + len(use)) + [VMEM] * (len(args) - 1 - len(use)),
            scratch=[
                pltpu.VMEM((len(chips) * quarter, depth), BF16),
                pltpu.VMEM((len(use), depth, half), BF16),
                pltpu.SemaphoreType.DMA((1 + len(use),)),
            ],
        )
        return dict(zip(places, blocks))

    def far_first(self, left, rights, after):
        return self.products(left, rights, [(1, 1)], after=after)

    def far_rest(self, left, rights, after):
        return self.products(left, rights, [(0, 1), (1, 0), (0, 0)], after=after)

    def near_first(self, left, rights, far, after):
        return self.products(left, rights, [(1, 1)], far, after)

    def near_rest(self, left, rights, far, after):
        return self.products(left, rights, [(0, 1), (1, 0), (0, 0)], far, after)

    def layer(self, tokens, gate_weight, up_weight, down_weight, cotangent):
        def gather_units(array):
            return lax.all_gather(array, "wt", axis=0, tiled=True)

        def scatter_units(array):
            return lax.psum_scatter(array, "wt", scatter_dimension=0, tiled=True)

        gate_mine, gate_theirs = self.unit_halves(gate_weight.T)
        up_mine, up_theirs = self.unit_halves(up_weight.T)
        down_mine, down_theirs = self.unit_halves(down_weight)
        width, half = gate_mine.shape
        own_units = gather_units(jnp.concatenate([gate_mine, up_mine]))
        other_units = gather_units(self.other(jnp.concatenate([gate_theirs, up_theirs])))
        down = gather_units(jnp.concatenate([down_mine, self.other(down_theirs)], axis=1))
        rows_in = self.gather(tokens)
        rows_cot = self.gather(cotangent)
        step = rows_in.step
        count = len(rows_in.blocks) * step
        units = down.shape[0]

        hidden, hidden_turned, silu, rest = call(
            functools.partial(hidden_kernel, rows_in, width),
            [shape(count, units), shape(units, count), shape(count, units), shape(count, units)],
            8 * count * units * half,
            [*rows_in.pieces, own_units, other_units],
            limit=44,
        )
        (down_term,) = call(
            functools.partial(weight_kernel, rows_cot, (0, 1), 256),
            [shape(units, 2 * half)],
            4 * count * units * half,
            [*rows_cot.pieces, hidden_turned],
            limit=44,
        )
        down_sum = scatter_units(down_term)
        down_sides = [(down, 0, half), (down, 1, half)]
        output_far = self.far_first(hidden, down_sides, [down_term])
        output_far |= self.far_rest(hidden, down_sides, [output_far[1, 1]])
        act, act_turned = call(
            functools.partial(grads_kernel, rows_cot, width),
            [shape(count, 2 * units), shape(2 * units, count)],
            4 * count * units * half,
            [*rows_cot.pieces, down, silu, rest],
            after=list(output_far.values()),
            limit=44,
        )

        def unit_term(side, after):
            return call(
                functools.partial(weight_kernel, rows_in, (side,), 256),
                [shape(2 * units, half)],
                4 * count * units * half,
                [*rows_in.pieces, act_turned],
                after,
                limit=44,
            )[0]

        output_far = {place: self.core(block) for place, block in output_far.items()}
        sums = self.near_first(hidden, down_sides, output_far, [act])
        corner = sums[1, 1]
        by_other, by_chip = self.other(corner[:step]), self.chip(corner[step:])
        sums |= self.near_rest(hidden, down_sides, output_far, [corner])
        other_term = unit_term(1, [sums[0, 0]])
        other_sum = scatter_units(other_term)
        unit_sides = [(own_units, 0, half), (other_units, 0, half)]
        grads_far = self.far_first(act, unit_sides, [other_term, by_other, by_chip])
        grads_far |= self.far_rest(act, unit_sides, [grads_far[1, 1]])
        zeros = jnp.zeros((step, half), F32)
        to_chip = (sums[1, 0].astype(F32) + jnp.concatenate([by_other.astype(F32), zeros])).astype(BF16)
        to_other = (sums[0, 1].astype(F32) + jnp.concatenate([zeros, by_chip.astype(F32)])).astype(BF16)
        output_chip, output_other = self.chip(to_chip), self.other(to_other)
        own_term = unit_term(0, list(grads_far.values()))
        own_sum = scatter_units(own_term)
        grads_far = {place: self.core(block) for place, block in grads_far.items()}
        grads = self.near_first(act, unit_sides, grads_far, [own_term])
        corner = self.chip(grads[1, 1])
        down_back = self.other(down_sum[:, half:])
        grads |= self.near_rest(act, unit_sides, grads_far, [grads[1, 1], output_chip, output_other])
        by_chip = self.chip(grads[1, 0])
        (to_other,) = call(sum_kernel, [shape(2 * step, half)], 0, [grads[0, 1], corner])
        by_other = self.other(to_other)
        total = sums[0, 0].astype(F32) + output_chip.astype(F32) + output_other.astype(F32)
        output = total.astype(BF16).reshape(2, step, half)
        units_back = self.other(other_sum)
        (partial,) = call(sum_kernel, [shape(2 * step, half)], 0, [grads[0, 0], by_chip], [down_back])
        (total,) = call(sum_kernel, [shape(2 * step, half)], 0, [partial, by_other], [units_back])
        grad_tokens = total.reshape(2, step, half)

        at_out = lax.axis_index("out").astype(jnp.int32).reshape(1)
        mine, theirs = down_sum[:, :half].astype(F32), down_back.astype(F32)
        first = at_out[0] == 0
        grad_down = jnp.where(first, jnp.concatenate([mine, theirs]), jnp.concatenate([theirs, mine]))
        grad_gate, grad_up = call(
            finish_kernel,
            [shape(half, 2 * width, dtype=F32)] * 2,
            0,
            [at_out, own_sum, units_back],
            [total],
            specs=[SMEM, VMEM, VMEM],
        )
        return (output, grad_tokens, grad_gate, grad_up, grad_down)


class Plain:
    def units(self, weight):
        own = lax.all_to_all(weight, "out", split_axis=0, concat_axis=1, tiled=True)
        return lax.all_gather(own, "wt", axis=0, tiled=True)

    def unit_sums(self, grad):
        own = lax.psum_scatter(grad.astype(BF16), "wt", scatter_dimension=0, tiled=True)
        return lax.all_to_all(own, "out", split_axis=1, concat_axis=0, tiled=True).astype(F32)

    def gather(self, array):
        array = lax.all_gather(lax.all_gather(array, "inp", axis=1, tiled=True), "out", axis=2, tiled=True)
        return array.reshape(-1, array.shape[2])

    def scatter(self, partial, batches):
        partial = partial.astype(BF16).reshape(batches, -1, partial.shape[1])
        partial = lax.psum_scatter(partial, "out", scatter_dimension=2, tiled=True)
        return lax.psum_scatter(partial, "inp", scatter_dimension=1, tiled=True)

    def layer(self, tokens, gate_weight, up_weight, down_weight, cotangent):
        gate, up, down = self.units(gate_weight.T), self.units(up_weight.T), self.units(down_weight)
        rows_in, rows_cot = self.gather(tokens), self.gather(cotangent)
        gate_sum = matmul(rows_in, gate, (1, 1))
        up_sum = matmul(rows_in, up, (1, 1))
        silu_g, hidden, rest = gated(gate_sum, up_sum)
        hidden = hidden.astype(BF16)
        grad_down = self.unit_sums(matmul(hidden, rows_cot, (0, 0)))
        back_sum = matmul(rows_cot, down, (1, 1))
        gate_act, up_act = (back_sum * rest).astype(BF16), (back_sum * silu_g).astype(BF16)
        grad_gate = self.unit_sums(matmul(gate_act, rows_in, (0, 0))).T
        grad_up = self.unit_sums(matmul(up_act, rows_in, (0, 0))).T
        output = self.scatter(matmul(hidden, down, (1, 0)), tokens.shape[0])
        partial = matmul(gate_act, gate, (1, 0)) + matmul(up_act, up, (1, 0))
        grad_tokens = self.scatter(partial, tokens.shape[0])
        return (output, grad_tokens, grad_gate, grad_up, grad_down)


def solution(mesh):
    square = mesh.shape["inp"] == 4 and mesh.shape["out"] == 2

    def on_device(tokens, *others):
        places = Square() if square and tokens.shape[0] == 2 else Plain()
        return places.layer(tokens, *others)

    rows_spec = P(None, ("inp", "wt"), "out")
    in_spec = P("out", ("wt", "inp"))
    down_spec = P(("wt", "inp"), "out")
    return jax.shard_map(
        on_device,
        mesh=mesh,
        in_specs=(rows_spec, in_spec, in_spec, down_spec, rows_spec),
        out_specs=(rows_spec, rows_spec, in_spec, in_spec, down_spec),
        check_vma=False,
    )
```

```python
import functools

import jax
import jax.numpy as jnp
from jax import lax
from jax.experimental import pallas as pl
from jax.experimental.pallas import tpu as pltpu
from jax.sharding import PartitionSpec as P

F32 = jnp.float32
BF16 = jnp.bfloat16
MIB = 1024 * 1024


def matmul(a, b, contract):
    return lax.dot_general(a, b, ((contract[:1], contract[1:]), ((), ())), preferred_element_type=F32)


def gated(gate_sum, up_sum):
    sigmoid_g = jax.nn.sigmoid(gate_sum)
    silu_g = gate_sum * sigmoid_g
    slope = sigmoid_g * (1.0 + gate_sum * (1.0 - sigmoid_g))
    return silu_g, silu_g * up_sum, up_sum * slope


def shape(*dims, dtype=BF16):
    return jax.ShapeDtypeStruct(dims, dtype)


def call(kernel, outs, flops, args, after=(), specs=None, scratch=(), limit=24):
    everything = [*args, *after]
    moved = sum(a.size * a.dtype.itemsize for a in args) + sum(o.size * o.dtype.itemsize for o in outs)
    specs = specs or [pl.BlockSpec(memory_space=pltpu.VMEM)] * len(args)

    def body(*refs):
        kernel(*refs[: len(args)], *refs[len(everything) :])

    return pl.pallas_call(
        body,
        out_shape=list(outs),
        in_specs=[*specs, *[pl.BlockSpec(memory_space=pl.ANY)] * len(after)],
        out_specs=[pl.BlockSpec(memory_space=pltpu.VMEM)] * len(outs),
        scratch_shapes=list(scratch),
        compiler_params=pltpu.CompilerParams(vmem_limit_bytes=limit * MIB),
        cost_estimate=pl.CostEstimate(flops=flops, bytes_accessed=moved, transcendentals=0),
    )(*everything)


ANY = pl.BlockSpec(memory_space=pl.ANY)
HBM = pl.BlockSpec(memory_space=pltpu.HBM)
VMEM = pl.BlockSpec(memory_space=pltpu.VMEM)
SMEM = pl.BlockSpec(memory_space=pltpu.SMEM)


class Rows:
    def __init__(self, pieces, blocks, step):
        self.pieces, self.blocks, self.step = pieces, blocks, step

    def read(self, refs, at, side):
        piece, first = self.blocks[at][side]
        return refs[piece].at[first : first + self.step]


def hidden_kernel(rows, width, *refs):
    count = len(rows.pieces)
    pieces, (own_ref, other_ref, hidden_ref, turned_ref, silu_ref, rest_ref) = refs[:count], refs[count:]
    groups = own_ref.shape[0] // (2 * width)
    for at in range(len(rows.blocks)):
        span = slice(at * rows.step, (at + 1) * rows.step)
        sums = matmul(rows.read(pieces, at, 0)[...], own_ref[...], (1, 1))
        sums = sums + matmul(rows.read(pieces, at, 1)[...], other_ref[...], (1, 1))
        for group in range(groups):
            low = 2 * group * width
            silu_g, hidden, rest = gated(sums[:, low : low + width], sums[:, low + width : low + 2 * width])
            cols = slice(group * width, (group + 1) * width)
            hidden_ref[span, cols] = hidden.astype(BF16)
            turned_ref[cols, span] = hidden.T.astype(BF16)
            silu_ref[span, cols] = silu_g.astype(BF16)
            rest_ref[span, cols] = rest.astype(BF16)


def grads_kernel(rows, width, *refs):
    count = len(rows.pieces)
    pieces, (down_ref, silu_ref, rest_ref, act_ref, turned_ref) = refs[:count], refs[count:]
    groups = down_ref.shape[0] // width
    half = down_ref.shape[1] // 2
    for at in range(len(rows.blocks)):
        span = slice(at * rows.step, (at + 1) * rows.step)
        back = matmul(rows.read(pieces, at, 0)[...], down_ref[:, :half], (1, 1))
        back = back + matmul(rows.read(pieces, at, 1)[...], down_ref[:, half:], (1, 1))
        for group in range(groups):
            cols = slice(group * width, (group + 1) * width)
            for part, factor in enumerate((rest_ref, silu_ref)):
                grad = back[:, cols] * factor[span, cols].astype(F32)
                low = (2 * group + part) * width
                act_ref[span, low : low + width] = grad.astype(BF16)
                turned_ref[low : low + width, span] = grad.T.astype(BF16)


def weight_kernel(rows, sides, tile, *refs):
    count = len(rows.pieces)
    pieces, (turned_ref, out_ref) = refs[:count], refs[count:]
    half = out_ref.shape[1] // len(sides)
    for place, side in enumerate(sides):

        @pl.loop(0, half // tile)
        def _(index):
            cols = pl.ds(pl.multiple_of(index * tile, tile), tile)
            total = jnp.zeros((out_ref.shape[0], tile), F32)
            for at in range(len(rows.blocks)):
                span = slice(at * rows.step, (at + 1) * rows.step)
                total = total + matmul(turned_ref[:, span], rows.read(pieces, at, side)[:, cols], (1, 0))
            out_ref[:, pl.ds(pl.multiple_of(place * half + index * tile, tile), tile)] = total.astype(BF16)


def block_kernel(first, places, sides, added, *refs):
    rights, many = len(sides), len(places)
    left_any, right_any, refs = refs[0], refs[1 : 1 + rights], refs[1 + rights :]
    adds, refs = refs[: many * added], refs[many * added :]
    outs, (left_ref, right_ref, sems) = refs[:many], refs[many:]
    depth, half = right_ref.shape[1:]
    copies = [pltpu.make_async_copy(left_any.at[pl.ds(first, left_ref.shape[0])], left_ref, sems.at[0])]
    for at, side in enumerate(sides):
        source = right_any[at].at[:, pl.ds(side * half, half)]
        copies.append(pltpu.make_async_copy(source, right_ref.at[at], sems.at[1 + at]))
    for copy in copies:
        copy.start()
    for copy in copies:
        copy.wait()
    for at, (row, right) in enumerate(places):
        total = matmul(left_ref[row : row + outs[at].shape[0]], right_ref[right], (1, 0))
        if added:
            total = total + adds[at][...].astype(F32)
        outs[at][...] = total.astype(BF16)


def copy_kernel(in_ref, out_ref):
    out_ref[...] = in_ref[...]


def sum_kernel(left_ref, right_ref, out_ref):
    out_ref[...] = (left_ref[...].astype(F32) + right_ref[...].astype(F32)).astype(BF16)


def finish_kernel(at_ref, mine_ref, theirs_ref, gate_ref, up_ref):
    width = mine_ref.shape[0] // 2
    for part, out_ref in enumerate((gate_ref, up_ref)):
        span = slice(part * width, (part + 1) * width)
        mine, theirs = mine_ref[span].astype(F32).T, theirs_ref[span].astype(F32).T
        first = at_ref[0] == 0
        out_ref[:, :width] = jnp.where(first, mine, theirs)
        out_ref[:, width:] = jnp.where(first, theirs, mine)


class Square:
    def core(self, array):
        return lax.ppermute(array, "inp", [(at, at ^ 1) for at in range(4)])

    def chip(self, array):
        return lax.ppermute(array, "inp", [(at, at ^ 2) for at in range(4)])

    def other(self, array):
        return lax.ppermute(array, "out", [(0, 1), (1, 0)])

    def unit_halves(self, weight):
        half = weight.shape[0] // 2
        at = lax.axis_index("out")
        return (
            lax.dynamic_slice_in_dim(weight, at * half, half, 0),
            lax.dynamic_slice_in_dim(weight, (1 - at) * half, half, 0),
        )

    def in_order(self, mine, theirs):
        mine, theirs = mine.astype(F32), theirs.astype(F32)
        first = lax.axis_index("out") == 0
        return jnp.where(first, jnp.concatenate([mine, theirs]), jnp.concatenate([theirs, mine]))

    def gather(self, array):
        step = array.shape[1]
        own = array.reshape(2 * step, array.shape[2])
        by_chip, by_other = self.chip(own), self.other(own)
        corner = [self.other(by_chip[:step]), self.chip(by_other[step:])]
        pieces = [own, by_other, by_chip] + corner
        pieces = pieces + [self.core(piece) for piece in pieces]
        blocks = []
        for base in (0, 5):
            blocks += [((base, 0), (base + 1, 0)), ((base, step), (base + 1, step))]
            blocks += [((base + 2, 0), (base + 3, 0)), ((base + 2, step), (base + 4, 0))]
        return Rows(pieces, blocks, step)

    def products(self, left, rights, places, adds=(), after=()):
        far = int(not adds)
        quarter, depth = left.shape[0] // 4, left.shape[1]
        half = rights[0][2]
        outs = [shape(quarter, half)] * len(places)
        use = sorted({other for _, other in places})
        chips = sorted({chip for chip, _ in places})
        first = 2 * far * quarter + chips[0] * quarter
        wanted = [((chip - chips[0]) * quarter, use.index(other)) for chip, other in places]
        args = [left] + [rights[other][0] for other in use] + [adds[place] for place in places if adds]
        blocks = call(
            functools.partial(block_kernel, first, wanted, [rights[other][1] for other in use], bool(adds)),
            outs,
            2 * len(places) * quarter * depth * half,
            args,
            after,
            specs=[ANY] * (1 + len(use)) + [VMEM] * (len(args) - 1 - len(use)),
            scratch=[
                pltpu.VMEM((len(chips) * quarter, depth), BF16),
                pltpu.VMEM((len(use), depth, half), BF16),
                pltpu.SemaphoreType.DMA((1 + len(use),)),
            ],
        )
        return dict(zip(places, blocks))

    def far_first(self, left, rights, after):
        return self.products(left, rights, [(1, 1)], after=after)

    def far_rest(self, left, rights, after):
        return self.products(left, rights, [(0, 1), (1, 0), (0, 0)], after=after)

    def near_first(self, left, rights, far, after):
        return self.products(left, rights, [(1, 1)], far, after)

    def near_rest(self, left, rights, far, after):
        return self.products(left, rights, [(0, 1), (1, 0), (0, 0)], far, after)

    def layer(self, tokens, gate_weight, up_weight, down_weight, cotangent):
        def gather_units(array):
            return lax.all_gather(array, "wt", axis=0, tiled=True)

        def scatter_units(array):
            return lax.psum_scatter(array, "wt", scatter_dimension=0, tiled=True)

        gate_mine, gate_theirs = self.unit_halves(gate_weight.T)
        up_mine, up_theirs = self.unit_halves(up_weight.T)
        down_mine, down_theirs = self.unit_halves(down_weight)
        width, half = gate_mine.shape
        own_units = gather_units(jnp.concatenate([gate_mine, up_mine]))
        other_units = gather_units(self.other(jnp.concatenate([gate_theirs, up_theirs])))
        down = gather_units(jnp.concatenate([down_mine, self.other(down_theirs)], axis=1))
        rows_in = self.gather(tokens)
        rows_cot = self.gather(cotangent)
        step = rows_in.step
        count = len(rows_in.blocks) * step
        units = down.shape[0]

        hidden, hidden_turned, silu, rest = call(
            functools.partial(hidden_kernel, rows_in, width),
            [shape(count, units), shape(units, count), shape(count, units), shape(count, units)],
            8 * count * units * half,
            [*rows_in.pieces, own_units, other_units],
            limit=44,
        )
        (down_term,) = call(
            functools.partial(weight_kernel, rows_cot, (0, 1), 256),
            [shape(units, 2 * half)],
            4 * count * units * half,
            [*rows_cot.pieces, hidden_turned],
            limit=44,
        )
        down_sum = scatter_units(down_term)
        down_sides = [(down, 0, half), (down, 1, half)]
        output_far = self.far_first(hidden, down_sides, [down_term])
        output_far |= self.far_rest(hidden, down_sides, [output_far[1, 1]])
        act, act_turned = call(
            functools.partial(grads_kernel, rows_cot, width),
            [shape(count, 2 * units), shape(2 * units, count)],
            4 * count * units * half,
            [*rows_cot.pieces, down, silu, rest],
            after=list(output_far.values()),
            limit=44,
        )

        def unit_term(side, after):
            return call(
                functools.partial(weight_kernel, rows_in, (side,), 256),
                [shape(2 * units, half)],
                4 * count * units * half,
                [*rows_in.pieces, act_turned],
                after,
                limit=44,
            )[0]

        output_far = {place: self.core(block) for place, block in output_far.items()}
        sums = self.near_first(hidden, down_sides, output_far, [act])
        corner = sums[1, 1]
        by_other, by_chip = self.other(corner[:step]), self.chip(corner[step:])
        sums |= self.near_rest(hidden, down_sides, output_far, [corner])
        other_term = unit_term(1, [sums[0, 0]])
        other_sum = scatter_units(call(copy_kernel, [shape(*other_term.shape)], 0, [other_term], [down_sum])[0])
        unit_sides = [(own_units, 0, half), (other_units, 0, half)]
        grads_far = self.far_first(act, unit_sides, [other_term, by_other, by_chip])
        grads_far |= self.far_rest(act, unit_sides, [grads_far[1, 1]])
        zeros = jnp.zeros((step, half), F32)
        to_chip = (sums[1, 0].astype(F32) + jnp.concatenate([by_other.astype(F32), zeros])).astype(BF16)
        to_other = (sums[0, 1].astype(F32) + jnp.concatenate([zeros, by_chip.astype(F32)])).astype(BF16)
        output_chip, output_other = self.chip(to_chip), self.other(to_other)
        own_term = unit_term(0, list(grads_far.values()))
        own_sum = scatter_units(call(copy_kernel, [shape(*own_term.shape)], 0, [own_term], [other_sum])[0])
        grads_far = {place: self.core(block) for place, block in grads_far.items()}
        grads = self.near_first(act, unit_sides, grads_far, [own_term])
        corner = self.chip(grads[1, 1])
        down_back = self.other(down_sum[:, half:])
        grads |= self.near_rest(act, unit_sides, grads_far, [grads[1, 1], output_chip, output_other])
        by_chip = self.chip(grads[1, 0])
        (to_other,) = call(sum_kernel, [shape(2 * step, half)], 0, [grads[0, 1], corner])
        by_other = self.other(to_other)
        total = sums[0, 0].astype(F32) + output_chip.astype(F32) + output_other.astype(F32)
        output = total.astype(BF16).reshape(2, step, half)
        units_back = self.other(other_sum)
        (partial,) = call(sum_kernel, [shape(2 * step, half)], 0, [grads[0, 0], by_chip], [down_back])
        (total,) = call(sum_kernel, [shape(2 * step, half)], 0, [partial, by_other], [units_back])
        grad_tokens = total.reshape(2, step, half)

        at_out = lax.axis_index("out").astype(jnp.int32).reshape(1)
        mine, theirs = down_sum[:, :half].astype(F32), down_back.astype(F32)
        first = at_out[0] == 0
        grad_down = jnp.where(first, jnp.concatenate([mine, theirs]), jnp.concatenate([theirs, mine]))
        grad_gate, grad_up = call(
            finish_kernel,
            [shape(half, 2 * width, dtype=F32)] * 2,
            0,
            [at_out, own_sum, units_back],
            [total],
            specs=[SMEM, VMEM, VMEM],
        )
        return (output, grad_tokens, grad_gate, grad_up, grad_down)


class Plain:
    def units(self, weight):
        own = lax.all_to_all(weight, "out", split_axis=0, concat_axis=1, tiled=True)
        return lax.all_gather(own, "wt", axis=0, tiled=True)

    def unit_sums(self, grad):
        own = lax.psum_scatter(grad.astype(BF16), "wt", scatter_dimension=0, tiled=True)
        return lax.all_to_all(own, "out", split_axis=1, concat_axis=0, tiled=True).astype(F32)

    def gather(self, array):
        array = lax.all_gather(lax.all_gather(array, "inp", axis=1, tiled=True), "out", axis=2, tiled=True)
        return array.reshape(-1, array.shape[2])

    def scatter(self, partial, batches):
        partial = partial.astype(BF16).reshape(batches, -1, partial.shape[1])
        partial = lax.psum_scatter(partial, "out", scatter_dimension=2, tiled=True)
        return lax.psum_scatter(partial, "inp", scatter_dimension=1, tiled=True)

    def layer(self, tokens, gate_weight, up_weight, down_weight, cotangent):
        gate, up, down = self.units(gate_weight.T), self.units(up_weight.T), self.units(down_weight)
        rows_in, rows_cot = self.gather(tokens), self.gather(cotangent)
        gate_sum = matmul(rows_in, gate, (1, 1))
        up_sum = matmul(rows_in, up, (1, 1))
        silu_g, hidden, rest = gated(gate_sum, up_sum)
        hidden = hidden.astype(BF16)
        grad_down = self.unit_sums(matmul(hidden, rows_cot, (0, 0)))
        back_sum = matmul(rows_cot, down, (1, 1))
        gate_act, up_act = (back_sum * rest).astype(BF16), (back_sum * silu_g).astype(BF16)
        grad_gate = self.unit_sums(matmul(gate_act, rows_in, (0, 0))).T
        grad_up = self.unit_sums(matmul(up_act, rows_in, (0, 0))).T
        output = self.scatter(matmul(hidden, down, (1, 0)), tokens.shape[0])
        partial = matmul(gate_act, gate, (1, 0)) + matmul(up_act, up, (1, 0))
        grad_tokens = self.scatter(partial, tokens.shape[0])
        return (output, grad_tokens, grad_gate, grad_up, grad_down)


def solution(mesh):
    square = mesh.shape["inp"] == 4 and mesh.shape["out"] == 2

    def on_device(tokens, *others):
        places = Square() if square and tokens.shape[0] == 2 else Plain()
        return places.layer(tokens, *others)

    rows_spec = P(None, ("inp", "wt"), "out")
    in_spec = P("out", ("wt", "inp"))
    down_spec = P(("wt", "inp"), "out")
    return jax.shard_map(
        on_device,
        mesh=mesh,
        in_specs=(rows_spec, in_spec, in_spec, down_spec, rows_spec),
        out_specs=(rows_spec, rows_spec, in_spec, in_spec, down_spec),
        check_vma=False,
    )
```

```python
import functools

import jax
import jax.numpy as jnp
from jax import lax
from jax.experimental import pallas as pl
from jax.experimental.pallas import tpu as pltpu
from jax.sharding import PartitionSpec as P

F32 = jnp.float32
BF16 = jnp.bfloat16
MIB = 1024 * 1024


def matmul(a, b, contract):
    return lax.dot_general(a, b, ((contract[:1], contract[1:]), ((), ())), preferred_element_type=F32)


def gated(gate_sum, up_sum):
    sigmoid_g = jax.nn.sigmoid(gate_sum)
    silu_g = gate_sum * sigmoid_g
    slope = sigmoid_g * (1.0 + gate_sum * (1.0 - sigmoid_g))
    return silu_g, silu_g * up_sum, up_sum * slope


def shape(*dims, dtype=BF16):
    return jax.ShapeDtypeStruct(dims, dtype)


def call(kernel, outs, flops, args, after=(), specs=None, scratch=(), limit=24):
    everything = [*args, *after]
    moved = sum(a.size * a.dtype.itemsize for a in args) + sum(o.size * o.dtype.itemsize for o in outs)
    specs = specs or [pl.BlockSpec(memory_space=pltpu.VMEM)] * len(args)

    def body(*refs):
        kernel(*refs[: len(args)], *refs[len(everything) :])

    return pl.pallas_call(
        body,
        out_shape=list(outs),
        in_specs=[*specs, *[pl.BlockSpec(memory_space=pl.ANY)] * len(after)],
        out_specs=[pl.BlockSpec(memory_space=pltpu.VMEM)] * len(outs),
        scratch_shapes=list(scratch),
        compiler_params=pltpu.CompilerParams(vmem_limit_bytes=limit * MIB),
        cost_estimate=pl.CostEstimate(flops=flops, bytes_accessed=moved, transcendentals=0),
    )(*everything)


ANY = pl.BlockSpec(memory_space=pl.ANY)
HBM = pl.BlockSpec(memory_space=pltpu.HBM)
VMEM = pl.BlockSpec(memory_space=pltpu.VMEM)
SMEM = pl.BlockSpec(memory_space=pltpu.SMEM)


class Rows:
    def __init__(self, pieces, blocks, step):
        self.pieces, self.blocks, self.step = pieces, blocks, step

    def read(self, refs, at, side):
        piece, first = self.blocks[at][side]
        return refs[piece].at[first : first + self.step]


def hidden_kernel(rows, width, *refs):
    count = len(rows.pieces)
    pieces, (own_ref, other_ref, hidden_ref, turned_ref, silu_ref, rest_ref) = refs[:count], refs[count:]
    groups = own_ref.shape[0] // (2 * width)
    for at in range(len(rows.blocks)):
        span = slice(at * rows.step, (at + 1) * rows.step)
        sums = matmul(rows.read(pieces, at, 0)[...], own_ref[...], (1, 1))
        sums = sums + matmul(rows.read(pieces, at, 1)[...], other_ref[...], (1, 1))
        for group in range(groups):
            low = 2 * group * width
            silu_g, hidden, rest = gated(sums[:, low : low + width], sums[:, low + width : low + 2 * width])
            cols = slice(group * width, (group + 1) * width)
            hidden_ref[span, cols] = hidden.astype(BF16)
            turned_ref[cols, span] = hidden.T.astype(BF16)
            silu_ref[span, cols] = silu_g.astype(BF16)
            rest_ref[span, cols] = rest.astype(BF16)


def grads_kernel(rows, width, *refs):
    count = len(rows.pieces)
    pieces, (down_ref, silu_ref, rest_ref, act_ref, turned_ref) = refs[:count], refs[count:]
    groups = down_ref.shape[0] // width
    half = down_ref.shape[1] // 2
    for at in range(len(rows.blocks)):
        span = slice(at * rows.step, (at + 1) * rows.step)
        back = matmul(rows.read(pieces, at, 0)[...], down_ref[:, :half], (1, 1))
        back = back + matmul(rows.read(pieces, at, 1)[...], down_ref[:, half:], (1, 1))
        for group in range(groups):
            cols = slice(group * width, (group + 1) * width)
            for part, factor in enumerate((rest_ref, silu_ref)):
                grad = back[:, cols] * factor[span, cols].astype(F32)
                low = (2 * group + part) * width
                act_ref[span, low : low + width] = grad.astype(BF16)
                turned_ref[low : low + width, span] = grad.T.astype(BF16)


def weight_kernel(rows, sides, tile, *refs):
    count = len(rows.pieces)
    pieces, (turned_ref, out_ref) = refs[:count], refs[count:]
    half = out_ref.shape[1] // len(sides)
    for place, side in enumerate(sides):

        @pl.loop(0, half // tile)
        def _(index):
            cols = pl.ds(pl.multiple_of(index * tile, tile), tile)
            total = jnp.zeros((out_ref.shape[0], tile), F32)
            for at in range(len(rows.blocks)):
                span = slice(at * rows.step, (at + 1) * rows.step)
                total = total + matmul(turned_ref[:, span], rows.read(pieces, at, side)[:, cols], (1, 0))
            out_ref[:, pl.ds(pl.multiple_of(place * half + index * tile, tile), tile)] = total.astype(BF16)


def block_kernel(first, places, sides, added, *refs):
    rights, many = len(sides), len(places)
    left_any, right_any, refs = refs[0], refs[1 : 1 + rights], refs[1 + rights :]
    adds, refs = refs[: many * added], refs[many * added :]
    outs, (left_ref, right_ref, sems) = refs[:many], refs[many:]
    depth, half = right_ref.shape[1:]
    copies = [pltpu.make_async_copy(left_any.at[pl.ds(first, left_ref.shape[0])], left_ref, sems.at[0])]
    for at, side in enumerate(sides):
        source = right_any[at].at[:, pl.ds(side * half, half)]
        copies.append(pltpu.make_async_copy(source, right_ref.at[at], sems.at[1 + at]))
    for copy in copies:
        copy.start()
    for copy in copies:
        copy.wait()
    for at, (row, right) in enumerate(places):
        total = matmul(left_ref[row : row + outs[at].shape[0]], right_ref[right], (1, 0))
        if added:
            total = total + adds[at][...].astype(F32)
        outs[at][...] = total.astype(BF16)


def copy_kernel(in_ref, out_ref):
    out_ref[...] = in_ref[...]


def sum_kernel(left_ref, right_ref, out_ref):
    out_ref[...] = (left_ref[...].astype(F32) + right_ref[...].astype(F32)).astype(BF16)


def finish_kernel(at_ref, mine_ref, theirs_ref, gate_ref, up_ref):
    width = mine_ref.shape[0] // 2
    for part, out_ref in enumerate((gate_ref, up_ref)):
        span = slice(part * width, (part + 1) * width)
        mine, theirs = mine_ref[span].astype(F32).T, theirs_ref[span].astype(F32).T
        first = at_ref[0] == 0
        out_ref[:, :width] = jnp.where(first, mine, theirs)
        out_ref[:, width:] = jnp.where(first, theirs, mine)


class Square:
    def core(self, array):
        return lax.ppermute(array, "inp", [(at, at ^ 1) for at in range(4)])

    def chip(self, array):
        return lax.ppermute(array, "inp", [(at, at ^ 2) for at in range(4)])

    def other(self, array):
        return lax.ppermute(array, "out", [(0, 1), (1, 0)])

    def unit_halves(self, weight):
        half = weight.shape[0] // 2
        at = lax.axis_index("out")
        return (
            lax.dynamic_slice_in_dim(weight, at * half, half, 0),
            lax.dynamic_slice_in_dim(weight, (1 - at) * half, half, 0),
        )

    def in_order(self, mine, theirs):
        mine, theirs = mine.astype(F32), theirs.astype(F32)
        first = lax.axis_index("out") == 0
        return jnp.where(first, jnp.concatenate([mine, theirs]), jnp.concatenate([theirs, mine]))

    def gather(self, array):
        step = array.shape[1]
        own = array.reshape(2 * step, array.shape[2])
        by_chip, by_other = self.chip(own), self.other(own)
        corner = [self.other(by_chip[:step]), self.chip(by_other[step:])]
        pieces = [own, by_other, by_chip] + corner
        pieces = pieces + [self.core(piece) for piece in pieces]
        blocks = []
        for base in (0, 5):
            blocks += [((base, 0), (base + 1, 0)), ((base, step), (base + 1, step))]
            blocks += [((base + 2, 0), (base + 3, 0)), ((base + 2, step), (base + 4, 0))]
        return Rows(pieces, blocks, step)

    def products(self, left, rights, places, adds=(), after=()):
        far = int(not adds)
        quarter, depth = left.shape[0] // 4, left.shape[1]
        half = rights[0][2]
        outs = [shape(quarter, half)] * len(places)
        use = sorted({other for _, other in places})
        chips = sorted({chip for chip, _ in places})
        first = 2 * far * quarter + chips[0] * quarter
        wanted = [((chip - chips[0]) * quarter, use.index(other)) for chip, other in places]
        args = [left] + [rights[other][0] for other in use] + [adds[place] for place in places if adds]
        blocks = call(
            functools.partial(block_kernel, first, wanted, [rights[other][1] for other in use], bool(adds)),
            outs,
            2 * len(places) * quarter * depth * half,
            args,
            after,
            specs=[ANY] * (1 + len(use)) + [VMEM] * (len(args) - 1 - len(use)),
            scratch=[
                pltpu.VMEM((len(chips) * quarter, depth), BF16),
                pltpu.VMEM((len(use), depth, half), BF16),
                pltpu.SemaphoreType.DMA((1 + len(use),)),
            ],
        )
        return dict(zip(places, blocks))

    def far_first(self, left, rights, after):
        return self.products(left, rights, [(1, 1)], after=after)

    def far_rest(self, left, rights, after):
        return self.products(left, rights, [(0, 1), (1, 0), (0, 0)], after=after)

    def near_first(self, left, rights, far, after):
        return self.products(left, rights, [(1, 1)], far, after)

    def near_rest(self, left, rights, far, after):
        return self.products(left, rights, [(0, 1), (1, 0), (0, 0)], far, after)

    def layer(self, tokens, gate_weight, up_weight, down_weight, cotangent):
        def gather_units(array):
            return lax.all_gather(array, "wt", axis=0, tiled=True)

        def scatter_units(array):
            return lax.psum_scatter(array, "wt", scatter_dimension=0, tiled=True)

        gate_mine, gate_theirs = self.unit_halves(gate_weight.T)
        up_mine, up_theirs = self.unit_halves(up_weight.T)
        down_mine, down_theirs = self.unit_halves(down_weight)
        width, half = gate_mine.shape
        own_units = gather_units(jnp.concatenate([gate_mine, up_mine]))
        other_units = gather_units(self.other(jnp.concatenate([gate_theirs, up_theirs])))
        down = gather_units(jnp.concatenate([down_mine, self.other(down_theirs)], axis=1))
        rows_in = self.gather(tokens)
        rows_cot = self.gather(cotangent)
        step = rows_in.step
        count = len(rows_in.blocks) * step
        units = down.shape[0]

        hidden, hidden_turned, silu, rest = call(
            functools.partial(hidden_kernel, rows_in, width),
            [shape(count, units), shape(units, count), shape(count, units), shape(count, units)],
            8 * count * units * half,
            [*rows_in.pieces, own_units, other_units],
            limit=44,
        )
        (down_term,) = call(
            functools.partial(weight_kernel, rows_cot, (0, 1), 256),
            [shape(units, 2 * half)],
            4 * count * units * half,
            [*rows_cot.pieces, hidden_turned],
            limit=44,
        )
        down_sum = scatter_units(down_term)
        down_sides = [(down, 0, half), (down, 1, half)]
        output_far = self.far_first(hidden, down_sides, [down_term])
        output_far |= self.far_rest(hidden, down_sides, [output_far[1, 1]])
        act, act_turned = call(
            functools.partial(grads_kernel, rows_cot, width),
            [shape(count, 2 * units), shape(2 * units, count)],
            4 * count * units * half,
            [*rows_cot.pieces, down, silu, rest],
            after=list(output_far.values()),
            limit=44,
        )

        def unit_term(side, after):
            return call(
                functools.partial(weight_kernel, rows_in, (side,), 256),
                [shape(2 * units, half)],
                4 * count * units * half,
                [*rows_in.pieces, act_turned],
                after,
                limit=44,
            )[0]

        output_far = {place: self.core(block) for place, block in output_far.items()}
        sums = self.near_first(hidden, down_sides, output_far, [act])
        corner = sums[1, 1]
        by_other, by_chip = self.other(corner[:step]), self.chip(corner[step:])
        sums |= self.near_rest(hidden, down_sides, output_far, [corner])
        other_term = unit_term(1, [sums[0, 0], by_other, by_chip])
        (term,) = call(copy_kernel, [shape(*other_term.shape)], 0, [other_term], [down_sum])
        other_sum = scatter_units(term)
        zeros = jnp.zeros((step, half), F32)

        def with_corner(sums, by_chip, by_other):
            to_chip = sums[1, 0].astype(F32) + jnp.concatenate([by_other.astype(F32), zeros])
            to_other = sums[0, 1].astype(F32) + jnp.concatenate([zeros, by_chip.astype(F32)])
            return self.chip(to_chip.astype(BF16)), self.other(to_other.astype(BF16))

        output_chip, output_other = with_corner(sums, by_chip, by_other)
        unit_sides = [(own_units, 0, half), (other_units, 0, half)]
        grads_far = self.far_first(act, unit_sides, [other_term])
        grads_far |= self.far_rest(act, unit_sides, [grads_far[1, 1]])
        grads_far = {place: self.core(block) for place, block in grads_far.items()}
        grads = self.near_first(act, unit_sides, grads_far, [])
        corner = grads[1, 1]
        by_other, by_chip = self.other(corner[:step]), self.chip(corner[step:])
        grads |= self.near_rest(act, unit_sides, grads_far, [corner])
        own_term = unit_term(0, [grads[0, 0], output_chip, output_other])
        down_back = self.other(down_sum[:, half:])
        waits = [other_sum, by_other, by_chip, down_back]
        (term,) = call(copy_kernel, [shape(*own_term.shape)], 0, [own_term], waits)
        own_sum = scatter_units(term)
        grads_chip, grads_other = with_corner(grads, by_chip, by_other)
        total = sums[0, 0].astype(F32) + output_chip.astype(F32) + output_other.astype(F32)
        output = total.astype(BF16).reshape(2, step, half)
        units_back = self.other(other_sum)
        (partial,) = call(sum_kernel, [shape(2 * step, half)], 0, [grads[0, 0], grads_chip])
        (total,) = call(sum_kernel, [shape(2 * step, half)], 0, [partial, grads_other], [units_back])
        grad_tokens = total.reshape(2, step, half)

        at_out = lax.axis_index("out").astype(jnp.int32).reshape(1)
        mine, theirs = down_sum[:, :half].astype(F32), down_back.astype(F32)
        first = at_out[0] == 0
        grad_down = jnp.where(first, jnp.concatenate([mine, theirs]), jnp.concatenate([theirs, mine]))
        grad_gate, grad_up = call(
            finish_kernel,
            [shape(half, 2 * width, dtype=F32)] * 2,
            0,
            [at_out, own_sum, units_back],
            [total],
            specs=[SMEM, VMEM, VMEM],
        )
        return (output, grad_tokens, grad_gate, grad_up, grad_down)


class Plain:
    def units(self, weight):
        own = lax.all_to_all(weight, "out", split_axis=0, concat_axis=1, tiled=True)
        return lax.all_gather(own, "wt", axis=0, tiled=True)

    def unit_sums(self, grad):
        own = lax.psum_scatter(grad.astype(BF16), "wt", scatter_dimension=0, tiled=True)
        return lax.all_to_all(own, "out", split_axis=1, concat_axis=0, tiled=True).astype(F32)

    def gather(self, array):
        array = lax.all_gather(lax.all_gather(array, "inp", axis=1, tiled=True), "out", axis=2, tiled=True)
        return array.reshape(-1, array.shape[2])

    def scatter(self, partial, batches):
        partial = partial.astype(BF16).reshape(batches, -1, partial.shape[1])
        partial = lax.psum_scatter(partial, "out", scatter_dimension=2, tiled=True)
        return lax.psum_scatter(partial, "inp", scatter_dimension=1, tiled=True)

    def layer(self, tokens, gate_weight, up_weight, down_weight, cotangent):
        gate, up, down = self.units(gate_weight.T), self.units(up_weight.T), self.units(down_weight)
        rows_in, rows_cot = self.gather(tokens), self.gather(cotangent)
        gate_sum = matmul(rows_in, gate, (1, 1))
        up_sum = matmul(rows_in, up, (1, 1))
        silu_g, hidden, rest = gated(gate_sum, up_sum)
        hidden = hidden.astype(BF16)
        grad_down = self.unit_sums(matmul(hidden, rows_cot, (0, 0)))
        back_sum = matmul(rows_cot, down, (1, 1))
        gate_act, up_act = (back_sum * rest).astype(BF16), (back_sum * silu_g).astype(BF16)
        grad_gate = self.unit_sums(matmul(gate_act, rows_in, (0, 0))).T
        grad_up = self.unit_sums(matmul(up_act, rows_in, (0, 0))).T
        output = self.scatter(matmul(hidden, down, (1, 0)), tokens.shape[0])
        partial = matmul(gate_act, gate, (1, 0)) + matmul(up_act, up, (1, 0))
        grad_tokens = self.scatter(partial, tokens.shape[0])
        return (output, grad_tokens, grad_gate, grad_up, grad_down)


def solution(mesh):
    square = mesh.shape["inp"] == 4 and mesh.shape["out"] == 2

    def on_device(tokens, *others):
        places = Square() if square and tokens.shape[0] == 2 else Plain()
        return places.layer(tokens, *others)

    rows_spec = P(None, ("inp", "wt"), "out")
    in_spec = P("out", ("wt", "inp"))
    down_spec = P(("wt", "inp"), "out")
    return jax.shard_map(
        on_device,
        mesh=mesh,
        in_specs=(rows_spec, in_spec, in_spec, down_spec, rows_spec),
        out_specs=(rows_spec, rows_spec, in_spec, in_spec, down_spec),
        check_vma=False,
    )
```

```python
import functools

import jax
import jax.numpy as jnp
from jax import lax
from jax.experimental import pallas as pl
from jax.experimental.pallas import tpu as pltpu
from jax.sharding import PartitionSpec as P

F32 = jnp.float32
BF16 = jnp.bfloat16
MIB = 1024 * 1024


def matmul(a, b, contract):
    return lax.dot_general(a, b, ((contract[:1], contract[1:]), ((), ())), preferred_element_type=F32)


def gated(gate_sum, up_sum):
    sigmoid_g = jax.nn.sigmoid(gate_sum)
    silu_g = gate_sum * sigmoid_g
    slope = sigmoid_g * (1.0 + gate_sum * (1.0 - sigmoid_g))
    return silu_g, silu_g * up_sum, up_sum * slope


def shape(*dims, dtype=BF16):
    return jax.ShapeDtypeStruct(dims, dtype)


def call(kernel, outs, flops, args, after=(), specs=None, scratch=(), limit=24):
    everything = [*args, *after]
    moved = sum(a.size * a.dtype.itemsize for a in args) + sum(o.size * o.dtype.itemsize for o in outs)
    specs = specs or [pl.BlockSpec(memory_space=pltpu.VMEM)] * len(args)

    def body(*refs):
        kernel(*refs[: len(args)], *refs[len(everything) :])

    return pl.pallas_call(
        body,
        out_shape=list(outs),
        in_specs=[*specs, *[pl.BlockSpec(memory_space=pl.ANY)] * len(after)],
        out_specs=[pl.BlockSpec(memory_space=pltpu.VMEM)] * len(outs),
        scratch_shapes=list(scratch),
        compiler_params=pltpu.CompilerParams(vmem_limit_bytes=limit * MIB),
        cost_estimate=pl.CostEstimate(flops=flops, bytes_accessed=moved, transcendentals=0),
    )(*everything)


ANY = pl.BlockSpec(memory_space=pl.ANY)
HBM = pl.BlockSpec(memory_space=pltpu.HBM)
VMEM = pl.BlockSpec(memory_space=pltpu.VMEM)
SMEM = pl.BlockSpec(memory_space=pltpu.SMEM)


class Rows:
    def __init__(self, pieces, blocks, step):
        self.pieces, self.blocks, self.step = pieces, blocks, step
        self.count, self.half = len(blocks) * step, pieces[0].shape[1]

    def copies(self, refs, sides, scratch, sems):
        found = []
        for at, pair in enumerate(self.blocks):
            found.append([])
            for place, side in enumerate(sides):
                piece, first = pair[side]
                into = scratch.at[pl.ds(at * self.step, self.step), pl.ds(place * self.half, self.half)]
                source = refs[piece].at[pl.ds(first, self.step)]
                found[-1].append(pltpu.make_async_copy(source, into, sems.at[at * len(sides) + place]))
        return found


def hidden_kernel(rows, width, *refs):
    count = len(rows.pieces)
    pieces = refs[:count]
    own_ref, other_ref, hidden_ref, turned_ref, silu_ref, rest_ref, in_ref, unit_ref, sems, unit_sems = refs[count:]
    half = rows.half
    loads = [
        pltpu.make_async_copy(own_ref, unit_ref.at[:, pl.ds(0, half)], unit_sems.at[0]),
        pltpu.make_async_copy(other_ref, unit_ref.at[:, pl.ds(half, half)], unit_sems.at[1]),
    ]
    copies = rows.copies(pieces, (0, 1), in_ref, sems)
    for copy in loads + [copy for block in copies for copy in block]:
        copy.start()
    for copy in loads:
        copy.wait()
    for pair in range(len(copies) // 2):
        for copy in copies[2 * pair] + copies[2 * pair + 1]:
            copy.wait()
        span = slice(2 * pair * rows.step, 2 * (pair + 1) * rows.step)

        @pl.loop(0, unit_ref.shape[0] // (2 * width))
        def _(group):
            units = pl.ds(pl.multiple_of(group * 2 * width, 2 * width), 2 * width)
            sums = matmul(in_ref[span], unit_ref[units], (1, 1))
            silu_g, hidden, rest = gated(sums[:, :width], sums[:, width:])
            cols = pl.ds(pl.multiple_of(group * width, width), width)
            hidden_ref[span, cols] = hidden.astype(BF16)
            turned_ref[cols, span] = hidden.T.astype(BF16)
            silu_ref[span, cols] = silu_g.astype(BF16)
            rest_ref[span, cols] = rest.astype(BF16)


def grads_kernel(rows, width, *refs):
    count = len(rows.pieces)
    pieces = refs[:count]
    down_ref, silu_ref, rest_ref, act_ref, turned_ref, cot_ref, sems = refs[count:]
    copies = rows.copies(pieces, (0, 1), cot_ref, sems)
    for copy in [copy for block in copies for copy in block]:
        copy.start()
    for pair in range(len(copies) // 2):
        for copy in copies[2 * pair] + copies[2 * pair + 1]:
            copy.wait()
        span = slice(2 * pair * rows.step, 2 * (pair + 1) * rows.step)

        @pl.loop(0, down_ref.shape[0] // (2 * width))
        def _(group):
            units = pl.ds(pl.multiple_of(group * 2 * width, 2 * width), 2 * width)
            back = matmul(cot_ref[span], down_ref[units], (1, 1))
            for part, factor in enumerate((rest_ref, silu_ref)):
                grads = back * factor[span, units].astype(F32)
                for side in range(2):
                    grad = grads[:, side * width : (side + 1) * width]
                    low = pl.ds(pl.multiple_of((4 * group + 2 * side + part) * width, width), width)
                    act_ref[span, low] = grad.astype(BF16)
                    turned_ref[low, span] = grad.T.astype(BF16)


def weight_kernel(rows, sides, tile, *refs):
    count = len(rows.pieces)
    pieces, (turned_ref, out_ref, rows_ref, sems) = refs[:count], refs[count:]
    copies = [copy for block in rows.copies(pieces, sides, rows_ref, sems) for copy in block]
    for copy in copies:
        copy.start()
    for copy in copies:
        copy.wait()

    @pl.loop(0, out_ref.shape[1] // tile)
    def _(index):
        cols = pl.ds(pl.multiple_of(index * tile, tile), tile)
        out_ref[:, cols] = matmul(turned_ref[...], rows_ref[:, cols], (1, 0)).astype(BF16)


def block_kernel(first, places, sides, added, *refs):
    rights, many = len(sides), len(places)
    left_any, right_any, refs = refs[0], refs[1 : 1 + rights], refs[1 + rights :]
    adds, refs = refs[: many * added], refs[many * added :]
    outs, (left_ref, right_ref, sems) = refs[:many], refs[many:]
    depth, half = right_ref.shape[1:]
    copies = [pltpu.make_async_copy(left_any.at[pl.ds(first, left_ref.shape[0])], left_ref, sems.at[0])]
    for at, side in enumerate(sides):
        source = right_any[at].at[:, pl.ds(side * half, half)]
        copies.append(pltpu.make_async_copy(source, right_ref.at[at], sems.at[1 + at]))
    for copy in copies:
        copy.start()
    for copy in copies:
        copy.wait()
    for at, (row, right) in enumerate(places):
        total = matmul(left_ref[row : row + outs[at].shape[0]], right_ref[right], (1, 0))
        if added:
            total = total + adds[at][...].astype(F32)
        outs[at][...] = total.astype(BF16)


def copy_kernel(in_ref, out_ref):
    out_ref[...] = in_ref[...]


def sum_kernel(left_ref, right_ref, out_ref):
    out_ref[...] = (left_ref[...].astype(F32) + right_ref[...].astype(F32)).astype(BF16)


def finish_kernel(at_ref, mine_ref, theirs_ref, gate_ref, up_ref):
    width = mine_ref.shape[0] // 2
    for part, out_ref in enumerate((gate_ref, up_ref)):
        span = slice(part * width, (part + 1) * width)
        mine, theirs = mine_ref[span].astype(F32).T, theirs_ref[span].astype(F32).T
        first = at_ref[0] == 0
        out_ref[:, :width] = jnp.where(first, mine, theirs)
        out_ref[:, width:] = jnp.where(first, theirs, mine)


class Square:
    def core(self, array):
        return lax.ppermute(array, "inp", [(at, at ^ 1) for at in range(4)])

    def chip(self, array):
        return lax.ppermute(array, "inp", [(at, at ^ 2) for at in range(4)])

    def other(self, array):
        return lax.ppermute(array, "out", [(0, 1), (1, 0)])

    def unit_halves(self, weight):
        half = weight.shape[0] // 2
        at = lax.axis_index("out")
        return (
            lax.dynamic_slice_in_dim(weight, at * half, half, 0),
            lax.dynamic_slice_in_dim(weight, (1 - at) * half, half, 0),
        )

    def in_order(self, mine, theirs):
        mine, theirs = mine.astype(F32), theirs.astype(F32)
        first = lax.axis_index("out") == 0
        return jnp.where(first, jnp.concatenate([mine, theirs]), jnp.concatenate([theirs, mine]))

    def gather(self, array):
        step = array.shape[1]
        own = array.reshape(2 * step, array.shape[2])
        by_chip, by_other = self.chip(own), self.other(own)
        corner = [self.other(by_chip[:step]), self.chip(by_other[step:])]
        pieces = [own, by_other, by_chip] + corner
        pieces = pieces + [self.core(piece) for piece in pieces]
        blocks = []
        for base in (0, 5):
            blocks += [((base, 0), (base + 1, 0)), ((base, step), (base + 1, step))]
            blocks += [((base + 2, 0), (base + 3, 0)), ((base + 2, step), (base + 4, 0))]
        return Rows(pieces, blocks, step)

    def products(self, left, rights, places, adds=(), after=()):
        far = int(not adds)
        quarter, depth = left.shape[0] // 4, left.shape[1]
        half = rights[0][2]
        outs = [shape(quarter, half)] * len(places)
        use = sorted({other for _, other in places})
        chips = sorted({chip for chip, _ in places})
        first = 2 * far * quarter + chips[0] * quarter
        wanted = [((chip - chips[0]) * quarter, use.index(other)) for chip, other in places]
        args = [left] + [rights[other][0] for other in use] + [adds[place] for place in places if adds]
        blocks = call(
            functools.partial(block_kernel, first, wanted, [rights[other][1] for other in use], bool(adds)),
            outs,
            2 * len(places) * quarter * depth * half,
            args,
            after,
            specs=[HBM] * (1 + len(use)) + [VMEM] * (len(args) - 1 - len(use)),
            scratch=[
                pltpu.VMEM((len(chips) * quarter, depth), BF16),
                pltpu.VMEM((len(use), depth, half), BF16),
                pltpu.SemaphoreType.DMA((1 + len(use),)),
            ],
        )
        return dict(zip(places, blocks))

    def far_first(self, left, rights, after):
        return self.products(left, rights, [(1, 1)], after=after)

    def far_rest(self, left, rights, after):
        return self.products(left, rights, [(0, 1), (1, 0), (0, 0)], after=after)

    def near_first(self, left, rights, far, after):
        return self.products(left, rights, [(1, 1)], far, after)

    def near_rest(self, left, rights, far, after):
        return self.products(left, rights, [(0, 1), (1, 0), (0, 0)], far, after)

    def layer(self, tokens, gate_weight, up_weight, down_weight, cotangent):
        def gather_units(array):
            return lax.all_gather(array, "wt", axis=0, tiled=True)

        def scatter_units(array):
            return lax.psum_scatter(array, "wt", scatter_dimension=0, tiled=True)

        gate_mine, gate_theirs = self.unit_halves(gate_weight.T)
        up_mine, up_theirs = self.unit_halves(up_weight.T)
        down_mine, down_theirs = self.unit_halves(down_weight)
        width, half = gate_mine.shape
        own_units = gather_units(jnp.concatenate([gate_mine, up_mine]))
        other_units = gather_units(self.other(jnp.concatenate([gate_theirs, up_theirs])))
        down = gather_units(jnp.concatenate([down_mine, self.other(down_theirs)], axis=1))
        rows_in = self.gather(tokens)
        rows_cot = self.gather(cotangent)
        step = rows_in.step
        count = len(rows_in.blocks) * step
        units = down.shape[0]
        loads = len(rows_in.blocks)
        both = pltpu.VMEM((count, 2 * half), BF16)

        hidden, hidden_turned, silu, rest = call(
            functools.partial(hidden_kernel, rows_in, width),
            [shape(count, units), shape(units, count), shape(count, units), shape(count, units)],
            8 * count * units * half,
            [*rows_in.pieces, own_units, other_units],
            specs=[HBM] * (len(rows_in.pieces) + 2),
            scratch=[
                both,
                pltpu.VMEM((2 * units, 2 * half), BF16),
                pltpu.SemaphoreType.DMA((2 * loads,)),
                pltpu.SemaphoreType.DMA((2,)),
            ],
            limit=32,
        )
        (down_term,) = call(
            functools.partial(weight_kernel, rows_cot, (0, 1), 256),
            [shape(units, 2 * half)],
            4 * count * units * half,
            [*rows_cot.pieces, hidden_turned],
            specs=[HBM] * len(rows_cot.pieces) + [VMEM],
            scratch=[both, pltpu.SemaphoreType.DMA((2 * loads,))],
            limit=20,
        )
        down_sum = scatter_units(down_term)
        down_sides = [(down, 0, half), (down, 1, half)]
        output_far = self.far_first(hidden, down_sides, [down_term])
        output_far |= self.far_rest(hidden, down_sides, [output_far[1, 1]])
        act, act_turned = call(
            functools.partial(grads_kernel, rows_cot, width),
            [shape(count, 2 * units), shape(2 * units, count)],
            4 * count * units * half,
            [*rows_cot.pieces, down, silu, rest],
            after=list(output_far.values()),
            specs=[HBM] * len(rows_cot.pieces) + [VMEM] * 3,
            scratch=[both, pltpu.SemaphoreType.DMA((2 * loads,))],
            limit=32,
        )

        def unit_term(side, after):
            return call(
                functools.partial(weight_kernel, rows_in, (side,), 256),
                [shape(2 * units, half)],
                4 * count * units * half,
                [*rows_in.pieces, act_turned],
                after,
                specs=[HBM] * len(rows_in.pieces) + [VMEM],
                scratch=[pltpu.VMEM((count, half), BF16), pltpu.SemaphoreType.DMA((loads,))],
                limit=20,
            )[0]

        output_far = {place: self.core(block) for place, block in output_far.items()}
        sums = self.near_first(hidden, down_sides, output_far, [act])
        corner = sums[1, 1]
        by_other, by_chip = self.other(corner[:step]), self.chip(corner[step:])
        sums |= self.near_rest(hidden, down_sides, output_far, [corner])
        other_term = unit_term(1, [sums[0, 0], by_other, by_chip])
        (term,) = call(copy_kernel, [shape(*other_term.shape)], 0, [other_term], [down_sum])
        other_sum = scatter_units(term)
        zeros = jnp.zeros((step, half), F32)

        def with_corner(sums, by_chip, by_other):
            to_chip = sums[1, 0].astype(F32) + jnp.concatenate([by_other.astype(F32), zeros])
            to_other = sums[0, 1].astype(F32) + jnp.concatenate([zeros, by_chip.astype(F32)])
            return self.chip(to_chip.astype(BF16)), self.other(to_other.astype(BF16))

        output_chip, output_other = with_corner(sums, by_chip, by_other)
        unit_sides = [(own_units, 0, half), (other_units, 0, half)]
        grads_far = self.far_first(act, unit_sides, [other_term])
        grads_far |= self.far_rest(act, unit_sides, [grads_far[1, 1]])
        grads_far = {place: self.core(block) for place, block in grads_far.items()}
        grads = self.near_first(act, unit_sides, grads_far, [output_chip, output_other])
        corner = grads[1, 1]
        by_other, by_chip = self.other(corner[:step]), self.chip(corner[step:])
        own_term = unit_term(0, [corner])
        grads |= self.near_rest(act, unit_sides, grads_far, [own_term])
        down_back = self.other(down_sum[:, half:])
        waits = [other_sum, by_other, by_chip, down_back, grads[0, 0]]
        (term,) = call(copy_kernel, [shape(*own_term.shape)], 0, [own_term], waits)
        own_sum = scatter_units(term)
        grads_chip, grads_other = with_corner(grads, by_chip, by_other)
        total = sums[0, 0].astype(F32) + output_chip.astype(F32) + output_other.astype(F32)
        output = total.astype(BF16).reshape(2, step, half)
        units_back = self.other(other_sum)
        (partial,) = call(sum_kernel, [shape(2 * step, half)], 0, [grads[0, 0], grads_chip])
        (total,) = call(sum_kernel, [shape(2 * step, half)], 0, [partial, grads_other], [units_back])
        grad_tokens = total.reshape(2, step, half)

        at_out = lax.axis_index("out").astype(jnp.int32).reshape(1)
        mine, theirs = down_sum[:, :half].astype(F32), down_back.astype(F32)
        first = at_out[0] == 0
        grad_down = jnp.where(first, jnp.concatenate([mine, theirs]), jnp.concatenate([theirs, mine]))
        grad_gate, grad_up = call(
            finish_kernel,
            [shape(half, 2 * width, dtype=F32)] * 2,
            0,
            [at_out, own_sum, units_back],
            [total],
            specs=[SMEM, VMEM, VMEM],
        )
        return (output, grad_tokens, grad_gate, grad_up, grad_down)


class Plain:
    def units(self, weight):
        own = lax.all_to_all(weight, "out", split_axis=0, concat_axis=1, tiled=True)
        return lax.all_gather(own, "wt", axis=0, tiled=True)

    def unit_sums(self, grad):
        own = lax.psum_scatter(grad.astype(BF16), "wt", scatter_dimension=0, tiled=True)
        return lax.all_to_all(own, "out", split_axis=1, concat_axis=0, tiled=True).astype(F32)

    def gather(self, array):
        array = lax.all_gather(lax.all_gather(array, "inp", axis=1, tiled=True), "out", axis=2, tiled=True)
        return array.reshape(-1, array.shape[2])

    def scatter(self, partial, batches):
        partial = partial.astype(BF16).reshape(batches, -1, partial.shape[1])
        partial = lax.psum_scatter(partial, "out", scatter_dimension=2, tiled=True)
        return lax.psum_scatter(partial, "inp", scatter_dimension=1, tiled=True)

    def layer(self, tokens, gate_weight, up_weight, down_weight, cotangent):
        gate, up, down = self.units(gate_weight.T), self.units(up_weight.T), self.units(down_weight)
        rows_in, rows_cot = self.gather(tokens), self.gather(cotangent)
        gate_sum = matmul(rows_in, gate, (1, 1))
        up_sum = matmul(rows_in, up, (1, 1))
        silu_g, hidden, rest = gated(gate_sum, up_sum)
        hidden = hidden.astype(BF16)
        grad_down = self.unit_sums(matmul(hidden, rows_cot, (0, 0)))
        back_sum = matmul(rows_cot, down, (1, 1))
        gate_act, up_act = (back_sum * rest).astype(BF16), (back_sum * silu_g).astype(BF16)
        grad_gate = self.unit_sums(matmul(gate_act, rows_in, (0, 0))).T
        grad_up = self.unit_sums(matmul(up_act, rows_in, (0, 0))).T
        output = self.scatter(matmul(hidden, down, (1, 0)), tokens.shape[0])
        partial = matmul(gate_act, gate, (1, 0)) + matmul(up_act, up, (1, 0))
        grad_tokens = self.scatter(partial, tokens.shape[0])
        return (output, grad_tokens, grad_gate, grad_up, grad_down)


def solution(mesh):
    square = mesh.shape["inp"] == 4 and mesh.shape["out"] == 2

    def on_device(tokens, *others):
        places = Square() if square and tokens.shape[0] == 2 else Plain()
        return places.layer(tokens, *others)

    rows_spec = P(None, ("inp", "wt"), "out")
    in_spec = P("out", ("wt", "inp"))
    down_spec = P(("wt", "inp"), "out")
    return jax.shard_map(
        on_device,
        mesh=mesh,
        in_specs=(rows_spec, in_spec, in_spec, down_spec, rows_spec),
        out_specs=(rows_spec, rows_spec, in_spec, in_spec, down_spec),
        check_vma=False,
    )
```

```python
import functools

import jax
import jax.numpy as jnp
from jax import lax
from jax.experimental import pallas as pl
from jax.experimental.pallas import tpu as pltpu
from jax.sharding import PartitionSpec as P

F32 = jnp.float32
BF16 = jnp.bfloat16
MIB = 1024 * 1024


def matmul(a, b, contract):
    return lax.dot_general(a, b, ((contract[:1], contract[1:]), ((), ())), preferred_element_type=F32)


def gated(gate_sum, up_sum):
    sigmoid_g = jax.nn.sigmoid(gate_sum)
    silu_g = gate_sum * sigmoid_g
    slope = sigmoid_g * (1.0 + gate_sum * (1.0 - sigmoid_g))
    return silu_g, silu_g * up_sum, up_sum * slope


def shape(*dims, dtype=BF16):
    return jax.ShapeDtypeStruct(dims, dtype)


def call(kernel, outs, flops, args, after=(), specs=None, scratch=(), limit=24, out=None):
    everything = [*args, *after]
    moved = sum(a.size * a.dtype.itemsize for a in args) + sum(o.size * o.dtype.itemsize for o in outs)
    specs = specs or [pl.BlockSpec(memory_space=pltpu.VMEM)] * len(args)

    def body(*refs):
        kernel(*refs[: len(args)], *refs[len(everything) :])

    return pl.pallas_call(
        body,
        out_shape=list(outs),
        in_specs=[*specs, *[pl.BlockSpec(memory_space=pl.ANY)] * len(after)],
        out_specs=[out or pl.BlockSpec(memory_space=pltpu.VMEM)] * len(outs),
        scratch_shapes=list(scratch),
        compiler_params=pltpu.CompilerParams(vmem_limit_bytes=limit * MIB),
        cost_estimate=pl.CostEstimate(flops=flops, bytes_accessed=moved, transcendentals=0),
    )(*everything)


ANY = pl.BlockSpec(memory_space=pl.ANY)
HBM = pl.BlockSpec(memory_space=pltpu.HBM)
VMEM = pl.BlockSpec(memory_space=pltpu.VMEM)
SMEM = pl.BlockSpec(memory_space=pltpu.SMEM)


def held(array, after):
    scratch = [pltpu.SemaphoreType.DMA]
    return call(copy_kernel, [shape(*array.shape)], 0, [array], after, specs=[HBM], scratch=scratch, out=HBM)[0]


class Rows:
    def __init__(self, pieces, blocks, step):
        self.pieces, self.blocks, self.step = pieces, blocks, step
        self.count, self.half = len(blocks) * step, pieces[0].shape[1]

    def copies(self, refs, sides, scratch, sems):
        found = []
        for at, pair in enumerate(self.blocks):
            found.append([])
            for place, side in enumerate(sides):
                piece, first = pair[side]
                into = scratch.at[pl.ds(at * self.step, self.step), pl.ds(place * self.half, self.half)]
                source = refs[piece].at[pl.ds(first, self.step)]
                found[-1].append(pltpu.make_async_copy(source, into, sems.at[at * len(sides) + place]))
        return found


def hidden_kernel(rows, width, *refs):
    count = len(rows.pieces)
    pieces = refs[:count]
    own_ref, other_ref, hidden_ref, turned_ref, silu_ref, rest_ref, in_ref, unit_ref, sems, unit_sems = refs[count:]
    half = rows.half
    loads = [
        pltpu.make_async_copy(own_ref, unit_ref.at[:, pl.ds(0, half)], unit_sems.at[0]),
        pltpu.make_async_copy(other_ref, unit_ref.at[:, pl.ds(half, half)], unit_sems.at[1]),
    ]
    copies = rows.copies(pieces, (0, 1), in_ref, sems)
    for copy in loads + [copy for block in copies for copy in block]:
        copy.start()
    for copy in loads:
        copy.wait()
    for pair in range(len(copies) // 2):
        for copy in copies[2 * pair] + copies[2 * pair + 1]:
            copy.wait()
        span = slice(2 * pair * rows.step, 2 * (pair + 1) * rows.step)

        @pl.loop(0, unit_ref.shape[0] // (2 * width))
        def _(group):
            units = pl.ds(pl.multiple_of(group * 2 * width, 2 * width), 2 * width)
            sums = matmul(in_ref[span], unit_ref[units], (1, 1))
            silu_g, hidden, rest = gated(sums[:, :width], sums[:, width:])
            cols = pl.ds(pl.multiple_of(group * width, width), width)
            hidden_ref[span, cols] = hidden.astype(BF16)
            turned_ref[cols, span] = hidden.T.astype(BF16)
            silu_ref[span, cols] = silu_g.astype(BF16)
            rest_ref[span, cols] = rest.astype(BF16)


def grads_kernel(rows, width, *refs):
    count = len(rows.pieces)
    pieces = refs[:count]
    down_ref, silu_ref, rest_ref, act_ref, turned_ref, cot_ref, sems = refs[count:]
    copies = rows.copies(pieces, (0, 1), cot_ref, sems)
    for copy in [copy for block in copies for copy in block]:
        copy.start()
    for pair in range(len(copies) // 2):
        for copy in copies[2 * pair] + copies[2 * pair + 1]:
            copy.wait()
        span = slice(2 * pair * rows.step, 2 * (pair + 1) * rows.step)

        @pl.loop(0, down_ref.shape[0] // (2 * width))
        def _(group):
            units = pl.ds(pl.multiple_of(group * 2 * width, 2 * width), 2 * width)
            back = matmul(cot_ref[span], down_ref[units], (1, 1))
            for part, factor in enumerate((rest_ref, silu_ref)):
                grads = back * factor[span, units].astype(F32)
                for side in range(2):
                    grad = grads[:, side * width : (side + 1) * width]
                    low = pl.ds(pl.multiple_of((4 * group + 2 * side + part) * width, width), width)
                    act_ref[span, low] = grad.astype(BF16)
                    turned_ref[low, span] = grad.T.astype(BF16)


def weight_kernel(rows, sides, tile, *refs):
    count = len(rows.pieces)
    pieces, (turned_ref, out_ref, rows_ref, sems) = refs[:count], refs[count:]
    copies = [copy for block in rows.copies(pieces, sides, rows_ref, sems) for copy in block]
    for copy in copies:
        copy.start()
    for copy in copies:
        copy.wait()

    @pl.loop(0, out_ref.shape[1] // tile)
    def _(index):
        cols = pl.ds(pl.multiple_of(index * tile, tile), tile)
        out_ref[:, cols] = matmul(turned_ref[...], rows_ref[:, cols], (1, 0)).astype(BF16)


def block_kernel(first, places, sides, added, *refs):
    rights, many = len(sides), len(places)
    left_any, right_any, refs = refs[0], refs[1 : 1 + rights], refs[1 + rights :]
    adds, refs = refs[: many * added], refs[many * added :]
    outs, (left_ref, right_ref, sems) = refs[:many], refs[many:]
    depth, half = right_ref.shape[1:]
    copies = [pltpu.make_async_copy(left_any.at[pl.ds(first, left_ref.shape[0])], left_ref, sems.at[0])]
    for at, side in enumerate(sides):
        source = right_any[at].at[:, pl.ds(side * half, half)]
        copies.append(pltpu.make_async_copy(source, right_ref.at[at], sems.at[1 + at]))
    for copy in copies:
        copy.start()
    for copy in copies:
        copy.wait()
    for at, (row, right) in enumerate(places):
        total = matmul(left_ref[row : row + outs[at].shape[0]], right_ref[right], (1, 0))
        if added:
            total = total + adds[at][...].astype(F32)
        outs[at][...] = total.astype(BF16)


def copy_kernel(in_ref, out_ref, sem):
    copy = pltpu.make_async_copy(in_ref, out_ref, sem)
    copy.start()
    copy.wait()


def sum_kernel(left_ref, right_ref, out_ref):
    out_ref[...] = (left_ref[...].astype(F32) + right_ref[...].astype(F32)).astype(BF16)


def finish_kernel(at_ref, mine_ref, theirs_ref, gate_ref, up_ref):
    width = mine_ref.shape[0] // 2
    for part, out_ref in enumerate((gate_ref, up_ref)):
        span = slice(part * width, (part + 1) * width)
        mine, theirs = mine_ref[span].astype(F32).T, theirs_ref[span].astype(F32).T
        first = at_ref[0] == 0
        out_ref[:, :width] = jnp.where(first, mine, theirs)
        out_ref[:, width:] = jnp.where(first, theirs, mine)


class Square:
    def core(self, array):
        return lax.ppermute(array, "inp", [(at, at ^ 1) for at in range(4)])

    def chip(self, array):
        return lax.ppermute(array, "inp", [(at, at ^ 2) for at in range(4)])

    def other(self, array):
        return lax.ppermute(array, "out", [(0, 1), (1, 0)])

    def unit_halves(self, weight):
        half = weight.shape[0] // 2
        at = lax.axis_index("out")
        return (
            lax.dynamic_slice_in_dim(weight, at * half, half, 0),
            lax.dynamic_slice_in_dim(weight, (1 - at) * half, half, 0),
        )

    def in_order(self, mine, theirs):
        mine, theirs = mine.astype(F32), theirs.astype(F32)
        first = lax.axis_index("out") == 0
        return jnp.where(first, jnp.concatenate([mine, theirs]), jnp.concatenate([theirs, mine]))

    def gather(self, array):
        step = array.shape[1]
        own = array.reshape(2 * step, array.shape[2])
        by_chip, by_other = self.chip(own), self.other(own)
        corner = [self.other(by_chip[:step]), self.chip(by_other[step:])]
        pieces = [own, by_other, by_chip] + corner
        pieces = pieces + [self.core(piece) for piece in pieces]
        blocks = []
        for base in (0, 5):
            blocks += [((base, 0), (base + 1, 0)), ((base, step), (base + 1, step))]
            blocks += [((base + 2, 0), (base + 3, 0)), ((base + 2, step), (base + 4, 0))]
        return Rows(pieces, blocks, step)

    def products(self, left, rights, places, adds=(), after=()):
        far = int(not adds)
        quarter, depth = left.shape[0] // 4, left.shape[1]
        half = rights[0][2]
        outs = [shape(quarter, half)] * len(places)
        use = sorted({other for _, other in places})
        chips = sorted({chip for chip, _ in places})
        first = 2 * far * quarter + chips[0] * quarter
        wanted = [((chip - chips[0]) * quarter, use.index(other)) for chip, other in places]
        args = [left] + [rights[other][0] for other in use] + [adds[place] for place in places if adds]
        blocks = call(
            functools.partial(block_kernel, first, wanted, [rights[other][1] for other in use], bool(adds)),
            outs,
            2 * len(places) * quarter * depth * half,
            args,
            after,
            specs=[HBM] * (1 + len(use)) + [VMEM] * (len(args) - 1 - len(use)),
            scratch=[
                pltpu.VMEM((len(chips) * quarter, depth), BF16),
                pltpu.VMEM((len(use), depth, half), BF16),
                pltpu.SemaphoreType.DMA((1 + len(use),)),
            ],
        )
        return dict(zip(places, blocks))

    def far_first(self, left, rights, after):
        return self.products(left, rights, [(1, 1)], after=after)

    def far_rest(self, left, rights, after):
        return self.products(left, rights, [(0, 1), (1, 0), (0, 0)], after=after)

    def near_first(self, left, rights, far, after):
        return self.products(left, rights, [(1, 1)], far, after)

    def near_rest(self, left, rights, far, after):
        return self.products(left, rights, [(0, 1), (1, 0), (0, 0)], far, after)

    def layer(self, tokens, gate_weight, up_weight, down_weight, cotangent):
        def gather_units(array):
            return lax.all_gather(array, "wt", axis=0, tiled=True)

        def scatter_units(array):
            return lax.psum_scatter(array, "wt", scatter_dimension=0, tiled=True)

        gate_mine, gate_theirs = self.unit_halves(gate_weight.T)
        up_mine, up_theirs = self.unit_halves(up_weight.T)
        down_mine, down_theirs = self.unit_halves(down_weight)
        width, half = gate_mine.shape
        own_units = gather_units(jnp.concatenate([gate_mine, up_mine]))
        other_units = gather_units(self.other(jnp.concatenate([gate_theirs, up_theirs])))
        down = gather_units(jnp.concatenate([down_mine, self.other(down_theirs)], axis=1))
        rows_in = self.gather(tokens)
        rows_cot = self.gather(cotangent)
        step = rows_in.step
        count = len(rows_in.blocks) * step
        units = down.shape[0]
        loads = len(rows_in.blocks)
        both = pltpu.VMEM((count, 2 * half), BF16)

        hidden, hidden_turned, silu, rest = call(
            functools.partial(hidden_kernel, rows_in, width),
            [shape(count, units), shape(units, count), shape(count, units), shape(count, units)],
            8 * count * units * half,
            [*rows_in.pieces, own_units, other_units],
            specs=[HBM] * (len(rows_in.pieces) + 2),
            scratch=[
                both,
                pltpu.VMEM((2 * units, 2 * half), BF16),
                pltpu.SemaphoreType.DMA((2 * loads,)),
                pltpu.SemaphoreType.DMA((2,)),
            ],
            limit=32,
        )
        (down_term,) = call(
            functools.partial(weight_kernel, rows_cot, (0, 1), 256),
            [shape(units, 2 * half)],
            4 * count * units * half,
            [*rows_cot.pieces, hidden_turned],
            specs=[HBM] * len(rows_cot.pieces) + [VMEM],
            scratch=[both, pltpu.SemaphoreType.DMA((2 * loads,))],
            limit=20,
        )
        down_sum = scatter_units(down_term)
        down_sides = [(down, 0, half), (down, 1, half)]
        output_far = self.far_first(hidden, down_sides, [down_term])
        output_far |= self.far_rest(hidden, down_sides, [output_far[1, 1]])
        act, act_turned = call(
            functools.partial(grads_kernel, rows_cot, width),
            [shape(count, 2 * units), shape(2 * units, count)],
            4 * count * units * half,
            [*rows_cot.pieces, down, silu, rest],
            after=list(output_far.values()),
            specs=[HBM] * len(rows_cot.pieces) + [VMEM] * 3,
            scratch=[both, pltpu.SemaphoreType.DMA((2 * loads,))],
            limit=32,
        )

        def unit_term(side, after):
            return call(
                functools.partial(weight_kernel, rows_in, (side,), 256),
                [shape(2 * units, half)],
                4 * count * units * half,
                [*rows_in.pieces, act_turned],
                after,
                specs=[HBM] * len(rows_in.pieces) + [VMEM],
                scratch=[pltpu.VMEM((count, half), BF16), pltpu.SemaphoreType.DMA((loads,))],
                limit=20,
            )[0]

        output_far = {place: self.core(block) for place, block in output_far.items()}
        sums = self.near_first(hidden, down_sides, output_far, [act])
        corner = sums[1, 1]
        by_other, by_chip = self.other(corner[:step]), self.chip(corner[step:])
        sums |= self.near_rest(hidden, down_sides, output_far, [corner])
        other_term = unit_term(1, [sums[0, 0], by_other, by_chip])
        other_sum = scatter_units(held(other_term, [down_sum]))
        zeros = jnp.zeros((step, half), F32)

        def with_corner(sums, by_chip, by_other):
            to_chip = sums[1, 0].astype(F32) + jnp.concatenate([by_other.astype(F32), zeros])
            to_other = sums[0, 1].astype(F32) + jnp.concatenate([zeros, by_chip.astype(F32)])
            return self.chip(to_chip.astype(BF16)), self.other(to_other.astype(BF16))

        output_chip, output_other = with_corner(sums, by_chip, by_other)
        unit_sides = [(own_units, 0, half), (other_units, 0, half)]
        grads_far = self.far_first(act, unit_sides, [other_term])
        own_term = unit_term(0, [grads_far[1, 1]])
        grads_far |= self.far_rest(act, unit_sides, [grads_far[1, 1], output_chip, output_other])
        grads_far = {place: self.core(block) for place, block in grads_far.items()}
        grads = self.near_first(act, unit_sides, grads_far, [own_term])
        corner = grads[1, 1]
        by_other, by_chip = self.other(corner[:step]), self.chip(corner[step:])
        grads |= self.near_rest(act, unit_sides, grads_far, [corner])
        down_back = self.other(down_sum[:, half:])
        own_sum = scatter_units(held(own_term, [other_sum, by_other, by_chip, down_back, grads[0, 0]]))
        grads_chip, grads_other = with_corner(grads, by_chip, by_other)
        total = sums[0, 0].astype(F32) + output_chip.astype(F32) + output_other.astype(F32)
        output = total.astype(BF16).reshape(2, step, half)
        units_back = self.other(other_sum)
        (partial,) = call(sum_kernel, [shape(2 * step, half)], 0, [grads[0, 0], grads_chip])
        (total,) = call(sum_kernel, [shape(2 * step, half)], 0, [partial, grads_other], [units_back])
        grad_tokens = total.reshape(2, step, half)

        at_out = lax.axis_index("out").astype(jnp.int32).reshape(1)
        mine, theirs = down_sum[:, :half].astype(F32), down_back.astype(F32)
        first = at_out[0] == 0
        grad_down = jnp.where(first, jnp.concatenate([mine, theirs]), jnp.concatenate([theirs, mine]))
        grad_gate, grad_up = call(
            finish_kernel,
            [shape(half, 2 * width, dtype=F32)] * 2,
            0,
            [at_out, own_sum, units_back],
            [total],
            specs=[SMEM, VMEM, VMEM],
        )
        return (output, grad_tokens, grad_gate, grad_up, grad_down)


class Plain:
    def units(self, weight):
        own = lax.all_to_all(weight, "out", split_axis=0, concat_axis=1, tiled=True)
        return lax.all_gather(own, "wt", axis=0, tiled=True)

    def unit_sums(self, grad):
        own = lax.psum_scatter(grad.astype(BF16), "wt", scatter_dimension=0, tiled=True)
        return lax.all_to_all(own, "out", split_axis=1, concat_axis=0, tiled=True).astype(F32)

    def gather(self, array):
        array = lax.all_gather(lax.all_gather(array, "inp", axis=1, tiled=True), "out", axis=2, tiled=True)
        return array.reshape(-1, array.shape[2])

    def scatter(self, partial, batches):
        partial = partial.astype(BF16).reshape(batches, -1, partial.shape[1])
        partial = lax.psum_scatter(partial, "out", scatter_dimension=2, tiled=True)
        return lax.psum_scatter(partial, "inp", scatter_dimension=1, tiled=True)

    def layer(self, tokens, gate_weight, up_weight, down_weight, cotangent):
        gate, up, down = self.units(gate_weight.T), self.units(up_weight.T), self.units(down_weight)
        rows_in, rows_cot = self.gather(tokens), self.gather(cotangent)
        gate_sum = matmul(rows_in, gate, (1, 1))
        up_sum = matmul(rows_in, up, (1, 1))
        silu_g, hidden, rest = gated(gate_sum, up_sum)
        hidden = hidden.astype(BF16)
        grad_down = self.unit_sums(matmul(hidden, rows_cot, (0, 0)))
        back_sum = matmul(rows_cot, down, (1, 1))
        gate_act, up_act = (back_sum * rest).astype(BF16), (back_sum * silu_g).astype(BF16)
        grad_gate = self.unit_sums(matmul(gate_act, rows_in, (0, 0))).T
        grad_up = self.unit_sums(matmul(up_act, rows_in, (0, 0))).T
        output = self.scatter(matmul(hidden, down, (1, 0)), tokens.shape[0])
        partial = matmul(gate_act, gate, (1, 0)) + matmul(up_act, up, (1, 0))
        grad_tokens = self.scatter(partial, tokens.shape[0])
        return (output, grad_tokens, grad_gate, grad_up, grad_down)


def solution(mesh):
    square = mesh.shape["inp"] == 4 and mesh.shape["out"] == 2

    def on_device(tokens, *others):
        places = Square() if square and tokens.shape[0] == 2 else Plain()
        return places.layer(tokens, *others)

    rows_spec = P(None, ("inp", "wt"), "out")
    in_spec = P("out", ("wt", "inp"))
    down_spec = P(("wt", "inp"), "out")
    return jax.shard_map(
        on_device,
        mesh=mesh,
        in_specs=(rows_spec, in_spec, in_spec, down_spec, rows_spec),
        out_specs=(rows_spec, rows_spec, in_spec, in_spec, down_spec),
        check_vma=False,
    )
```

```python
import functools

import jax
import jax.numpy as jnp
from jax import lax
from jax.experimental import pallas as pl
from jax.experimental.pallas import tpu as pltpu
from jax.sharding import PartitionSpec as P

F32 = jnp.float32
BF16 = jnp.bfloat16
MIB = 1024 * 1024


def matmul(a, b, contract):
    return lax.dot_general(a, b, ((contract[:1], contract[1:]), ((), ())), preferred_element_type=F32)


def gated(gate_sum, up_sum):
    sigmoid_g = jax.nn.sigmoid(gate_sum)
    silu_g = gate_sum * sigmoid_g
    slope = sigmoid_g * (1.0 + gate_sum * (1.0 - sigmoid_g))
    return silu_g, silu_g * up_sum, up_sum * slope


def call(kernel, outs, flops, *args):
    moved = sum(a.size * a.dtype.itemsize for a in args) + sum(o.size * o.dtype.itemsize for o in outs)
    return pl.pallas_call(
        kernel,
        out_shape=outs,
        in_specs=[pl.BlockSpec(memory_space=pltpu.VMEM)] * len(args),
        out_specs=[pl.BlockSpec(memory_space=pltpu.VMEM)] * len(outs),
        compiler_params=pltpu.CompilerParams(vmem_limit_bytes=44 * MIB),
        cost_estimate=pl.CostEstimate(flops=flops, bytes_accessed=moved, transcendentals=0),
    )(*args)


def shape(*dims):
    return jax.ShapeDtypeStruct(dims, BF16)


class Rows:
    def __init__(self, pieces, blocks, step):
        self.pieces, self.blocks, self.step = pieces, blocks, step

    def read(self, refs, at, side):
        piece, first = self.blocks[at][side]
        return refs[piece].at[first : first + self.step]


def hidden_kernel(rows, width, *refs):
    count = len(rows.pieces)
    pieces, (own_ref, other_ref, hidden_ref, turned_ref, silu_ref, rest_ref) = refs[:count], refs[count:]
    groups = own_ref.shape[0] // (2 * width)
    for at in range(len(rows.blocks)):
        span = slice(at * rows.step, (at + 1) * rows.step)
        sums = matmul(rows.read(pieces, at, 0)[...], own_ref[...], (1, 1))
        sums = sums + matmul(rows.read(pieces, at, 1)[...], other_ref[...], (1, 1))
        for group in range(groups):
            low = 2 * group * width
            silu_g, hidden, rest = gated(sums[:, low : low + width], sums[:, low + width : low + 2 * width])
            cols = slice(group * width, (group + 1) * width)
            hidden_ref[span, cols] = hidden.astype(BF16)
            turned_ref[cols, span] = hidden.T.astype(BF16)
            silu_ref[span, cols] = silu_g.astype(BF16)
            rest_ref[span, cols] = rest.astype(BF16)


def grads_kernel(rows, width, *refs):
    count = len(rows.pieces)
    pieces, (down_ref, silu_ref, rest_ref, act_ref, turned_ref) = refs[:count], refs[count:]
    groups = down_ref.shape[0] // width
    half = down_ref.shape[1] // 2
    for at in range(len(rows.blocks)):
        span = slice(at * rows.step, (at + 1) * rows.step)
        back = matmul(rows.read(pieces, at, 0)[...], down_ref[:, :half], (1, 1))
        back = back + matmul(rows.read(pieces, at, 1)[...], down_ref[:, half:], (1, 1))
        for group in range(groups):
            cols = slice(group * width, (group + 1) * width)
            for part, factor in enumerate((rest_ref, silu_ref)):
                grad = back[:, cols] * factor[span, cols].astype(F32)
                low = (2 * group + part) * width
                act_ref[span, low : low + width] = grad.astype(BF16)
                turned_ref[low : low + width, span] = grad.T.astype(BF16)


def weight_kernel(rows, sides, tile, *refs):
    count = len(rows.pieces)
    pieces, (turned_ref, out_ref) = refs[:count], refs[count:]
    half = out_ref.shape[1] // len(sides)
    for place, side in enumerate(sides):

        @pl.loop(0, half // tile)
        def _(index):
            cols = pl.ds(pl.multiple_of(index * tile, tile), tile)
            total = jnp.zeros((out_ref.shape[0], tile), F32)
            for at in range(len(rows.blocks)):
                span = slice(at * rows.step, (at + 1) * rows.step)
                total = total + matmul(turned_ref[:, span], rows.read(pieces, at, side)[:, cols], (1, 0))
            out_ref[:, pl.ds(pl.multiple_of(place * half + index * tile, tile), tile)] = total.astype(BF16)


def finish_kernel(at_ref, mine_ref, theirs_ref, gate_ref, up_ref):
    width = mine_ref.shape[0] // 2
    for part, out_ref in enumerate((gate_ref, up_ref)):
        span = slice(part * width, (part + 1) * width)
        mine, theirs = mine_ref[span].astype(F32).T, theirs_ref[span].astype(F32).T
        first = at_ref[0] == 0
        out_ref[:, :width] = jnp.where(first, mine, theirs)
        out_ref[:, width:] = jnp.where(first, theirs, mine)


class Square:
    def core(self, array):
        return lax.ppermute(array, "inp", [(at, at ^ 1) for at in range(4)])

    def chip(self, array):
        return lax.ppermute(array, "inp", [(at, at ^ 2) for at in range(4)])

    def other(self, array):
        return lax.ppermute(array, "out", [(0, 1), (1, 0)])

    def unit_halves(self, weight):
        half = weight.shape[0] // 2
        at = lax.axis_index("out")
        return (
            lax.dynamic_slice_in_dim(weight, at * half, half, 0),
            lax.dynamic_slice_in_dim(weight, (1 - at) * half, half, 0),
        )

    def in_order(self, mine, theirs):
        mine, theirs = mine.astype(F32), theirs.astype(F32)
        first = lax.axis_index("out") == 0
        return jnp.where(first, jnp.concatenate([mine, theirs]), jnp.concatenate([theirs, mine]))

    def gather(self, array):
        step = array.shape[1]
        own = array.reshape(2 * step, array.shape[2])
        by_chip, by_other = self.chip(own), self.other(own)
        corner = [self.other(by_chip[:step]), self.chip(by_other[step:])]
        pieces = [own, by_other, by_chip] + corner
        pieces = pieces + [self.core(piece) for piece in pieces]
        blocks = []
        for base in (0, 5):
            blocks += [((base, 0), (base + 1, 0)), ((base, step), (base + 1, step))]
            blocks += [((base + 2, 0), (base + 3, 0)), ((base + 2, step), (base + 4, 0))]
        return Rows(pieces, blocks, step)

    def scatter(self, product, rows, cols, split):
        half, quarter = rows // 2, rows // 4
        far = {}
        for chip in (1, 0):
            for other in (1, 0):
                at = slice(half + chip * quarter, half + (chip + 1) * quarter)
                far[chip, other] = self.core(product(at, other).astype(BF16))
        sums = {}
        for chip in (1, 0):
            for other in (1, 0):
                at = slice(chip * quarter, (chip + 1) * quarter)
                sums[chip, other] = product(at, other) + far[chip, other].astype(F32)
        batch = quarter // 2
        corner = sums[1, 1].astype(BF16)
        if split:
            from_other = self.other(corner[:batch]).astype(F32)
            from_chip = self.chip(corner[batch:]).astype(F32)
            zeros = jnp.zeros_like(from_other)
            to_chip = sums[1, 0] + jnp.concatenate([from_other, zeros])
            to_other = sums[0, 1] + jnp.concatenate([zeros, from_chip])
        else:
            to_chip = sums[1, 0]
            to_other = sums[0, 1] + self.chip(corner).astype(F32)
        total = sums[0, 0] + self.chip(to_chip.astype(BF16)).astype(F32) + self.other(to_other.astype(BF16)).astype(F32)
        return total.astype(BF16).reshape(2, batch, cols // 2)

    def layer(self, tokens, gate_weight, up_weight, down_weight, cotangent):
        def gather_units(array):
            return lax.all_gather(array, "wt", axis=0, tiled=True)

        def scatter_units(array):
            return lax.psum_scatter(array, "wt", scatter_dimension=0, tiled=True)

        gate_mine, gate_theirs = self.unit_halves(gate_weight.T)
        up_mine, up_theirs = self.unit_halves(up_weight.T)
        down_mine, down_theirs = self.unit_halves(down_weight)
        width, half = gate_mine.shape
        own_units = gather_units(jnp.concatenate([gate_mine, up_mine]))
        other_units = gather_units(self.other(jnp.concatenate([gate_theirs, up_theirs])))
        down = gather_units(jnp.concatenate([down_mine, self.other(down_theirs)], axis=1))
        rows_in = self.gather(tokens)
        rows_cot = self.gather(cotangent)
        count = len(rows_in.blocks) * rows_in.step
        units = down.shape[0]

        hidden, hidden_turned, silu, rest = call(
            functools.partial(hidden_kernel, rows_in, width),
            [shape(count, units), shape(units, count), shape(count, units), shape(count, units)],
            8 * count * units * half,
            *rows_in.pieces,
            own_units,
            other_units,
        )
        (down_term,) = call(
            functools.partial(weight_kernel, rows_cot, (0, 1), 256),
            [shape(units, 2 * half)],
            4 * count * units * half,
            *rows_cot.pieces,
            hidden_turned,
        )
        down_sum = scatter_units(down_term)
        act, act_turned = call(
            functools.partial(grads_kernel, rows_cot, width),
            [shape(count, 2 * units), shape(2 * units, count)],
            4 * count * units * half,
            *rows_cot.pieces,
            down,
            silu,
            rest,
        )
        terms = [
            call(
                functools.partial(weight_kernel, rows_in, (side,), 256),
                [shape(2 * units, half)],
                4 * count * units * half,
                *rows_in.pieces,
                act_turned,
            )[0]
            for side in (1, 0)
        ]
        other_sum, own_sum = scatter_units(terms[0]), scatter_units(terms[1])
        down_back = self.other(down_sum[:, half:])
        units_back = self.other(other_sum)
        grad_down = self.in_order(down_sum[:, :half], down_back)
        grad_gate, grad_up = pl.pallas_call(
            finish_kernel,
            out_shape=[jax.ShapeDtypeStruct((half, 2 * width), F32)] * 2,
            in_specs=[pl.BlockSpec(memory_space=pltpu.SMEM)] + [pl.BlockSpec(memory_space=pltpu.VMEM)] * 2,
            out_specs=[pl.BlockSpec(memory_space=pltpu.VMEM)] * 2,
            compiler_params=pltpu.CompilerParams(vmem_limit_bytes=16 * MIB),
            cost_estimate=pl.CostEstimate(flops=0, bytes_accessed=5 * MIB, transcendentals=0),
        )(lax.axis_index("out").astype(jnp.int32).reshape(1), own_sum, units_back)

        def output_block(at, other):
            return matmul(hidden[at], down[:, other * half : (other + 1) * half], (1, 0))

        def input_block(at, other):
            return matmul(act[at], other_units if other else own_units, (1, 0))

        output = self.scatter(output_block, count, 2 * half, True)
        grad_tokens = self.scatter(input_block, count, 2 * half, False)
        return (output, grad_tokens, grad_gate, grad_up, grad_down)


class Plain:
    def units(self, weight):
        own = lax.all_to_all(weight, "out", split_axis=0, concat_axis=1, tiled=True)
        return lax.all_gather(own, "wt", axis=0, tiled=True)

    def unit_sums(self, grad):
        own = lax.psum_scatter(grad.astype(BF16), "wt", scatter_dimension=0, tiled=True)
        return lax.all_to_all(own, "out", split_axis=1, concat_axis=0, tiled=True).astype(F32)

    def gather(self, array):
        array = lax.all_gather(lax.all_gather(array, "inp", axis=1, tiled=True), "out", axis=2, tiled=True)
        return array.reshape(-1, array.shape[2])

    def scatter(self, partial, batches):
        partial = partial.astype(BF16).reshape(batches, -1, partial.shape[1])
        partial = lax.psum_scatter(partial, "out", scatter_dimension=2, tiled=True)
        return lax.psum_scatter(partial, "inp", scatter_dimension=1, tiled=True)

    def layer(self, tokens, gate_weight, up_weight, down_weight, cotangent):
        gate, up, down = self.units(gate_weight.T), self.units(up_weight.T), self.units(down_weight)
        rows_in, rows_cot = self.gather(tokens), self.gather(cotangent)
        gate_sum = matmul(rows_in, gate, (1, 1))
        up_sum = matmul(rows_in, up, (1, 1))
        silu_g, hidden, rest = gated(gate_sum, up_sum)
        hidden = hidden.astype(BF16)
        grad_down = self.unit_sums(matmul(hidden, rows_cot, (0, 0)))
        back_sum = matmul(rows_cot, down, (1, 1))
        gate_act, up_act = (back_sum * rest).astype(BF16), (back_sum * silu_g).astype(BF16)
        grad_gate = self.unit_sums(matmul(gate_act, rows_in, (0, 0))).T
        grad_up = self.unit_sums(matmul(up_act, rows_in, (0, 0))).T
        output = self.scatter(matmul(hidden, down, (1, 0)), tokens.shape[0])
        partial = matmul(gate_act, gate, (1, 0)) + matmul(up_act, up, (1, 0))
        grad_tokens = self.scatter(partial, tokens.shape[0])
        return (output, grad_tokens, grad_gate, grad_up, grad_down)


def solution(mesh):
    square = mesh.shape["inp"] == 4 and mesh.shape["out"] == 2

    def on_device(tokens, *others):
        places = Square() if square and tokens.shape[0] == 2 else Plain()
        return places.layer(tokens, *others)

    rows_spec = P(None, ("inp", "wt"), "out")
    in_spec = P("out", ("wt", "inp"))
    down_spec = P(("wt", "inp"), "out")
    return jax.shard_map(
        on_device,
        mesh=mesh,
        in_specs=(rows_spec, in_spec, in_spec, down_spec, rows_spec),
        out_specs=(rows_spec, rows_spec, in_spec, in_spec, down_spec),
        check_vma=False,
    )
```

```python
import functools

import jax
import jax.numpy as jnp
from jax import lax
from jax.experimental import pallas as pl
from jax.experimental.pallas import tpu as pltpu
from jax.sharding import PartitionSpec as P

F32 = jnp.float32
BF16 = jnp.bfloat16
MIB = 1024 * 1024


def matmul(a, b, contract):
    return lax.dot_general(a, b, ((contract[:1], contract[1:]), ((), ())), preferred_element_type=F32)


def gated(gate_sum, up_sum):
    sigmoid_g = jax.nn.sigmoid(gate_sum)
    silu_g = gate_sum * sigmoid_g
    slope = sigmoid_g * (1.0 + gate_sum * (1.0 - sigmoid_g))
    return silu_g, silu_g * up_sum, up_sum * slope


def call(kernel, outs, flops, *args):
    moved = sum(a.size * a.dtype.itemsize for a in args) + sum(o.size * o.dtype.itemsize for o in outs)
    return pl.pallas_call(
        kernel,
        out_shape=outs,
        in_specs=[pl.BlockSpec(memory_space=pltpu.VMEM)] * len(args),
        out_specs=[pl.BlockSpec(memory_space=pltpu.VMEM)] * len(outs),
        compiler_params=pltpu.CompilerParams(vmem_limit_bytes=44 * MIB),
        cost_estimate=pl.CostEstimate(flops=flops, bytes_accessed=moved, transcendentals=0),
    )(*args)


def shape(*dims):
    return jax.ShapeDtypeStruct(dims, BF16)


def run(kernel, outs, flops, args, after=(), specs=None, scratch=(), limit=24):
    everything = [*args, *after]
    moved = sum(a.size * a.dtype.itemsize for a in args) + sum(o.size * o.dtype.itemsize for o in outs)
    specs = specs or [pl.BlockSpec(memory_space=pltpu.VMEM)] * len(args)

    def body(*refs):
        kernel(*refs[: len(args)], *refs[len(everything) :])

    return pl.pallas_call(
        body,
        out_shape=list(outs),
        in_specs=[*specs, *[pl.BlockSpec(memory_space=pl.ANY)] * len(after)],
        out_specs=[pl.BlockSpec(memory_space=pltpu.VMEM)] * len(outs),
        scratch_shapes=list(scratch),
        compiler_params=pltpu.CompilerParams(vmem_limit_bytes=limit * MIB),
        cost_estimate=pl.CostEstimate(flops=flops, bytes_accessed=moved, transcendentals=0),
    )(*everything)


ANY = pl.BlockSpec(memory_space=pl.ANY)
VMEM = pl.BlockSpec(memory_space=pltpu.VMEM)


class Rows:
    def __init__(self, pieces, blocks, step):
        self.pieces, self.blocks, self.step = pieces, blocks, step

    def read(self, refs, at, side):
        piece, first = self.blocks[at][side]
        return refs[piece].at[first : first + self.step]


def hidden_kernel(rows, width, *refs):
    count = len(rows.pieces)
    pieces, (own_ref, other_ref, hidden_ref, turned_ref, silu_ref, rest_ref) = refs[:count], refs[count:]
    groups = own_ref.shape[0] // (2 * width)
    for at in range(len(rows.blocks)):
        span = slice(at * rows.step, (at + 1) * rows.step)
        sums = matmul(rows.read(pieces, at, 0)[...], own_ref[...], (1, 1))
        sums = sums + matmul(rows.read(pieces, at, 1)[...], other_ref[...], (1, 1))
        for group in range(groups):
            low = 2 * group * width
            silu_g, hidden, rest = gated(sums[:, low : low + width], sums[:, low + width : low + 2 * width])
            cols = slice(group * width, (group + 1) * width)
            hidden_ref[span, cols] = hidden.astype(BF16)
            turned_ref[cols, span] = hidden.T.astype(BF16)
            silu_ref[span, cols] = silu_g.astype(BF16)
            rest_ref[span, cols] = rest.astype(BF16)


def grads_kernel(rows, width, *refs):
    count = len(rows.pieces)
    pieces, (down_ref, silu_ref, rest_ref, act_ref, turned_ref) = refs[:count], refs[count:]
    groups = down_ref.shape[0] // width
    half = down_ref.shape[1] // 2
    for at in range(len(rows.blocks)):
        span = slice(at * rows.step, (at + 1) * rows.step)
        back = matmul(rows.read(pieces, at, 0)[...], down_ref[:, :half], (1, 1))
        back = back + matmul(rows.read(pieces, at, 1)[...], down_ref[:, half:], (1, 1))
        for group in range(groups):
            cols = slice(group * width, (group + 1) * width)
            for part, factor in enumerate((rest_ref, silu_ref)):
                grad = back[:, cols] * factor[span, cols].astype(F32)
                low = (2 * group + part) * width
                act_ref[span, low : low + width] = grad.astype(BF16)
                turned_ref[low : low + width, span] = grad.T.astype(BF16)


def weight_kernel(rows, sides, tile, *refs):
    count = len(rows.pieces)
    pieces, (turned_ref, out_ref) = refs[:count], refs[count:]
    half = out_ref.shape[1] // len(sides)
    for place, side in enumerate(sides):

        @pl.loop(0, half // tile)
        def _(index):
            cols = pl.ds(pl.multiple_of(index * tile, tile), tile)
            total = jnp.zeros((out_ref.shape[0], tile), F32)
            for at in range(len(rows.blocks)):
                span = slice(at * rows.step, (at + 1) * rows.step)
                total = total + matmul(turned_ref[:, span], rows.read(pieces, at, side)[:, cols], (1, 0))
            out_ref[:, pl.ds(pl.multiple_of(place * half + index * tile, tile), tile)] = total.astype(BF16)


def block_kernel(first, places, sides, added, *refs):
    rights, many = len(sides), len(places)
    left_any, right_any, refs = refs[0], refs[1 : 1 + rights], refs[1 + rights :]
    adds, refs = refs[: many * added], refs[many * added :]
    outs, (left_ref, right_ref, sems) = refs[:many], refs[many:]
    depth, half = right_ref.shape[1:]
    copies = [pltpu.make_async_copy(left_any.at[pl.ds(first, left_ref.shape[0])], left_ref, sems.at[0])]
    for at, side in enumerate(sides):
        source = right_any[at].at[:, pl.ds(side * half, half)]
        copies.append(pltpu.make_async_copy(source, right_ref.at[at], sems.at[1 + at]))
    for copy in copies:
        copy.start()
    for copy in copies:
        copy.wait()
    for at, (row, right) in enumerate(places):
        total = matmul(left_ref[row : row + outs[at].shape[0]], right_ref[right], (1, 0))
        if added:
            total = total + adds[at][...].astype(F32)
        outs[at][...] = total.astype(BF16)


def finish_kernel(at_ref, mine_ref, theirs_ref, gate_ref, up_ref):
    width = mine_ref.shape[0] // 2
    for part, out_ref in enumerate((gate_ref, up_ref)):
        span = slice(part * width, (part + 1) * width)
        mine, theirs = mine_ref[span].astype(F32).T, theirs_ref[span].astype(F32).T
        first = at_ref[0] == 0
        out_ref[:, :width] = jnp.where(first, mine, theirs)
        out_ref[:, width:] = jnp.where(first, theirs, mine)


class Square:
    def core(self, array):
        return lax.ppermute(array, "inp", [(at, at ^ 1) for at in range(4)])

    def chip(self, array):
        return lax.ppermute(array, "inp", [(at, at ^ 2) for at in range(4)])

    def other(self, array):
        return lax.ppermute(array, "out", [(0, 1), (1, 0)])

    def unit_halves(self, weight):
        half = weight.shape[0] // 2
        at = lax.axis_index("out")
        return (
            lax.dynamic_slice_in_dim(weight, at * half, half, 0),
            lax.dynamic_slice_in_dim(weight, (1 - at) * half, half, 0),
        )

    def in_order(self, mine, theirs):
        mine, theirs = mine.astype(F32), theirs.astype(F32)
        first = lax.axis_index("out") == 0
        return jnp.where(first, jnp.concatenate([mine, theirs]), jnp.concatenate([theirs, mine]))

    def gather(self, array):
        step = array.shape[1]
        own = array.reshape(2 * step, array.shape[2])
        by_chip, by_other = self.chip(own), self.other(own)
        corner = [self.other(by_chip[:step]), self.chip(by_other[step:])]
        pieces = [own, by_other, by_chip] + corner
        pieces = pieces + [self.core(piece) for piece in pieces]
        blocks = []
        for base in (0, 5):
            blocks += [((base, 0), (base + 1, 0)), ((base, step), (base + 1, step))]
            blocks += [((base + 2, 0), (base + 3, 0)), ((base + 2, step), (base + 4, 0))]
        return Rows(pieces, blocks, step)

    def products(self, left, rights, places, adds=(), after=()):
        far = int(not adds)
        quarter, depth = left.shape[0] // 4, left.shape[1]
        half = rights[0][2]
        outs = [shape(quarter, half)] * len(places)
        use = sorted({other for _, other in places})
        chips = sorted({chip for chip, _ in places})
        first = 2 * far * quarter + chips[0] * quarter
        wanted = [((chip - chips[0]) * quarter, use.index(other)) for chip, other in places]
        args = [left] + [rights[other][0] for other in use] + [adds[place] for place in places if adds]
        blocks = run(
            functools.partial(block_kernel, first, wanted, [rights[other][1] for other in use], bool(adds)),
            outs,
            2 * len(places) * quarter * depth * half,
            args,
            after,
            specs=[ANY] * (1 + len(use)) + [VMEM] * (len(args) - 1 - len(use)),
            scratch=[
                pltpu.VMEM((len(chips) * quarter, depth), BF16),
                pltpu.VMEM((len(use), depth, half), BF16),
                pltpu.SemaphoreType.DMA((1 + len(use),)),
            ],
        )
        return dict(zip(places, blocks))

    def scatter(self, product, rows, cols, split, far=None):
        half, quarter = rows // 2, rows // 4
        if far is None:
            far = {}
            for chip in (1, 0):
                for other in (1, 0):
                    at = slice(half + chip * quarter, half + (chip + 1) * quarter)
                    far[chip, other] = product(at, other).astype(BF16)
        far = {place: self.core(block) for place, block in far.items()}
        sums = {}
        for chip in (1, 0):
            for other in (1, 0):
                at = slice(chip * quarter, (chip + 1) * quarter)
                sums[chip, other] = product(at, other) + far[chip, other].astype(F32)
        batch = quarter // 2
        corner = sums[1, 1].astype(BF16)
        if split:
            from_other = self.other(corner[:batch]).astype(F32)
            from_chip = self.chip(corner[batch:]).astype(F32)
            zeros = jnp.zeros_like(from_other)
            to_chip = sums[1, 0] + jnp.concatenate([from_other, zeros])
            to_other = sums[0, 1] + jnp.concatenate([zeros, from_chip])
        else:
            to_chip = sums[1, 0]
            to_other = sums[0, 1] + self.chip(corner).astype(F32)
        total = sums[0, 0] + self.chip(to_chip.astype(BF16)).astype(F32) + self.other(to_other.astype(BF16)).astype(F32)
        return total.astype(BF16).reshape(2, batch, cols // 2)

    def layer(self, tokens, gate_weight, up_weight, down_weight, cotangent):
        def gather_units(array):
            return lax.all_gather(array, "wt", axis=0, tiled=True)

        def scatter_units(array):
            return lax.psum_scatter(array, "wt", scatter_dimension=0, tiled=True)

        gate_mine, gate_theirs = self.unit_halves(gate_weight.T)
        up_mine, up_theirs = self.unit_halves(up_weight.T)
        down_mine, down_theirs = self.unit_halves(down_weight)
        width, half = gate_mine.shape
        own_units = gather_units(jnp.concatenate([gate_mine, up_mine]))
        other_units = gather_units(self.other(jnp.concatenate([gate_theirs, up_theirs])))
        down = gather_units(jnp.concatenate([down_mine, self.other(down_theirs)], axis=1))
        rows_in = self.gather(tokens)
        rows_cot = self.gather(cotangent)
        count = len(rows_in.blocks) * rows_in.step
        units = down.shape[0]

        hidden, hidden_turned, silu, rest = call(
            functools.partial(hidden_kernel, rows_in, width),
            [shape(count, units), shape(units, count), shape(count, units), shape(count, units)],
            8 * count * units * half,
            *rows_in.pieces,
            own_units,
            other_units,
        )
        (down_term,) = call(
            functools.partial(weight_kernel, rows_cot, (0, 1), 256),
            [shape(units, 2 * half)],
            4 * count * units * half,
            *rows_cot.pieces,
            hidden_turned,
        )
        down_sum = scatter_units(down_term)
        down_sides = [(down, 0, half), (down, 1, half)]
        far = self.products(hidden, down_sides, [(1, 1)], after=[down_term])
        far |= self.products(hidden, down_sides, [(0, 1), (1, 0), (0, 0)], after=[far[1, 1]])
        act, act_turned = run(
            functools.partial(grads_kernel, rows_cot, width),
            [shape(count, 2 * units), shape(2 * units, count)],
            4 * count * units * half,
            [*rows_cot.pieces, down, silu, rest],
            after=list(far.values()),
            limit=44,
        )
        terms = [
            run(
                functools.partial(weight_kernel, rows_in, (side,), 256),
                [shape(2 * units, half)],
                4 * count * units * half,
                [*rows_in.pieces, act_turned],
                after=after,
                limit=44,
            )[0]
            for side, after in ((1, []), (0, [down_sum]))
        ]
        other_sum, own_sum = scatter_units(terms[0]), scatter_units(terms[1])
        down_back = self.other(down_sum[:, half:])
        units_back = self.other(other_sum)
        grad_down = self.in_order(down_sum[:, :half], down_back)
        grad_gate, grad_up = pl.pallas_call(
            finish_kernel,
            out_shape=[jax.ShapeDtypeStruct((half, 2 * width), F32)] * 2,
            in_specs=[pl.BlockSpec(memory_space=pltpu.SMEM)] + [pl.BlockSpec(memory_space=pltpu.VMEM)] * 2,
            out_specs=[pl.BlockSpec(memory_space=pltpu.VMEM)] * 2,
            compiler_params=pltpu.CompilerParams(vmem_limit_bytes=16 * MIB),
            cost_estimate=pl.CostEstimate(flops=0, bytes_accessed=5 * MIB, transcendentals=0),
        )(lax.axis_index("out").astype(jnp.int32).reshape(1), own_sum, units_back)

        def output_block(at, other):
            return matmul(hidden[at], down[:, other * half : (other + 1) * half], (1, 0))

        def input_block(at, other):
            return matmul(act[at], other_units if other else own_units, (1, 0))

        output = self.scatter(output_block, count, 2 * half, True, far)
        grad_tokens = self.scatter(input_block, count, 2 * half, False)
        return (output, grad_tokens, grad_gate, grad_up, grad_down)


class Plain:
    def units(self, weight):
        own = lax.all_to_all(weight, "out", split_axis=0, concat_axis=1, tiled=True)
        return lax.all_gather(own, "wt", axis=0, tiled=True)

    def unit_sums(self, grad):
        own = lax.psum_scatter(grad.astype(BF16), "wt", scatter_dimension=0, tiled=True)
        return lax.all_to_all(own, "out", split_axis=1, concat_axis=0, tiled=True).astype(F32)

    def gather(self, array):
        array = lax.all_gather(lax.all_gather(array, "inp", axis=1, tiled=True), "out", axis=2, tiled=True)
        return array.reshape(-1, array.shape[2])

    def scatter(self, partial, batches):
        partial = partial.astype(BF16).reshape(batches, -1, partial.shape[1])
        partial = lax.psum_scatter(partial, "out", scatter_dimension=2, tiled=True)
        return lax.psum_scatter(partial, "inp", scatter_dimension=1, tiled=True)

    def layer(self, tokens, gate_weight, up_weight, down_weight, cotangent):
        gate, up, down = self.units(gate_weight.T), self.units(up_weight.T), self.units(down_weight)
        rows_in, rows_cot = self.gather(tokens), self.gather(cotangent)
        gate_sum = matmul(rows_in, gate, (1, 1))
        up_sum = matmul(rows_in, up, (1, 1))
        silu_g, hidden, rest = gated(gate_sum, up_sum)
        hidden = hidden.astype(BF16)
        grad_down = self.unit_sums(matmul(hidden, rows_cot, (0, 0)))
        back_sum = matmul(rows_cot, down, (1, 1))
        gate_act, up_act = (back_sum * rest).astype(BF16), (back_sum * silu_g).astype(BF16)
        grad_gate = self.unit_sums(matmul(gate_act, rows_in, (0, 0))).T
        grad_up = self.unit_sums(matmul(up_act, rows_in, (0, 0))).T
        output = self.scatter(matmul(hidden, down, (1, 0)), tokens.shape[0])
        partial = matmul(gate_act, gate, (1, 0)) + matmul(up_act, up, (1, 0))
        grad_tokens = self.scatter(partial, tokens.shape[0])
        return (output, grad_tokens, grad_gate, grad_up, grad_down)


def solution(mesh):
    square = mesh.shape["inp"] == 4 and mesh.shape["out"] == 2

    def on_device(tokens, *others):
        places = Square() if square and tokens.shape[0] == 2 else Plain()
        return places.layer(tokens, *others)

    rows_spec = P(None, ("inp", "wt"), "out")
    in_spec = P("out", ("wt", "inp"))
    down_spec = P(("wt", "inp"), "out")
    return jax.shard_map(
        on_device,
        mesh=mesh,
        in_specs=(rows_spec, in_spec, in_spec, down_spec, rows_spec),
        out_specs=(rows_spec, rows_spec, in_spec, in_spec, down_spec),
        check_vma=False,
    )
```

```python
import functools

import jax
import jax.numpy as jnp
from jax import lax
from jax.experimental import pallas as pl
from jax.experimental.pallas import tpu as pltpu
from jax.sharding import PartitionSpec as P

F32 = jnp.float32
BF16 = jnp.bfloat16
MIB = 1024 * 1024


def matmul(a, b, contract):
    return lax.dot_general(a, b, ((contract[:1], contract[1:]), ((), ())), preferred_element_type=F32)


def gated(gate_sum, up_sum):
    sigmoid_g = jax.nn.sigmoid(gate_sum)
    silu_g = gate_sum * sigmoid_g
    slope = sigmoid_g * (1.0 + gate_sum * (1.0 - sigmoid_g))
    return silu_g, silu_g * up_sum, up_sum * slope


def call(kernel, outs, flops, *args):
    moved = sum(a.size * a.dtype.itemsize for a in args) + sum(o.size * o.dtype.itemsize for o in outs)
    return pl.pallas_call(
        kernel,
        out_shape=outs,
        in_specs=[pl.BlockSpec(memory_space=pltpu.VMEM)] * len(args),
        out_specs=[pl.BlockSpec(memory_space=pltpu.VMEM)] * len(outs),
        compiler_params=pltpu.CompilerParams(vmem_limit_bytes=44 * MIB),
        cost_estimate=pl.CostEstimate(flops=flops, bytes_accessed=moved, transcendentals=0),
    )(*args)


def shape(*dims):
    return jax.ShapeDtypeStruct(dims, BF16)


def run(kernel, outs, flops, args, after=(), specs=None, scratch=(), limit=24):
    everything = [*args, *after]
    moved = sum(a.size * a.dtype.itemsize for a in args) + sum(o.size * o.dtype.itemsize for o in outs)
    specs = specs or [pl.BlockSpec(memory_space=pltpu.VMEM)] * len(args)

    def body(*refs):
        kernel(*refs[: len(args)], *refs[len(everything) :])

    return pl.pallas_call(
        body,
        out_shape=list(outs),
        in_specs=[*specs, *[pl.BlockSpec(memory_space=pl.ANY)] * len(after)],
        out_specs=[pl.BlockSpec(memory_space=pltpu.VMEM)] * len(outs),
        scratch_shapes=list(scratch),
        compiler_params=pltpu.CompilerParams(vmem_limit_bytes=limit * MIB),
        cost_estimate=pl.CostEstimate(flops=flops, bytes_accessed=moved, transcendentals=0),
    )(*everything)


class Rows:
    def __init__(self, pieces, blocks, step):
        self.pieces, self.blocks, self.step = pieces, blocks, step

    def read(self, refs, at, side):
        piece, first = self.blocks[at][side]
        return refs[piece].at[first : first + self.step]


def hidden_kernel(rows, width, *refs):
    count = len(rows.pieces)
    pieces, (own_ref, other_ref, hidden_ref, turned_ref, silu_ref, rest_ref) = refs[:count], refs[count:]
    groups = own_ref.shape[0] // (2 * width)
    for at in range(len(rows.blocks)):
        span = slice(at * rows.step, (at + 1) * rows.step)
        sums = matmul(rows.read(pieces, at, 0)[...], own_ref[...], (1, 1))
        sums = sums + matmul(rows.read(pieces, at, 1)[...], other_ref[...], (1, 1))
        for group in range(groups):
            low = 2 * group * width
            silu_g, hidden, rest = gated(sums[:, low : low + width], sums[:, low + width : low + 2 * width])
            cols = slice(group * width, (group + 1) * width)
            hidden_ref[span, cols] = hidden.astype(BF16)
            turned_ref[cols, span] = hidden.T.astype(BF16)
            silu_ref[span, cols] = silu_g.astype(BF16)
            rest_ref[span, cols] = rest.astype(BF16)


def grads_kernel(rows, width, *refs):
    count = len(rows.pieces)
    pieces, (down_ref, silu_ref, rest_ref, act_ref, turned_ref) = refs[:count], refs[count:]
    groups = down_ref.shape[0] // width
    half = down_ref.shape[1] // 2
    for at in range(len(rows.blocks)):
        span = slice(at * rows.step, (at + 1) * rows.step)
        back = matmul(rows.read(pieces, at, 0)[...], down_ref[:, :half], (1, 1))
        back = back + matmul(rows.read(pieces, at, 1)[...], down_ref[:, half:], (1, 1))
        for group in range(groups):
            cols = slice(group * width, (group + 1) * width)
            for part, factor in enumerate((rest_ref, silu_ref)):
                grad = back[:, cols] * factor[span, cols].astype(F32)
                low = (2 * group + part) * width
                act_ref[span, low : low + width] = grad.astype(BF16)
                turned_ref[low : low + width, span] = grad.T.astype(BF16)


def weight_kernel(rows, sides, tile, *refs):
    count = len(rows.pieces)
    pieces, (turned_ref, out_ref) = refs[:count], refs[count:]
    half = out_ref.shape[1] // len(sides)
    for place, side in enumerate(sides):

        @pl.loop(0, half // tile)
        def _(index):
            cols = pl.ds(pl.multiple_of(index * tile, tile), tile)
            total = jnp.zeros((out_ref.shape[0], tile), F32)
            for at in range(len(rows.blocks)):
                span = slice(at * rows.step, (at + 1) * rows.step)
                total = total + matmul(turned_ref[:, span], rows.read(pieces, at, side)[:, cols], (1, 0))
            out_ref[:, pl.ds(pl.multiple_of(place * half + index * tile, tile), tile)] = total.astype(BF16)


def finish_kernel(at_ref, mine_ref, theirs_ref, gate_ref, up_ref):
    width = mine_ref.shape[0] // 2
    for part, out_ref in enumerate((gate_ref, up_ref)):
        span = slice(part * width, (part + 1) * width)
        mine, theirs = mine_ref[span].astype(F32).T, theirs_ref[span].astype(F32).T
        first = at_ref[0] == 0
        out_ref[:, :width] = jnp.where(first, mine, theirs)
        out_ref[:, width:] = jnp.where(first, theirs, mine)


class Square:
    def core(self, array):
        return lax.ppermute(array, "inp", [(at, at ^ 1) for at in range(4)])

    def chip(self, array):
        return lax.ppermute(array, "inp", [(at, at ^ 2) for at in range(4)])

    def other(self, array):
        return lax.ppermute(array, "out", [(0, 1), (1, 0)])

    def unit_halves(self, weight):
        half = weight.shape[0] // 2
        at = lax.axis_index("out")
        return (
            lax.dynamic_slice_in_dim(weight, at * half, half, 0),
            lax.dynamic_slice_in_dim(weight, (1 - at) * half, half, 0),
        )

    def in_order(self, mine, theirs):
        mine, theirs = mine.astype(F32), theirs.astype(F32)
        first = lax.axis_index("out") == 0
        return jnp.where(first, jnp.concatenate([mine, theirs]), jnp.concatenate([theirs, mine]))

    def gather(self, array):
        step = array.shape[1]
        own = array.reshape(2 * step, array.shape[2])
        by_chip, by_other = self.chip(own), self.other(own)
        corner = [self.other(by_chip[:step]), self.chip(by_other[step:])]
        pieces = [own, by_other, by_chip] + corner
        pieces = pieces + [self.core(piece) for piece in pieces]
        blocks = []
        for base in (0, 5):
            blocks += [((base, 0), (base + 1, 0)), ((base, step), (base + 1, step))]
            blocks += [((base + 2, 0), (base + 3, 0)), ((base + 2, step), (base + 4, 0))]
        return Rows(pieces, blocks, step)

    def scatter(self, product, rows, cols, split):
        half, quarter = rows // 2, rows // 4
        far = {}
        for chip in (1, 0):
            for other in (1, 0):
                at = slice(half + chip * quarter, half + (chip + 1) * quarter)
                far[chip, other] = self.core(product(at, other).astype(BF16))
        sums = {}
        for chip in (1, 0):
            for other in (1, 0):
                at = slice(chip * quarter, (chip + 1) * quarter)
                sums[chip, other] = product(at, other) + far[chip, other].astype(F32)
        batch = quarter // 2
        corner = sums[1, 1].astype(BF16)
        if split:
            self.came = [self.other(corner[:batch]), self.chip(corner[batch:])]
            from_other, from_chip = [piece.astype(F32) for piece in self.came]
            zeros = jnp.zeros_like(from_other)
            to_chip = sums[1, 0] + jnp.concatenate([from_other, zeros])
            to_other = sums[0, 1] + jnp.concatenate([zeros, from_chip])
        else:
            to_chip = sums[1, 0]
            to_other = sums[0, 1] + self.chip(corner).astype(F32)
        total = sums[0, 0] + self.chip(to_chip.astype(BF16)).astype(F32) + self.other(to_other.astype(BF16)).astype(F32)
        return total.astype(BF16).reshape(2, batch, cols // 2)

    def layer(self, tokens, gate_weight, up_weight, down_weight, cotangent):
        def gather_units(array):
            return lax.all_gather(array, "wt", axis=0, tiled=True)

        def scatter_units(array):
            return lax.psum_scatter(array, "wt", scatter_dimension=0, tiled=True)

        gate_mine, gate_theirs = self.unit_halves(gate_weight.T)
        up_mine, up_theirs = self.unit_halves(up_weight.T)
        down_mine, down_theirs = self.unit_halves(down_weight)
        width, half = gate_mine.shape
        own_units = gather_units(jnp.concatenate([gate_mine, up_mine]))
        other_units = gather_units(self.other(jnp.concatenate([gate_theirs, up_theirs])))
        down = gather_units(jnp.concatenate([down_mine, self.other(down_theirs)], axis=1))
        rows_in = self.gather(tokens)
        rows_cot = self.gather(cotangent)
        count = len(rows_in.blocks) * rows_in.step
        units = down.shape[0]

        hidden, hidden_turned, silu, rest = call(
            functools.partial(hidden_kernel, rows_in, width),
            [shape(count, units), shape(units, count), shape(count, units), shape(count, units)],
            8 * count * units * half,
            *rows_in.pieces,
            own_units,
            other_units,
        )
        (down_term,) = call(
            functools.partial(weight_kernel, rows_cot, (0, 1), 256),
            [shape(units, 2 * half)],
            4 * count * units * half,
            *rows_cot.pieces,
            hidden_turned,
        )
        down_sum = scatter_units(down_term)
        act, act_turned = run(
            functools.partial(grads_kernel, rows_cot, width),
            [shape(count, 2 * units), shape(2 * units, count)],
            4 * count * units * half,
            [*rows_cot.pieces, down, silu, rest],
            limit=44,
        )
        def output_block(at, other):
            return matmul(hidden[at], down[:, other * half : (other + 1) * half], (1, 0))

        output = self.scatter(output_block, count, 2 * half, True)
        terms = [
            run(
                functools.partial(weight_kernel, rows_in, (side,), 256),
                [shape(2 * units, half)],
                4 * count * units * half,
                [*rows_in.pieces, act_turned],
                after=after,
                limit=44,
            )[0]
            for side, after in ((1, []), (0, self.came))
        ]
        other_sum, own_sum = scatter_units(terms[0]), scatter_units(terms[1])
        down_back = self.other(down_sum[:, half:])
        units_back = self.other(other_sum)
        grad_down = self.in_order(down_sum[:, :half], down_back)
        grad_gate, grad_up = pl.pallas_call(
            finish_kernel,
            out_shape=[jax.ShapeDtypeStruct((half, 2 * width), F32)] * 2,
            in_specs=[pl.BlockSpec(memory_space=pltpu.SMEM)] + [pl.BlockSpec(memory_space=pltpu.VMEM)] * 2,
            out_specs=[pl.BlockSpec(memory_space=pltpu.VMEM)] * 2,
            compiler_params=pltpu.CompilerParams(vmem_limit_bytes=16 * MIB),
            cost_estimate=pl.CostEstimate(flops=0, bytes_accessed=5 * MIB, transcendentals=0),
        )(lax.axis_index("out").astype(jnp.int32).reshape(1), own_sum, units_back)

        def input_block(at, other):
            return matmul(act[at], other_units if other else own_units, (1, 0))

        grad_tokens = self.scatter(input_block, count, 2 * half, False)
        return (output, grad_tokens, grad_gate, grad_up, grad_down)


class Plain:
    def units(self, weight):
        own = lax.all_to_all(weight, "out", split_axis=0, concat_axis=1, tiled=True)
        return lax.all_gather(own, "wt", axis=0, tiled=True)

    def unit_sums(self, grad):
        own = lax.psum_scatter(grad.astype(BF16), "wt", scatter_dimension=0, tiled=True)
        return lax.all_to_all(own, "out", split_axis=1, concat_axis=0, tiled=True).astype(F32)

    def gather(self, array):
        array = lax.all_gather(lax.all_gather(array, "inp", axis=1, tiled=True), "out", axis=2, tiled=True)
        return array.reshape(-1, array.shape[2])

    def scatter(self, partial, batches):
        partial = partial.astype(BF16).reshape(batches, -1, partial.shape[1])
        partial = lax.psum_scatter(partial, "out", scatter_dimension=2, tiled=True)
        return lax.psum_scatter(partial, "inp", scatter_dimension=1, tiled=True)

    def layer(self, tokens, gate_weight, up_weight, down_weight, cotangent):
        gate, up, down = self.units(gate_weight.T), self.units(up_weight.T), self.units(down_weight)
        rows_in, rows_cot = self.gather(tokens), self.gather(cotangent)
        gate_sum = matmul(rows_in, gate, (1, 1))
        up_sum = matmul(rows_in, up, (1, 1))
        silu_g, hidden, rest = gated(gate_sum, up_sum)
        hidden = hidden.astype(BF16)
        grad_down = self.unit_sums(matmul(hidden, rows_cot, (0, 0)))
        back_sum = matmul(rows_cot, down, (1, 1))
        gate_act, up_act = (back_sum * rest).astype(BF16), (back_sum * silu_g).astype(BF16)
        grad_gate = self.unit_sums(matmul(gate_act, rows_in, (0, 0))).T
        grad_up = self.unit_sums(matmul(up_act, rows_in, (0, 0))).T
        output = self.scatter(matmul(hidden, down, (1, 0)), tokens.shape[0])
        partial = matmul(gate_act, gate, (1, 0)) + matmul(up_act, up, (1, 0))
        grad_tokens = self.scatter(partial, tokens.shape[0])
        return (output, grad_tokens, grad_gate, grad_up, grad_down)


def solution(mesh):
    square = mesh.shape["inp"] == 4 and mesh.shape["out"] == 2

    def on_device(tokens, *others):
        places = Square() if square and tokens.shape[0] == 2 else Plain()
        return places.layer(tokens, *others)

    rows_spec = P(None, ("inp", "wt"), "out")
    in_spec = P("out", ("wt", "inp"))
    down_spec = P(("wt", "inp"), "out")
    return jax.shard_map(
        on_device,
        mesh=mesh,
        in_specs=(rows_spec, in_spec, in_spec, down_spec, rows_spec),
        out_specs=(rows_spec, rows_spec, in_spec, in_spec, down_spec),
        check_vma=False,
    )
```

```python
import functools

import jax
import jax.numpy as jnp
from jax import lax
from jax.experimental import pallas as pl
from jax.experimental.pallas import tpu as pltpu
from jax.sharding import PartitionSpec as P

F32 = jnp.float32
BF16 = jnp.bfloat16
MIB = 1024 * 1024


def matmul(a, b, contract):
    return lax.dot_general(a, b, ((contract[:1], contract[1:]), ((), ())), preferred_element_type=F32)


def gated(gate_sum, up_sum):
    sigmoid_g = jax.nn.sigmoid(gate_sum)
    silu_g = gate_sum * sigmoid_g
    slope = sigmoid_g * (1.0 + gate_sum * (1.0 - sigmoid_g))
    return silu_g, silu_g * up_sum, up_sum * slope


def call(kernel, outs, flops, *args):
    moved = sum(a.size * a.dtype.itemsize for a in args) + sum(o.size * o.dtype.itemsize for o in outs)
    return pl.pallas_call(
        kernel,
        out_shape=outs,
        in_specs=[pl.BlockSpec(memory_space=pltpu.VMEM)] * len(args),
        out_specs=[pl.BlockSpec(memory_space=pltpu.VMEM)] * len(outs),
        compiler_params=pltpu.CompilerParams(vmem_limit_bytes=44 * MIB),
        cost_estimate=pl.CostEstimate(flops=flops, bytes_accessed=moved, transcendentals=0),
    )(*args)


def shape(*dims):
    return jax.ShapeDtypeStruct(dims, BF16)


class Rows:
    def __init__(self, pieces, blocks, step):
        self.pieces, self.blocks, self.step = pieces, blocks, step

    def read(self, refs, at, side):
        piece, first = self.blocks[at][side]
        return refs[piece].at[first : first + self.step]


def hidden_kernel(rows, width, *refs):
    count = len(rows.pieces)
    pieces, (own_ref, other_ref, hidden_ref, turned_ref, silu_ref, rest_ref) = refs[:count], refs[count:]
    groups = own_ref.shape[0] // (2 * width)
    for at in range(len(rows.blocks)):
        span = slice(at * rows.step, (at + 1) * rows.step)
        sums = matmul(rows.read(pieces, at, 0)[...], own_ref[...], (1, 1))
        sums = sums + matmul(rows.read(pieces, at, 1)[...], other_ref[...], (1, 1))
        for group in range(groups):
            low = 2 * group * width
            silu_g, hidden, rest = gated(sums[:, low : low + width], sums[:, low + width : low + 2 * width])
            cols = slice(group * width, (group + 1) * width)
            hidden_ref[span, cols] = hidden.astype(BF16)
            turned_ref[cols, span] = hidden.T.astype(BF16)
            silu_ref[span, cols] = silu_g.astype(BF16)
            rest_ref[span, cols] = rest.astype(BF16)


def grads_kernel(rows, width, *refs):
    count = len(rows.pieces)
    pieces, (down_ref, silu_ref, rest_ref, act_ref, turned_ref) = refs[:count], refs[count:]
    groups = down_ref.shape[0] // width
    half = down_ref.shape[1] // 2
    for at in range(len(rows.blocks)):
        span = slice(at * rows.step, (at + 1) * rows.step)
        back = matmul(rows.read(pieces, at, 0)[...], down_ref[:, :half], (1, 1))
        back = back + matmul(rows.read(pieces, at, 1)[...], down_ref[:, half:], (1, 1))
        for group in range(groups):
            cols = slice(group * width, (group + 1) * width)
            for part, factor in enumerate((rest_ref, silu_ref)):
                grad = back[:, cols] * factor[span, cols].astype(F32)
                low = (2 * group + part) * width
                act_ref[span, low : low + width] = grad.astype(BF16)
                turned_ref[low : low + width, span] = grad.T.astype(BF16)


def weight_kernel(rows, sides, tile, *refs):
    count = len(rows.pieces)
    pieces, (turned_ref, out_ref) = refs[:count], refs[count:]
    half = out_ref.shape[1] // len(sides)
    for place, side in enumerate(sides):

        @pl.loop(0, half // tile)
        def _(index):
            cols = pl.ds(pl.multiple_of(index * tile, tile), tile)
            total = jnp.zeros((out_ref.shape[0], tile), F32)
            for at in range(len(rows.blocks)):
                span = slice(at * rows.step, (at + 1) * rows.step)
                total = total + matmul(turned_ref[:, span], rows.read(pieces, at, side)[:, cols], (1, 0))
            out_ref[:, pl.ds(pl.multiple_of(place * half + index * tile, tile), tile)] = total.astype(BF16)


def finish_kernel(at_ref, mine_ref, theirs_ref, gate_ref, up_ref):
    width = mine_ref.shape[0] // 2
    for part, out_ref in enumerate((gate_ref, up_ref)):
        span = slice(part * width, (part + 1) * width)
        mine, theirs = mine_ref[span].astype(F32).T, theirs_ref[span].astype(F32).T
        first = at_ref[0] == 0
        out_ref[:, :width] = jnp.where(first, mine, theirs)
        out_ref[:, width:] = jnp.where(first, theirs, mine)


class Square:
    def core(self, array):
        return lax.ppermute(array, "inp", [(at, at ^ 1) for at in range(4)])

    def chip(self, array):
        return lax.ppermute(array, "inp", [(at, at ^ 2) for at in range(4)])

    def other(self, array):
        return lax.ppermute(array, "out", [(0, 1), (1, 0)])

    def unit_halves(self, weight):
        half = weight.shape[0] // 2
        at = lax.axis_index("out")
        return (
            lax.dynamic_slice_in_dim(weight, at * half, half, 0),
            lax.dynamic_slice_in_dim(weight, (1 - at) * half, half, 0),
        )

    def in_order(self, mine, theirs):
        mine, theirs = mine.astype(F32), theirs.astype(F32)
        first = lax.axis_index("out") == 0
        return jnp.where(first, jnp.concatenate([mine, theirs]), jnp.concatenate([theirs, mine]))

    def gather(self, array):
        step = array.shape[1]
        own = array.reshape(2 * step, array.shape[2])
        by_chip, by_other = self.chip(own), self.other(own)
        corner = [self.other(by_chip[:step]), self.chip(by_other[step:])]
        pieces = [own, by_other, by_chip] + corner
        pieces = pieces + [self.core(piece) for piece in pieces]
        blocks = []
        for base in (0, 5):
            blocks += [((base, 0), (base + 1, 0)), ((base, step), (base + 1, step))]
            blocks += [((base + 2, 0), (base + 3, 0)), ((base + 2, step), (base + 4, 0))]
        return Rows(pieces, blocks, step)

    def scatter(self, product, rows, cols, over_y):
        half, quarter = rows // 2, rows // 4
        far = {}
        for chip in (1, 0):
            for other in (1, 0):
                at = slice(half + chip * quarter, half + (chip + 1) * quarter)
                far[chip, other] = self.core(product(at, other).astype(BF16))
        sums = {}
        for chip in (1, 0):
            for other in (1, 0):
                at = slice(chip * quarter, (chip + 1) * quarter)
                sums[chip, other] = product(at, other) + far[chip, other].astype(F32)
        batch = quarter // 2
        corner = sums[1, 1].astype(BF16)
        if over_y:
            to_chip = sums[1, 0] + self.other(corner).astype(F32)
            to_other = sums[0, 1]
        else:
            to_chip = sums[1, 0]
            to_other = sums[0, 1] + self.chip(corner).astype(F32)
        total = sums[0, 0] + self.chip(to_chip.astype(BF16)).astype(F32) + self.other(to_other.astype(BF16)).astype(F32)
        return total.astype(BF16).reshape(2, batch, cols // 2)

    def layer(self, tokens, gate_weight, up_weight, down_weight, cotangent):
        def gather_units(array):
            return lax.all_gather(array, "wt", axis=0, tiled=True)

        def scatter_units(array):
            return lax.psum_scatter(array, "wt", scatter_dimension=0, tiled=True)

        gate_mine, gate_theirs = self.unit_halves(gate_weight.T)
        up_mine, up_theirs = self.unit_halves(up_weight.T)
        down_mine, down_theirs = self.unit_halves(down_weight)
        width, half = gate_mine.shape
        own_units = gather_units(jnp.concatenate([gate_mine, up_mine]))
        other_units = gather_units(self.other(jnp.concatenate([gate_theirs, up_theirs])))
        down = gather_units(jnp.concatenate([down_mine, self.other(down_theirs)], axis=1))
        rows_in = self.gather(tokens)
        rows_cot = self.gather(cotangent)
        count = len(rows_in.blocks) * rows_in.step
        units = down.shape[0]

        hidden, hidden_turned, silu, rest = call(
            functools.partial(hidden_kernel, rows_in, width),
            [shape(count, units), shape(units, count), shape(count, units), shape(count, units)],
            8 * count * units * half,
            *rows_in.pieces,
            own_units,
            other_units,
        )
        (down_term,) = call(
            functools.partial(weight_kernel, rows_cot, (0, 1), 256),
            [shape(units, 2 * half)],
            4 * count * units * half,
            *rows_cot.pieces,
            hidden_turned,
        )
        down_sum = scatter_units(down_term)
        act, act_turned = call(
            functools.partial(grads_kernel, rows_cot, width),
            [shape(count, 2 * units), shape(2 * units, count)],
            4 * count * units * half,
            *rows_cot.pieces,
            down,
            silu,
            rest,
        )
        terms = [
            call(
                functools.partial(weight_kernel, rows_in, (side,), 256),
                [shape(2 * units, half)],
                4 * count * units * half,
                *rows_in.pieces,
                act_turned,
            )[0]
            for side in (1, 0)
        ]
        other_sum, own_sum = scatter_units(terms[0]), scatter_units(terms[1])
        down_back = self.other(down_sum[:, half:])
        units_back = self.other(other_sum)
        grad_down = self.in_order(down_sum[:, :half], down_back)
        grad_gate, grad_up = pl.pallas_call(
            finish_kernel,
            out_shape=[jax.ShapeDtypeStruct((half, 2 * width), F32)] * 2,
            in_specs=[pl.BlockSpec(memory_space=pltpu.SMEM)] + [pl.BlockSpec(memory_space=pltpu.VMEM)] * 2,
            out_specs=[pl.BlockSpec(memory_space=pltpu.VMEM)] * 2,
            compiler_params=pltpu.CompilerParams(vmem_limit_bytes=16 * MIB),
            cost_estimate=pl.CostEstimate(flops=0, bytes_accessed=5 * MIB, transcendentals=0),
        )(lax.axis_index("out").astype(jnp.int32).reshape(1), own_sum, units_back)

        def output_block(at, other):
            return matmul(hidden[at], down[:, other * half : (other + 1) * half], (1, 0))

        def input_block(at, other):
            return matmul(act[at], other_units if other else own_units, (1, 0))

        output = self.scatter(output_block, count, 2 * half, True)
        grad_tokens = self.scatter(input_block, count, 2 * half, False)
        return (output, grad_tokens, grad_gate, grad_up, grad_down)


class Plain:
    def units(self, weight):
        own = lax.all_to_all(weight, "out", split_axis=0, concat_axis=1, tiled=True)
        return lax.all_gather(own, "wt", axis=0, tiled=True)

    def unit_sums(self, grad):
        own = lax.psum_scatter(grad.astype(BF16), "wt", scatter_dimension=0, tiled=True)
        return lax.all_to_all(own, "out", split_axis=1, concat_axis=0, tiled=True).astype(F32)

    def gather(self, array):
        array = lax.all_gather(lax.all_gather(array, "inp", axis=1, tiled=True), "out", axis=2, tiled=True)
        return array.reshape(-1, array.shape[2])

    def scatter(self, partial, batches):
        partial = partial.astype(BF16).reshape(batches, -1, partial.shape[1])
        partial = lax.psum_scatter(partial, "out", scatter_dimension=2, tiled=True)
        return lax.psum_scatter(partial, "inp", scatter_dimension=1, tiled=True)

    def layer(self, tokens, gate_weight, up_weight, down_weight, cotangent):
        gate, up, down = self.units(gate_weight.T), self.units(up_weight.T), self.units(down_weight)
        rows_in, rows_cot = self.gather(tokens), self.gather(cotangent)
        gate_sum = matmul(rows_in, gate, (1, 1))
        up_sum = matmul(rows_in, up, (1, 1))
        silu_g, hidden, rest = gated(gate_sum, up_sum)
        hidden = hidden.astype(BF16)
        grad_down = self.unit_sums(matmul(hidden, rows_cot, (0, 0)))
        back_sum = matmul(rows_cot, down, (1, 1))
        gate_act, up_act = (back_sum * rest).astype(BF16), (back_sum * silu_g).astype(BF16)
        grad_gate = self.unit_sums(matmul(gate_act, rows_in, (0, 0))).T
        grad_up = self.unit_sums(matmul(up_act, rows_in, (0, 0))).T
        output = self.scatter(matmul(hidden, down, (1, 0)), tokens.shape[0])
        partial = matmul(gate_act, gate, (1, 0)) + matmul(up_act, up, (1, 0))
        grad_tokens = self.scatter(partial, tokens.shape[0])
        return (output, grad_tokens, grad_gate, grad_up, grad_down)


def solution(mesh):
    square = mesh.shape["inp"] == 4 and mesh.shape["out"] == 2

    def on_device(tokens, *others):
        places = Square() if square and tokens.shape[0] == 2 else Plain()
        return places.layer(tokens, *others)

    rows_spec = P(None, ("inp", "wt"), "out")
    in_spec = P("out", ("wt", "inp"))
    down_spec = P(("wt", "inp"), "out")
    return jax.shard_map(
        on_device,
        mesh=mesh,
        in_specs=(rows_spec, in_spec, in_spec, down_spec, rows_spec),
        out_specs=(rows_spec, rows_spec, in_spec, in_spec, down_spec),
        check_vma=False,
    )
```
